256 devices in a mesh: seq: 32 (over z, y_lo, core), head: 8 (over y_hi, x).
Axes of the slice: x: 4, y: 4 (y_hi: 2, y_lo: 2; y = y_hi * 2 + y_lo), z: 8, core: 2. Of those that a mesh axis runs over, the one named last changes fastest.
Arguments:
- query_rows: bfloat16 [8192, 4096], P(('seq', 'head')), may hold values from -48 to 48
- key_rows: bfloat16 [8192, 4096], P(('seq', 'head')), may hold values from -4 to 4
- value_rows: bfloat16 [8192, 4096], P(('seq', 'head')), may hold values from -6 to 6
- grad_rows: bfloat16 [8192, 4096], P(('seq', 'head')), may hold values from -6 to 6
Outputs:
- attended: bfloat16 [8192, 4096], P(('seq', 'head'))
- query_grad: bfloat16 [8192, 4096], P(('seq', 'head'))
- key_grad: bfloat16 [8192, 4096], P(('seq', 'head'))
- value_grad: bfloat16 [8192, 4096], P(('seq', 'head'))
The draws below stay inside these ranges and needn't reach their ends.
All inputs are finite; a program needn't handle non-finite values.
Results may differ from the reference program's by a relative error of at most 0.009.
Values may be sent and summed in bfloat16 or wider, within the bound.
No kernel may reach another device: no remote copies, remote signals or barrier semaphores. Data moves between devices by JAX's collectives and lax.ppermute only.
A program may use at most 128 MiB of HBM per device.

```python
import jax
import jax.numpy as jnp
from jax import lax

HEADS = 32
HEAD_DIM = 128
LEVELS = 4
D = 4096
TOKENS = 8192
SEG0 = 512


def shared_keys(key):
    left_key = jax.random.fold_in(key, 0)
    normal_part = jnp.clip(jax.random.normal(left_key, (TOKENS, HEADS, HEAD_DIM), jnp.float32), -4.0, 4.0)
    blended = normal_part
    in_block = jnp.arange(TOKENS) % 64
    near_copy = blended
    return jnp.where((in_block == 61)[:, None, None], near_copy, blended)


def draw_key_rows(key, part):
    rows_drawn = shared_keys(key)
    return rows_drawn.reshape(TOKENS, HEADS * HEAD_DIM).astype(jnp.bfloat16)


def draw_query_rows(key, part):
    key = jax.random.fold_in(key, 2)
    drawn_rows = 2.5 * jnp.clip(jax.random.normal(key, (TOKENS, HEADS, HEAD_DIM), jnp.float32), -6.0, 6.0)
    return jnp.clip(drawn_rows, -48.0, 48.0).reshape(TOKENS, HEADS * HEAD_DIM).astype(jnp.bfloat16)


def levels(rng, shape, cuts, low, top_value):
    gain = 1.0
    for axis_at, parts in cuts:
        draws = jax.random.uniform(jax.random.fold_in(jax.random.fold_in(rng, 6), axis_at), (parts,), jnp.float32, low / len(cuts), top_value / len(cuts))
        gain = gain * jnp.repeat(jnp.exp(draws), shape[axis_at] // parts).reshape((-1,) + (1,) * (len(shape) - 1 - axis_at))
    return gain


def scatter_about(key, shape, scale, bound, pieces=(), kind=jnp.bfloat16):
    result = jax.random.normal(key, shape, jnp.float32) * scale
    if len(pieces) > 0:
        result = levels(key, shape, pieces, -0.22, 0.18) * result
    return jnp.clip(result, min=-bound, max=bound).astype(kind)


def setup_inputs(seed: int = 0) -> dict:
    keys = jax.random.split(jax.random.key(seed), 5)
    return {
        "query_rows": draw_query_rows(jax.random.fold_in(keys[4], 71), 0),
        "key_rows": draw_key_rows(jax.random.fold_in(keys[4], 71), 0),
        "value_rows": scatter_about(keys[2], (TOKENS, D), 1.0, 6.0, ((0, 256),)),
        "grad_rows": scatter_about(keys[3], (TOKENS, D), 1.0, 6.0, ((0, 256),)),
    }


NEG = -1e30


def pick_level(source, stride, offset):
    shaped = source.reshape((source.shape[0] // stride, stride) + source.shape[1:])
    return lax.dynamic_index_in_dim(shaped, offset, axis=1, keepdims=False)


def place_level(source, stride, offset, filler):
    marks = jnp.arange(stride, dtype=jnp.int32) == offset
    marks = marks.reshape((1, stride) + (1,) * (source.ndim - 1))
    spread = jnp.where(marks, source[:, None], jnp.asarray(filler, source.dtype))
    return spread.reshape((source.shape[0] * stride,) + source.shape[1:])


def widen_layout(matrix):
    return lax.optimization_barrier(matrix.astype(jnp.bfloat16)).astype(jnp.float32)


def head_pass(inputs):
    head_num, queries, keys_all, values_all, grads_all = inputs
    dilation_factor = HEAD_DIM ** -0.5
    peak_list, total_list, summed_list = [], [], []
    for level_idx in range(LEVELS):
        stride = 2 ** level_idx
        offset = (head_num % stride).astype(jnp.int32)
        level_queries = pick_level(queries, stride, offset).reshape(-1, SEG0, HEAD_DIM).astype(jnp.float32)
        level_keys = pick_level(keys_all, stride, offset).reshape(-1, SEG0, HEAD_DIM).astype(jnp.float32)
        level_values = pick_level(values_all, stride, offset).reshape(-1, SEG0, HEAD_DIM).astype(jnp.float32)
        raw_scores = jnp.einsum("wei,whi->weh", level_queries, level_keys) * dilation_factor
        row_peak = jnp.max(raw_scores, axis=-1)
        weight_matrix = jnp.exp(raw_scores - row_peak[..., None])
        row_total = jnp.sum(weight_matrix, axis=-1)
        summed_weights = jnp.einsum("rxg,rgp->rxp", widen_layout(weight_matrix), level_values)
        peak_list.append(place_level(row_peak.reshape(-1), stride, offset, NEG))
        total_list.append(place_level(row_total.reshape(-1), stride, offset, 0.0))
        summed_list.append(place_level(summed_weights.reshape(-1, HEAD_DIM), stride, offset, 0.0))
    peak_stack = jnp.stack(peak_list)
    best_peak = jnp.max(peak_stack, axis=0)
    rescale = jnp.exp(peak_stack - best_peak)
    grand_total = jnp.sum(rescale * jnp.stack(total_list), axis=0)
    combined = jnp.sum(rescale[..., None] * jnp.stack(summed_list), axis=0) / grand_total[:, None]
    log_total = best_peak + jnp.log(grand_total)
    grad_dot = jnp.sum(grads_all.astype(jnp.float32) * combined, axis=-1)
    query_grad = jnp.zeros((TOKENS, HEAD_DIM), jnp.float32)
    key_grad = jnp.zeros((TOKENS, HEAD_DIM), jnp.float32)
    value_grad = jnp.zeros((TOKENS, HEAD_DIM), jnp.float32)
    for level_idx in range(LEVELS):
        stride = 2 ** level_idx
        offset = (head_num % stride).astype(jnp.int32)
        level_queries = pick_level(queries, stride, offset).reshape(-1, SEG0, HEAD_DIM).astype(jnp.float32)
        level_keys = pick_level(keys_all, stride, offset).reshape(-1, SEG0, HEAD_DIM).astype(jnp.float32)
        level_values = pick_level(values_all, stride, offset).reshape(-1, SEG0, HEAD_DIM).astype(jnp.float32)
        level_gradient = pick_level(grads_all, stride, offset).reshape(-1, SEG0, HEAD_DIM).astype(jnp.float32)
        lse_level = pick_level(log_total, stride, offset).reshape(-1, SEG0)
        dot_level = pick_level(grad_dot, stride, offset).reshape(-1, SEG0)
        raw_scores = jnp.einsum("wei,whi->weh", level_queries, level_keys) * dilation_factor
        probability_rows = jnp.exp(raw_scores - lse_level[..., None])
        probability_gradient = jnp.einsum("wei,whi->weh", level_gradient, level_values)
        score_gradient = widen_layout(probability_rows * (probability_gradient - dot_level[..., None]))
        query_portion = jnp.einsum("rxg,rgp->rxp", score_gradient, level_keys) * dilation_factor
        key_portion = jnp.einsum("rhe,rhm->rem", score_gradient, level_queries) * dilation_factor
        value_portion = jnp.einsum("rhe,rhm->rem", widen_layout(probability_rows), level_gradient)
        query_grad = query_grad + place_level(query_portion.reshape(-1, HEAD_DIM), stride, offset, 0.0)
        key_grad = key_grad + place_level(key_portion.reshape(-1, HEAD_DIM), stride, offset, 0.0)
        value_grad = value_grad + place_level(value_portion.reshape(-1, HEAD_DIM), stride, offset, 0.0)
    return (combined.astype(jnp.bfloat16), query_grad.astype(jnp.bfloat16),
            key_grad.astype(jnp.bfloat16), value_grad.astype(jnp.bfloat16))


def by_heads(matrix):
    return jnp.transpose(matrix.reshape(TOKENS, HEADS, HEAD_DIM), (1, 0, 2))


def to_rows(stacked):
    return jnp.transpose(stacked, (1, 0, 2)).reshape(TOKENS, HEADS * HEAD_DIM)


def reference(query_rows, key_rows, value_rows, grad_rows):
    head_nums = jnp.arange(HEADS, dtype=jnp.int32)
    results = lax.map(head_pass, (head_nums, by_heads(query_rows), by_heads(key_rows),
                                  by_heads(value_rows), by_heads(grad_rows)))
    return (to_rows(results[0]), to_rows(results[1]), to_rows(results[2]), to_rows(results[3]))
```

```python
import functools

import jax
import jax.numpy as jnp
from jax import lax
from jax.experimental import pallas as pl
from jax.experimental.pallas import tpu as pltpu
from jax.sharding import Mesh, PartitionSpec as P

HEAD_DIM = 128
PLANE = 32
ROWS = 32
TOKENS = PLANE * ROWS
SEG = 512
MID = 256
LOW = 384
SCALE = HEAD_DIM**-0.5
RATE = SCALE * 1.4426950408889634
NEG = -1e30
BF = jnp.bfloat16
F32 = jnp.float32


def nn(a, b):
    return jnp.dot(a, b, preferred_element_type=F32)


def nt(a, b):
    return lax.dot_general(a, b, (((1,), (1,)), ((), ())), preferred_element_type=F32)


def flip(a):
    return jnp.swapaxes(a, 0, 1)


def token_of(spot, offset, half):
    if half == 0:
        far = [2 * spot, 4 * (spot - 256), 8 * (spot - 384), 8 * (spot - 448)]
        tests = [spot < 256, spot < 384, spot < 448]
    else:
        far = [2 * (spot - 256), 4 * (spot - 128), 8 * (spot - 64), 8 * spot]
        tests = [spot >= 256, spot >= 128, spot >= 64]
    return jnp.where(
        tests[0],
        far[0] + ((offset + 1) & 1),
        jnp.where(
            tests[1],
            far[1] + ((offset + 2) & 3),
            jnp.where(tests[2], far[2] + ((offset + 4) & 7), far[3] + offset),
        ),
    )


def ordering(offset, half, first, count):
    spot = lax.broadcasted_iota(jnp.int32, (count, 1), 0) + first
    token = lax.broadcasted_iota(jnp.int32, (count, SEG), 1)
    return jnp.where(token_of(spot, offset, half) == token, 1.0, 0.0).astype(BF)


def unordering(offset, half, first, count):
    spot = lax.broadcasted_iota(jnp.int32, (1, count), 1) + first
    token = lax.broadcasted_iota(jnp.int32, (SEG, count), 0)
    return jnp.where(token_of(spot, offset, half) == token, 1.0, 0.0).astype(BF)


def head_offset():
    return lax.axis_index("plane") & 7


def pack_kernel(key_ref, value_ref, query_ref, grad_ref, out_ref):
    for index in range(out_ref.shape[0]):
        cut = slice(index * HEAD_DIM, (index + 1) * HEAD_DIM)
        out_ref[index, 0] = key_ref[:, cut]
        out_ref[index, 1] = value_ref[:, cut]
        out_ref[index, 2] = query_ref[:, cut]
        out_ref[index, 3] = grad_ref[:, cut]


def unpack_kernel(in_ref, att_ref, query_ref, key_ref, value_ref):
    for index in range(in_ref.shape[0]):
        cut = slice(index * HEAD_DIM, (index + 1) * HEAD_DIM)
        att_ref[:, cut] = in_ref[index, 0]
        query_ref[:, cut] = in_ref[index, 1]
        key_ref[:, cut] = in_ref[index, 2]
        value_ref[:, cut] = in_ref[index, 3]


def select_kernel(got_ref, out_ref):
    offset = head_offset()
    for half in range(2):
        rows = slice(half * 16, half * 16 + 16)
        pair = jnp.concatenate(
            [got_ref[rows, 0].reshape(SEG, HEAD_DIM), got_ref[rows, 1].reshape(SEG, HEAD_DIM)],
            axis=1,
        )
        picked = nn(ordering(offset, half, LOW if half == 0 else 0, 128), pair).astype(BF)
        out_ref[0, half * 128 : half * 128 + 128] = picked[:, :HEAD_DIM]
        out_ref[1, half * 128 : half * 128 + 128] = picked[:, HEAD_DIM:]


def segment_start(step):
    segment = step // 2
    start = jnp.where(segment == 2, 256, segment * SEG)
    return pl.multiple_of(start, 256), pl.multiple_of(start + (step % 2) * 256, 256)


def merge(peak, total, acc, peak_new, total_new, acc_new):
    best = jnp.maximum(peak, peak_new)
    left = jnp.exp2((peak - best) * RATE)
    right = jnp.exp2((peak_new - best) * RATE)
    return best, left * total + right * total_new, left * acc + right * acc_new


def local_kernel(got_ref, x_ref, mid_ref, stat_ref, comb_ref, mid_stat_ref, mid_acc_ref, vt, peak, total, acc):
    offset = head_offset()
    for half in range(2):
        rows = slice(half * 16, half * 16 + 16)
        four = jnp.concatenate(
            [got_ref[rows, index].reshape(SEG, HEAD_DIM) for index in range(4)], axis=1
        )
        ordered = nn(ordering(offset, half, 0, SEG), four).astype(BF)
        for index in range(4):
            x_ref[index, half * SEG : half * SEG + SEG] = ordered[
                :, index * HEAD_DIM : (index + 1) * HEAD_DIM
            ]
        vt[:, half * SEG : half * SEG + SEG] = flip(ordered[:, HEAD_DIM : 2 * HEAD_DIM])
    for index in range(4):
        mid_ref[index] = x_ref[index, LOW : LOW + MID]
    peak[...] = jnp.full_like(peak, NEG)
    total[...] = jnp.zeros_like(total)
    acc[...] = jnp.zeros_like(acc)

    def body(step, carry):
        start, first = segment_start(step)
        scores = nt(x_ref[0, pl.ds(start, SEG)], x_ref[2, pl.ds(first, 256)])
        top = jnp.max(scores, axis=0, keepdims=True)
        weights = jnp.exp2((scores - top) * RATE)
        cut = pl.ds(first, 256)
        peak[:, cut], total[:, cut], acc[:, cut] = merge(
            peak[:, cut],
            total[:, cut],
            acc[:, cut],
            top,
            jnp.sum(weights, axis=0, keepdims=True),
            nn(vt[:, pl.ds(start, SEG)], weights.astype(BF)),
        )
        return carry

    lax.fori_loop(0, 6, body, 0)
    mid_stat_ref[0:1] = peak[:, LOW : LOW + MID]
    mid_stat_ref[1:2] = total[:, LOW : LOW + MID]
    mid_acc_ref[...] = acc[:, LOW : LOW + MID]
    combined = acc[...] / total[...]
    comb_ref[...] = combined.astype(BF)
    stat_ref[0:1] = peak[...] * RATE + jnp.log2(total[...])
    stat_ref[1:2] = jnp.sum(flip(x_ref[3]).astype(F32) * combined, axis=0, keepdims=True)


def widen(part, filler):
    return pltpu.roll(jnp.concatenate([part, jnp.full_like(part, filler)], axis=1), 64, 1)


def narrow(whole):
    return pltpu.roll(whole, MID - 64, 1)[:, :128]


def forward_of(keys, values, queries):
    scores = nt(keys, queries)
    peak = jnp.max(scores, axis=0, keepdims=True)
    weights = jnp.exp2((scores - peak) * RATE)
    total = jnp.sum(weights, axis=0, keepdims=True)
    return peak, weights, total, nn(flip(values), weights.astype(BF))


def backward_of(probs, keys, values, queries, grads, dot):
    score_grad = (probs * (nt(values, grads) - dot)).astype(BF)
    return (
        nn(flip(keys), score_grad) * SCALE,
        nn(score_grad, queries) * SCALE,
        nn(probs.astype(BF), grads),
    )


def join(whole, part):
    return jnp.concatenate([whole[:64], whole[64:192] + part, whole[192:]], axis=0)


def far_kernel(mid_ref, stat_ref, acc_ref, one_ref, two_ref, three_ref,
               out_stat_ref, comb_ref, query_ref, own_ref, send_one_ref, send_two_ref, send_three_ref):
    keys2 = jnp.concatenate([mid_ref[0], one_ref[0]], axis=0)
    values2 = jnp.concatenate([mid_ref[1], one_ref[1]], axis=0)
    keys3 = jnp.concatenate([mid_ref[0, 64:192], one_ref[0, 64:192], two_ref[0], three_ref[0]], axis=0)
    values3 = jnp.concatenate([mid_ref[1, 64:192], one_ref[1, 64:192], two_ref[1], three_ref[1]], axis=0)
    queries2, grads2 = mid_ref[2], mid_ref[3]
    queries3, grads3 = mid_ref[2, 64:192], mid_ref[3, 64:192]
    peak2, weights2, total2, acc2 = forward_of(keys2, values2, queries2)
    peak3, weights3, total3, acc3 = forward_of(keys3, values3, queries3)
    state = merge(stat_ref[0:1], stat_ref[1:2], acc_ref[...], peak2, total2, acc2)
    peak, total, acc = merge(*state, widen(peak3, NEG), widen(total3, 0.0), widen(acc3, 0.0))
    combined = acc / total
    log_total = peak * RATE + jnp.log2(total)
    dot = jnp.sum(flip(grads2).astype(F32) * combined, axis=0, keepdims=True)
    out_stat_ref[0:1] = log_total
    out_stat_ref[1:2] = dot
    comb_ref[...] = combined.astype(BF)
    probs2 = weights2 * jnp.exp2(peak2 * RATE - log_total)
    probs3 = weights3 * jnp.exp2(peak3 * RATE - narrow(log_total))
    dq2, dk2, dv2 = backward_of(probs2, keys2, values2, queries2, grads2, dot)
    dq3, dk3, dv3 = backward_of(probs3, keys3, values3, queries3, grads3, narrow(dot))
    query_ref[...] = dq2 + widen(dq3, 0.0)
    for index, (near, far) in enumerate(((dk2, dk3), (dv2, dv3))):
        own_ref[index] = join(near[:MID], far[:128])
        send_one_ref[index] = join(near[MID:], far[128:256]).astype(BF)
        send_two_ref[index] = far[256:384].astype(BF)
        send_three_ref[index] = far[384:].astype(BF)


def back_kernel(x_ref, stat_ref, comb_ref, mid_stat_ref, mid_comb_ref, mid_query_ref,
                out_ref, mid_grad_ref, kt, stat, dq, dk, dv):
    offset = head_offset()
    kt[...] = flip(x_ref[0])
    stat[...] = stat_ref[...]
    stat[:, LOW : LOW + MID] = mid_stat_ref[...]
    dq[...] = jnp.zeros_like(dq)
    dk[...] = jnp.zeros_like(dk)
    dv[...] = jnp.zeros_like(dv)

    def body(step, carry):
        start, first = segment_start(step)
        keys, values = x_ref[0, pl.ds(start, SEG)], x_ref[1, pl.ds(start, SEG)]
        queries, grads = x_ref[2, pl.ds(first, 256)], x_ref[3, pl.ds(first, 256)]
        cut = pl.ds(first, 256)
        probs = jnp.exp2(nt(keys, queries) * RATE - stat[0:1, cut])
        score_grad = (probs * (nt(values, grads) - stat[1:2, cut])).astype(BF)
        dq[:, cut] += nn(kt[:, pl.ds(start, SEG)], score_grad)
        dk[pl.ds(start, SEG)] += nn(score_grad, queries)
        dv[pl.ds(start, SEG)] += nn(probs.astype(BF), grads)
        return carry

    lax.fori_loop(0, 6, body, 0)
    mid_grad_ref[0] = dk[LOW : LOW + MID] * SCALE
    mid_grad_ref[1] = dv[LOW : LOW + MID]
    query = dq[...] * SCALE
    query = jnp.concatenate(
        [query[:, :LOW], query[:, LOW : LOW + MID] + mid_query_ref[...], query[:, LOW + MID :]], axis=1
    ).astype(BF)
    comb = jnp.concatenate(
        [comb_ref[:, :LOW], mid_comb_ref[...], comb_ref[:, LOW + MID :]], axis=1
    )
    both = jnp.concatenate([comb, query], axis=0)
    for half in range(2):
        rows = slice(half * 16, half * 16 + 16)
        plain = nt(unordering(offset, half, 0, SEG), both[:, half * SEG : half * SEG + SEG]).astype(BF)
        out_ref[rows, 0] = plain[:, :HEAD_DIM].reshape(16, ROWS, HEAD_DIM)
        out_ref[rows, 1] = plain[:, HEAD_DIM:].reshape(16, ROWS, HEAD_DIM)
        outer = slice(0, LOW) if half == 0 else slice(LOW + MID, TOKENS)
        pair = jnp.concatenate([dk[outer] * SCALE, dv[outer]], axis=1).astype(BF)
        plain = nn(unordering(offset, half, 0 if half == 0 else 128, LOW), pair).astype(BF)
        out_ref[rows, 2] = plain[:, :HEAD_DIM].reshape(16, ROWS, HEAD_DIM)
        out_ref[rows, 3] = plain[:, HEAD_DIM:].reshape(16, ROWS, HEAD_DIM)


def finish_kernel(in_ref, mid_grad_ref, own_ref, one_ref, two_ref, three_ref, out_ref):
    offset = head_offset()
    grads = []
    for index in range(2):
        near = mid_grad_ref[index] + own_ref[index] + one_ref[index].astype(F32)
        far = two_ref[index].astype(F32) + three_ref[index].astype(F32)
        grads.append(join(near, far).astype(BF))
    pair = jnp.concatenate(grads, axis=1)
    for half in range(2):
        rows = slice(half * 16, half * 16 + 16)
        cut = slice(half * 128, half * 128 + 128)
        plain = nn(unordering(offset, half, LOW if half == 0 else 0, 128), pair[cut]).astype(BF)
        for index in range(2):
            part = plain[:, index * HEAD_DIM : (index + 1) * HEAD_DIM].reshape(16, ROWS, HEAD_DIM)
            out_ref[rows, index] = in_ref[rows, index] + part


def shape(dims, kind):
    return jax.ShapeDtypeStruct(dims, kind)


PARAMS = pltpu.CompilerParams(vmem_limit_bytes=32 * 1024 * 1024)


def whole(array):
    return pl.BlockSpec(array.shape, lambda: (0,) * len(array.shape))


def call(kernel, outs, args, scratch=(), flops=0):
    return pl.pallas_call(
        kernel,
        out_shape=outs,
        scratch_shapes=list(scratch),
        compiler_params=PARAMS,
        cost_estimate=pl.CostEstimate(flops=flops, bytes_accessed=2 << 20, transcendentals=0),
    )(*args)


def pack(arrays):
    step = 8
    return pl.pallas_call(
        pack_kernel,
        grid=(PLANE // step,),
        in_specs=[pl.BlockSpec((ROWS, step * HEAD_DIM), lambda i: (0, i))] * 4,
        out_specs=pl.BlockSpec((step, 4, ROWS, HEAD_DIM), lambda i: (i, 0, 0, 0)),
        out_shape=shape((PLANE, 4, ROWS, HEAD_DIM), BF),
        compiler_params=PARAMS,
    )(*arrays)


def unpack(packed):
    step = 8
    return pl.pallas_call(
        unpack_kernel,
        grid=(PLANE // step,),
        in_specs=[pl.BlockSpec((step, 4, ROWS, HEAD_DIM), lambda i: (i, 0, 0, 0))],
        out_specs=[pl.BlockSpec((ROWS, step * HEAD_DIM), lambda i: (0, i))] * 4,
        out_shape=[shape((ROWS, PLANE * HEAD_DIM), BF)] * 4,
        compiler_params=PARAMS,
    )(packed)


def plane_exchange(packed):
    return lax.all_to_all(packed, "plane", split_axis=0, concat_axis=0, tiled=True)


def z_exchange(block, apart):
    count = lax.axis_size("zed")
    return lax.ppermute(block, "zed", [(at, at ^ apart) for at in range(count)])


def per_device(query_rows, key_rows, value_rows, grad_rows):
    got = plane_exchange(pack([key_rows, value_rows, query_rows, grad_rows]))
    half_block = pl.BlockSpec((PLANE, 2, ROWS, HEAD_DIM), lambda i: (0, 0, 0, 0))
    near = pl.pallas_call(
        select_kernel,
        grid=(1,),
        in_specs=[half_block],
        out_specs=pl.BlockSpec((2, MID, HEAD_DIM), lambda i: (0, 0, 0)),
        out_shape=shape((2, MID, HEAD_DIM), BF),
        compiler_params=PARAMS,
    )(got)
    inner = near[:, 64:192]
    one = z_exchange(near, 1)
    two = z_exchange(inner, 2)
    three = z_exchange(inner, 3)
    ordered, mid, stat, comb, mid_stat, mid_acc = call(
        local_kernel,
        [
            shape((4, TOKENS, HEAD_DIM), BF),
            shape((4, MID, HEAD_DIM), BF),
            shape((2, TOKENS), F32),
            shape((HEAD_DIM, TOKENS), BF),
            shape((2, MID), F32),
            shape((HEAD_DIM, MID), F32),
        ],
        [got],
        [
            pltpu.VMEM((HEAD_DIM, TOKENS), BF),
            pltpu.VMEM((1, TOKENS), F32),
            pltpu.VMEM((1, TOKENS), F32),
            pltpu.VMEM((HEAD_DIM, TOKENS), F32),
        ],
        flops=3 * 4 * SEG * SEG * HEAD_DIM,
    )
    mid_out_stat, mid_comb, mid_query, own, send_one, send_two, send_three = call(
        far_kernel,
        [
            shape((2, MID), F32),
            shape((HEAD_DIM, MID), BF),
            shape((HEAD_DIM, MID), F32),
            shape((2, MID, HEAD_DIM), F32),
            shape((2, MID, HEAD_DIM), BF),
            shape((2, 128, HEAD_DIM), BF),
            shape((2, 128, HEAD_DIM), BF),
        ],
        [mid, mid_stat, mid_acc, one, two, three],
        flops=3 * 4 * SEG * SEG * HEAD_DIM,
    )
    back_one = z_exchange(send_one, 1)
    back_two = z_exchange(send_two, 2)
    back_three = z_exchange(send_three, 3)
    packed, mid_grad = call(
        back_kernel,
        [shape((PLANE, 4, ROWS, HEAD_DIM), BF), shape((2, MID, HEAD_DIM), F32)],
        [ordered, stat, comb, mid_out_stat, mid_comb, mid_query],
        [
            pltpu.VMEM((HEAD_DIM, TOKENS), BF),
            pltpu.VMEM((2, TOKENS), F32),
            pltpu.VMEM((HEAD_DIM, TOKENS), F32),
            pltpu.VMEM((TOKENS, HEAD_DIM), F32),
            pltpu.VMEM((TOKENS, HEAD_DIM), F32),
        ],
        flops=3 * 10 * SEG * SEG * HEAD_DIM,
    )
    upper_half = pl.BlockSpec((PLANE, 2, ROWS, HEAD_DIM), lambda i: (0, 1, 0, 0))
    mid_block = pl.BlockSpec((2, MID, HEAD_DIM), lambda i: (0, 0, 0))
    inner_block = pl.BlockSpec((2, 128, HEAD_DIM), lambda i: (0, 0, 0))
    packed = pl.pallas_call(
        finish_kernel,
        grid=(1,),
        in_specs=[upper_half, mid_block, mid_block, mid_block, inner_block, inner_block],
        out_specs=upper_half,
        out_shape=shape((PLANE, 4, ROWS, HEAD_DIM), BF),
        input_output_aliases={0: 0},
        compiler_params=PARAMS,
    )(packed, mid_grad, own, back_one, back_two, back_three)
    return tuple(unpack(plane_exchange(packed)))


def solution(mesh):
    planes = Mesh(mesh.devices.reshape(-1, PLANE), ("zed", "plane"))
    spec = P(("zed", "plane"), None)
    return jax.shard_map(
        per_device, mesh=planes, in_specs=(spec,) * 4, out_specs=(spec,) * 4, check_vma=False
    )
```

```python
import functools

import jax
import jax.numpy as jnp
from jax import lax
from jax.experimental import pallas as pl
from jax.experimental.pallas import tpu as pltpu
from jax.sharding import Mesh, PartitionSpec as P

HEAD_DIM = 128
PLANE = 32
ROWS = 32
TOKENS = PLANE * ROWS
SEG = 512
MID = 256
LOW = 384
SCALE = HEAD_DIM**-0.5
RATE = SCALE * 1.4426950408889634
NEG = -1e30
BF = jnp.bfloat16
F32 = jnp.float32


def nn(a, b):
    return jnp.dot(a, b, preferred_element_type=F32)


def nt(a, b):
    return lax.dot_general(a, b, (((1,), (1,)), ((), ())), preferred_element_type=F32)


def flip(a):
    return jnp.swapaxes(a, 0, 1)


def token_of(spot, offset, half):
    if half == 0:
        far = [2 * spot, 4 * (spot - 256), 8 * (spot - 384), 8 * (spot - 448)]
        tests = [spot < 256, spot < 384, spot < 448]
    else:
        far = [2 * (spot - 256), 4 * (spot - 128), 8 * (spot - 64), 8 * spot]
        tests = [spot >= 256, spot >= 128, spot >= 64]
    return jnp.where(
        tests[0],
        far[0] + ((offset + 1) & 1),
        jnp.where(
            tests[1],
            far[1] + ((offset + 2) & 3),
            jnp.where(tests[2], far[2] + ((offset + 4) & 7), far[3] + offset),
        ),
    )


def ordering(offset, half, first, count):
    spot = lax.broadcasted_iota(jnp.int32, (count, 1), 0) + first
    token = lax.broadcasted_iota(jnp.int32, (count, SEG), 1)
    return jnp.where(token_of(spot, offset, half) == token, 1.0, 0.0).astype(BF)


def unordering(offset, half, first, count):
    spot = lax.broadcasted_iota(jnp.int32, (1, count), 1) + first
    token = lax.broadcasted_iota(jnp.int32, (SEG, count), 0)
    return jnp.where(token_of(spot, offset, half) == token, 1.0, 0.0).astype(BF)


def head_offset():
    return lax.axis_index("plane") & 7


def pack_kernel(key_ref, value_ref, query_ref, grad_ref, out_ref, held, arrived):
    copies = [
        pltpu.make_async_copy(source, held.at[index], arrived.at[index])
        for index, source in enumerate((key_ref, value_ref, query_ref, grad_ref))
    ]
    for copy in copies:
        copy.start()
    for index, copy in enumerate(copies):
        copy.wait()
        for head in range(PLANE):
            out_ref[head, index] = held[index, :, head * HEAD_DIM : (head + 1) * HEAD_DIM]


def unpack_kernel(in_ref, att_ref, query_ref, key_ref, value_ref, held, sent):
    copies = []
    for index, target in enumerate((att_ref, query_ref, key_ref, value_ref)):
        for head in range(PLANE):
            held[index, :, head * HEAD_DIM : (head + 1) * HEAD_DIM] = in_ref[head, index]
        copies.append(pltpu.make_async_copy(held.at[index], target, sent.at[index]))
        copies[-1].start()
    for copy in copies:
        copy.wait()


def select_kernel(got_ref, out_ref):
    offset = head_offset()
    for half in range(2):
        rows = slice(half * 16, half * 16 + 16)
        pair = jnp.concatenate(
            [got_ref[rows, 0].reshape(SEG, HEAD_DIM), got_ref[rows, 1].reshape(SEG, HEAD_DIM)],
            axis=1,
        )
        picked = nn(ordering(offset, half, LOW if half == 0 else 0, 128), pair).astype(BF)
        out_ref[0, half * 128 : half * 128 + 128] = picked[:, :HEAD_DIM]
        out_ref[1, half * 128 : half * 128 + 128] = picked[:, HEAD_DIM:]


def segment_start(step):
    segment = step // 2
    start = jnp.where(segment == 2, 256, segment * SEG)
    return pl.multiple_of(start, 256), pl.multiple_of(start + (step % 2) * 256, 256)


def merge(peak, total, acc, peak_new, total_new, acc_new):
    best = jnp.maximum(peak, peak_new)
    left = jnp.exp2((peak - best) * RATE)
    right = jnp.exp2((peak_new - best) * RATE)
    return best, left * total + right * total_new, left * acc + right * acc_new


def local_kernel(got_ref, x_ref, mid_ref, stat_ref, comb_ref, mid_stat_ref, mid_acc_ref, vt, peak, total, acc):
    offset = head_offset()
    for half in range(2):
        rows = slice(half * 16, half * 16 + 16)
        four = jnp.concatenate(
            [got_ref[rows, index].reshape(SEG, HEAD_DIM) for index in range(4)], axis=1
        )
        ordered = nn(ordering(offset, half, 0, SEG), four).astype(BF)
        for index in range(4):
            x_ref[index, half * SEG : half * SEG + SEG] = ordered[
                :, index * HEAD_DIM : (index + 1) * HEAD_DIM
            ]
        vt[:, half * SEG : half * SEG + SEG] = flip(ordered[:, HEAD_DIM : 2 * HEAD_DIM])
    for index in range(4):
        mid_ref[index] = x_ref[index, LOW : LOW + MID]
    peak[...] = jnp.full_like(peak, NEG)
    total[...] = jnp.zeros_like(total)
    acc[...] = jnp.zeros_like(acc)

    def body(step, carry):
        start, first = segment_start(step)
        scores = nt(x_ref[0, pl.ds(start, SEG)], x_ref[2, pl.ds(first, 256)])
        top = jnp.max(scores, axis=0, keepdims=True)
        weights = jnp.exp2((scores - top) * RATE)
        cut = pl.ds(first, 256)
        peak[:, cut], total[:, cut], acc[:, cut] = merge(
            peak[:, cut],
            total[:, cut],
            acc[:, cut],
            top,
            jnp.sum(weights, axis=0, keepdims=True),
            nn(vt[:, pl.ds(start, SEG)], weights.astype(BF)),
        )
        return carry

    lax.fori_loop(0, 6, body, 0)
    mid_stat_ref[0:1] = peak[:, LOW : LOW + MID]
    mid_stat_ref[1:2] = total[:, LOW : LOW + MID]
    mid_acc_ref[...] = acc[:, LOW : LOW + MID]
    combined = acc[...] / total[...]
    comb_ref[...] = combined.astype(BF)
    stat_ref[0:1] = peak[...] * RATE + jnp.log2(total[...])
    stat_ref[1:2] = jnp.sum(flip(x_ref[3]).astype(F32) * combined, axis=0, keepdims=True)


def widen(part, filler):
    return pltpu.roll(jnp.concatenate([part, jnp.full_like(part, filler)], axis=1), 64, 1)


def narrow(whole):
    return pltpu.roll(whole, MID - 64, 1)[:, :128]


def forward_of(keys, values, queries):
    scores = nt(keys, queries)
    peak = jnp.max(scores, axis=0, keepdims=True)
    weights = jnp.exp2((scores - peak) * RATE)
    total = jnp.sum(weights, axis=0, keepdims=True)
    return peak, weights, total, nn(flip(values), weights.astype(BF))


def backward_of(probs, keys, values, queries, grads, dot):
    score_grad = (probs * (nt(values, grads) - dot)).astype(BF)
    return (
        nn(flip(keys), score_grad) * SCALE,
        nn(score_grad, queries) * SCALE,
        nn(probs.astype(BF), grads),
    )


def join(whole, part):
    return jnp.concatenate([whole[:64], whole[64:192] + part, whole[192:]], axis=0)


def far_kernel(mid_ref, stat_ref, acc_ref, one_ref, two_ref, three_ref,
               out_stat_ref, comb_ref, query_ref, own_ref, send_one_ref, send_two_ref, send_three_ref):
    keys2 = jnp.concatenate([mid_ref[0], one_ref[0]], axis=0)
    values2 = jnp.concatenate([mid_ref[1], one_ref[1]], axis=0)
    keys3 = jnp.concatenate([mid_ref[0, 64:192], one_ref[0, 64:192], two_ref[0], three_ref[0]], axis=0)
    values3 = jnp.concatenate([mid_ref[1, 64:192], one_ref[1, 64:192], two_ref[1], three_ref[1]], axis=0)
    queries2, grads2 = mid_ref[2], mid_ref[3]
    queries3, grads3 = mid_ref[2, 64:192], mid_ref[3, 64:192]
    peak2, weights2, total2, acc2 = forward_of(keys2, values2, queries2)
    peak3, weights3, total3, acc3 = forward_of(keys3, values3, queries3)
    state = merge(stat_ref[0:1], stat_ref[1:2], acc_ref[...], peak2, total2, acc2)
    peak, total, acc = merge(*state, widen(peak3, NEG), widen(total3, 0.0), widen(acc3, 0.0))
    combined = acc / total
    log_total = peak * RATE + jnp.log2(total)
    dot = jnp.sum(flip(grads2).astype(F32) * combined, axis=0, keepdims=True)
    out_stat_ref[0:1] = log_total
    out_stat_ref[1:2] = dot
    comb_ref[...] = combined.astype(BF)
    probs2 = weights2 * jnp.exp2(peak2 * RATE - log_total)
    probs3 = weights3 * jnp.exp2(peak3 * RATE - narrow(log_total))
    dq2, dk2, dv2 = backward_of(probs2, keys2, values2, queries2, grads2, dot)
    dq3, dk3, dv3 = backward_of(probs3, keys3, values3, queries3, grads3, narrow(dot))
    query_ref[...] = dq2 + widen(dq3, 0.0)
    for index, (near, far) in enumerate(((dk2, dk3), (dv2, dv3))):
        own_ref[index] = join(near[:MID], far[:128])
        send_one_ref[index] = join(near[MID:], far[128:256]).astype(BF)
        send_two_ref[index] = far[256:384].astype(BF)
        send_three_ref[index] = far[384:].astype(BF)


def back_kernel(x_ref, stat_ref, comb_ref, mid_stat_ref, mid_comb_ref, mid_query_ref,
                out_ref, mid_grad_ref, kt, stat, dq, dk, dv):
    offset = head_offset()
    kt[...] = flip(x_ref[0])
    stat[...] = stat_ref[...]
    stat[:, LOW : LOW + MID] = mid_stat_ref[...]
    dq[...] = jnp.zeros_like(dq)
    dk[...] = jnp.zeros_like(dk)
    dv[...] = jnp.zeros_like(dv)

    def body(step, carry):
        start, first = segment_start(step)
        keys, values = x_ref[0, pl.ds(start, SEG)], x_ref[1, pl.ds(start, SEG)]
        queries, grads = x_ref[2, pl.ds(first, 256)], x_ref[3, pl.ds(first, 256)]
        cut = pl.ds(first, 256)
        probs = jnp.exp2(nt(keys, queries) * RATE - stat[0:1, cut])
        score_grad = (probs * (nt(values, grads) - stat[1:2, cut])).astype(BF)
        dq[:, cut] += nn(kt[:, pl.ds(start, SEG)], score_grad)
        dk[pl.ds(start, SEG)] += nn(score_grad, queries)
        dv[pl.ds(start, SEG)] += nn(probs.astype(BF), grads)
        return carry

    lax.fori_loop(0, 6, body, 0)
    mid_grad_ref[0] = dk[LOW : LOW + MID] * SCALE
    mid_grad_ref[1] = dv[LOW : LOW + MID]
    query = dq[...] * SCALE
    query = jnp.concatenate(
        [query[:, :LOW], query[:, LOW : LOW + MID] + mid_query_ref[...], query[:, LOW + MID :]], axis=1
    ).astype(BF)
    comb = jnp.concatenate(
        [comb_ref[:, :LOW], mid_comb_ref[...], comb_ref[:, LOW + MID :]], axis=1
    )
    both = jnp.concatenate([comb, query], axis=0)
    for half in range(2):
        rows = slice(half * 16, half * 16 + 16)
        plain = nt(unordering(offset, half, 0, SEG), both[:, half * SEG : half * SEG + SEG]).astype(BF)
        out_ref[rows, 0] = plain[:, :HEAD_DIM].reshape(16, ROWS, HEAD_DIM)
        out_ref[rows, 1] = plain[:, HEAD_DIM:].reshape(16, ROWS, HEAD_DIM)
        outer = slice(0, LOW) if half == 0 else slice(LOW + MID, TOKENS)
        pair = jnp.concatenate([dk[outer] * SCALE, dv[outer]], axis=1).astype(BF)
        plain = nn(unordering(offset, half, 0 if half == 0 else 128, LOW), pair).astype(BF)
        out_ref[rows, 2] = plain[:, :HEAD_DIM].reshape(16, ROWS, HEAD_DIM)
        out_ref[rows, 3] = plain[:, HEAD_DIM:].reshape(16, ROWS, HEAD_DIM)


def finish_kernel(in_ref, mid_grad_ref, own_ref, one_ref, two_ref, three_ref, out_ref):
    offset = head_offset()
    grads = []
    for index in range(2):
        near = mid_grad_ref[index] + own_ref[index] + one_ref[index].astype(F32)
        far = two_ref[index].astype(F32) + three_ref[index].astype(F32)
        grads.append(join(near, far).astype(BF))
    pair = jnp.concatenate(grads, axis=1)
    for half in range(2):
        rows = slice(half * 16, half * 16 + 16)
        cut = slice(half * 128, half * 128 + 128)
        plain = nn(unordering(offset, half, LOW if half == 0 else 0, 128), pair[cut]).astype(BF)
        for index in range(2):
            part = plain[:, index * HEAD_DIM : (index + 1) * HEAD_DIM].reshape(16, ROWS, HEAD_DIM)
            out_ref[rows, index] = in_ref[rows, index] + part


def shape(dims, kind):
    return jax.ShapeDtypeStruct(dims, kind)


PARAMS = pltpu.CompilerParams(vmem_limit_bytes=32 * 1024 * 1024)


def whole(array):
    return pl.BlockSpec(array.shape, lambda: (0,) * len(array.shape))


def call(kernel, outs, args, scratch=(), flops=0):
    return pl.pallas_call(
        kernel,
        out_shape=outs,
        scratch_shapes=list(scratch),
        compiler_params=PARAMS,
        cost_estimate=pl.CostEstimate(flops=flops, bytes_accessed=2 << 20, transcendentals=0),
    )(*args)


def pack(arrays):
    return pl.pallas_call(
        pack_kernel,
        in_specs=[pl.BlockSpec(memory_space=pl.ANY)] * 4,
        out_shape=shape((PLANE, 4, ROWS, HEAD_DIM), BF),
        scratch_shapes=[
            pltpu.VMEM((4, ROWS, PLANE * HEAD_DIM), BF),
            pltpu.SemaphoreType.DMA((4,)),
        ],
        compiler_params=PARAMS,
    )(*[pltpu.with_memory_space_constraint(array, pltpu.HBM) for array in arrays])


def unpack(packed):
    return pl.pallas_call(
        unpack_kernel,
        out_specs=[pl.BlockSpec(memory_space=pl.ANY)] * 4,
        out_shape=[shape((ROWS, PLANE * HEAD_DIM), BF)] * 4,
        scratch_shapes=[
            pltpu.VMEM((4, ROWS, PLANE * HEAD_DIM), BF),
            pltpu.SemaphoreType.DMA((4,)),
        ],
        compiler_params=PARAMS,
    )(packed)


def plane_exchange(packed):
    return lax.all_to_all(packed, "plane", split_axis=0, concat_axis=0, tiled=True)


def z_exchange(block, apart):
    count = lax.axis_size("zed")
    return lax.ppermute(block, "zed", [(at, at ^ apart) for at in range(count)])


def per_device(query_rows, key_rows, value_rows, grad_rows):
    got = plane_exchange(pack([key_rows, value_rows, query_rows, grad_rows]))
    half_block = pl.BlockSpec((PLANE, 2, ROWS, HEAD_DIM), lambda i: (0, 0, 0, 0))
    near = pl.pallas_call(
        select_kernel,
        grid=(1,),
        in_specs=[half_block],
        out_specs=pl.BlockSpec((2, MID, HEAD_DIM), lambda i: (0, 0, 0)),
        out_shape=shape((2, MID, HEAD_DIM), BF),
        compiler_params=PARAMS,
    )(got)
    inner = near[:, 64:192]
    one = z_exchange(near, 1)
    two = z_exchange(inner, 2)
    three = z_exchange(inner, 3)
    ordered, mid, stat, comb, mid_stat, mid_acc = call(
        local_kernel,
        [
            shape((4, TOKENS, HEAD_DIM), BF),
            shape((4, MID, HEAD_DIM), BF),
            shape((2, TOKENS), F32),
            shape((HEAD_DIM, TOKENS), BF),
            shape((2, MID), F32),
            shape((HEAD_DIM, MID), F32),
        ],
        [got],
        [
            pltpu.VMEM((HEAD_DIM, TOKENS), BF),
            pltpu.VMEM((1, TOKENS), F32),
            pltpu.VMEM((1, TOKENS), F32),
            pltpu.VMEM((HEAD_DIM, TOKENS), F32),
        ],
        flops=3 * 4 * SEG * SEG * HEAD_DIM,
    )
    mid_out_stat, mid_comb, mid_query, own, send_one, send_two, send_three = call(
        far_kernel,
        [
            shape((2, MID), F32),
            shape((HEAD_DIM, MID), BF),
            shape((HEAD_DIM, MID), F32),
            shape((2, MID, HEAD_DIM), F32),
            shape((2, MID, HEAD_DIM), BF),
            shape((2, 128, HEAD_DIM), BF),
            shape((2, 128, HEAD_DIM), BF),
        ],
        [mid, mid_stat, mid_acc, one, two, three],
        flops=3 * 4 * SEG * SEG * HEAD_DIM,
    )
    back_one = z_exchange(send_one, 1)
    back_two = z_exchange(send_two, 2)
    back_three = z_exchange(send_three, 3)
    packed, mid_grad = call(
        back_kernel,
        [shape((PLANE, 4, ROWS, HEAD_DIM), BF), shape((2, MID, HEAD_DIM), F32)],
        [ordered, stat, comb, mid_out_stat, mid_comb, mid_query],
        [
            pltpu.VMEM((HEAD_DIM, TOKENS), BF),
            pltpu.VMEM((2, TOKENS), F32),
            pltpu.VMEM((HEAD_DIM, TOKENS), F32),
            pltpu.VMEM((TOKENS, HEAD_DIM), F32),
            pltpu.VMEM((TOKENS, HEAD_DIM), F32),
        ],
        flops=3 * 10 * SEG * SEG * HEAD_DIM,
    )
    upper_half = pl.BlockSpec((PLANE, 2, ROWS, HEAD_DIM), lambda i: (0, 1, 0, 0))
    mid_block = pl.BlockSpec((2, MID, HEAD_DIM), lambda i: (0, 0, 0))
    inner_block = pl.BlockSpec((2, 128, HEAD_DIM), lambda i: (0, 0, 0))
    packed = pl.pallas_call(
        finish_kernel,
        grid=(1,),
        in_specs=[upper_half, mid_block, mid_block, mid_block, inner_block, inner_block],
        out_specs=upper_half,
        out_shape=shape((PLANE, 4, ROWS, HEAD_DIM), BF),
        input_output_aliases={0: 0},
        compiler_params=PARAMS,
    )(packed, mid_grad, own, back_one, back_two, back_three)
    return tuple(unpack(plane_exchange(packed)))


def solution(mesh):
    planes = Mesh(mesh.devices.reshape(-1, PLANE), ("zed", "plane"))
    spec = P(("zed", "plane"), None)
    return jax.shard_map(
        per_device, mesh=planes, in_specs=(spec,) * 4, out_specs=(spec,) * 4, check_vma=False
    )
```

```python
import functools

import jax
import jax.numpy as jnp
from jax import lax
from jax.experimental import pallas as pl
from jax.experimental.pallas import tpu as pltpu
from jax.sharding import Mesh, PartitionSpec as P

HEAD_DIM = 128
PLANE = 32
ROWS = 32
TOKENS = PLANE * ROWS
SEG = 512
MID = 256
LOW = 384
SCALE = HEAD_DIM**-0.5
RATE = SCALE * 1.4426950408889634
NEG = -1e30
BF = jnp.bfloat16
F32 = jnp.float32

ORDER = [
    y_lo * 16 + core * 8 + y_hi * 4 + x
    for x in range(4)
    for y_lo in range(2)
    for y_hi in range(2)
    for core in range(2)
]
PLACE = [ORDER.index(device) for device in range(PLANE)]


def nn(a, b):
    return jnp.dot(a, b, preferred_element_type=F32)


def nt(a, b):
    return lax.dot_general(a, b, (((1,), (1,)), ((), ())), preferred_element_type=F32)


def flip(a):
    return jnp.swapaxes(a, 0, 1)


def token_of(spot, offset, half):
    if half == 0:
        far = [2 * spot, 4 * (spot - 256), 8 * (spot - 384), 8 * (spot - 448)]
        tests = [spot < 256, spot < 384, spot < 448]
    else:
        far = [2 * (spot - 256), 4 * (spot - 128), 8 * (spot - 64), 8 * spot]
        tests = [spot >= 256, spot >= 128, spot >= 64]
    return jnp.where(
        tests[0],
        far[0] + ((offset + 1) & 1),
        jnp.where(
            tests[1],
            far[1] + ((offset + 2) & 3),
            jnp.where(tests[2], far[2] + ((offset + 4) & 7), far[3] + offset),
        ),
    )


def ordering(offset, half, first, count):
    spot = lax.broadcasted_iota(jnp.int32, (count, 1), 0) + first
    token = lax.broadcasted_iota(jnp.int32, (count, SEG), 1)
    return jnp.where(token_of(spot, offset, half) == token, 1.0, 0.0).astype(BF)


def unordering(offset, half, first, count):
    spot = lax.broadcasted_iota(jnp.int32, (1, count), 1) + first
    token = lax.broadcasted_iota(jnp.int32, (SEG, count), 0)
    return jnp.where(token_of(spot, offset, half) == token, 1.0, 0.0).astype(BF)


def head_offset():
    return lax.axis_index("y_hi") * 4 + lax.axis_index("x")


def half_of(ref, half, index):
    return jnp.concatenate([ref[PLACE[block], index] for block in range(half * 16, half * 16 + 16)], axis=0)


def put_half(ref, half, index, value):
    for block in range(16):
        ref[PLACE[half * 16 + block], index] = value[block * ROWS : block * ROWS + ROWS]


def pack_kernel(key_ref, value_ref, query_ref, grad_ref, out_ref, held, arrived):
    copies = [
        pltpu.make_async_copy(source, held.at[index], arrived.at[index])
        for index, source in enumerate((key_ref, value_ref, query_ref, grad_ref))
    ]
    for copy in copies:
        copy.start()
    for index, copy in enumerate(copies):
        copy.wait()
        for head in range(PLANE):
            out_ref[PLACE[head], index] = held[index, :, head * HEAD_DIM : (head + 1) * HEAD_DIM]


def unpack_kernel(in_ref, att_ref, query_ref, key_ref, value_ref, held, sent):
    copies = []
    for index, target in enumerate((att_ref, query_ref, key_ref, value_ref)):
        for head in range(PLANE):
            held[index, :, head * HEAD_DIM : (head + 1) * HEAD_DIM] = in_ref[PLACE[head], index]
        copies.append(pltpu.make_async_copy(held.at[index], target, sent.at[index]))
        copies[-1].start()
    for copy in copies:
        copy.wait()


def select_kernel(got_ref, out_ref):
    offset = head_offset()
    for half in range(2):
        pair = jnp.concatenate([half_of(got_ref, half, 0), half_of(got_ref, half, 1)], axis=1)
        picked = nn(ordering(offset, half, LOW if half == 0 else 0, 128), pair).astype(BF)
        out_ref[0, half * 128 : half * 128 + 128] = picked[:, :HEAD_DIM]
        out_ref[1, half * 128 : half * 128 + 128] = picked[:, HEAD_DIM:]


def segment_start(step):
    segment = step // 2
    start = jnp.where(segment == 2, 256, segment * SEG)
    return pl.multiple_of(start, 256), pl.multiple_of(start + (step % 2) * 256, 256)


def merge(peak, total, acc, peak_new, total_new, acc_new):
    best = jnp.maximum(peak, peak_new)
    left = jnp.exp2((peak - best) * RATE)
    right = jnp.exp2((peak_new - best) * RATE)
    return best, left * total + right * total_new, left * acc + right * acc_new


def first_kernel(got_ref, x_ref, mid_ref, vt_ref, state_ref, acc_ref):
    offset = head_offset()
    for half in range(2):
        four = jnp.concatenate([half_of(got_ref, half, index) for index in range(4)], axis=1)
        ordered = nn(ordering(offset, half, 0, SEG), four).astype(BF)
        for index in range(4):
            x_ref[index, half * SEG : half * SEG + SEG] = ordered[
                :, index * HEAD_DIM : (index + 1) * HEAD_DIM
            ]
        vt_ref[:, half * SEG : half * SEG + SEG] = flip(ordered[:, HEAD_DIM : 2 * HEAD_DIM])
    for index in range(4):
        mid_ref[index] = x_ref[index, LOW : LOW + MID]

    def body(step, carry):
        start, first = segment_start(step)
        scores = nt(x_ref[0, pl.ds(start, SEG)], x_ref[2, pl.ds(first, 256)])
        peak = jnp.max(scores, axis=0, keepdims=True)
        weights = jnp.exp2((scores - peak) * RATE)
        cut = pl.ds(first, 256)
        state_ref[0:1, cut] = peak
        state_ref[1:2, cut] = jnp.sum(weights, axis=0, keepdims=True)
        acc_ref[:, cut] = nn(vt_ref[:, pl.ds(start, SEG)], weights.astype(BF))
        return carry

    lax.fori_loop(0, 4, body, 0, unroll=4)


def second_kernel(x_ref, vt_ref, state_in, acc_in, stat_ref, comb_ref, mid_stat_ref, mid_acc_ref, state, acc):
    state[...] = state_in[...]
    acc[...] = acc_in[...]

    def body(step, carry):
        start, first = segment_start(step)
        scores = nt(x_ref[0, pl.ds(start, SEG)], x_ref[2, pl.ds(first, 256)])
        top = jnp.max(scores, axis=0, keepdims=True)
        weights = jnp.exp2((scores - top) * RATE)
        cut = pl.ds(first, 256)
        state[0:1, cut], state[1:2, cut], acc[:, cut] = merge(
            state[0:1, cut],
            state[1:2, cut],
            acc[:, cut],
            top,
            jnp.sum(weights, axis=0, keepdims=True),
            nn(vt_ref[:, pl.ds(start, SEG)], weights.astype(BF)),
        )
        return carry

    lax.fori_loop(4, 6, body, 0, unroll=2)
    combined = acc[...] / state[1:2]
    comb_ref[...] = combined.astype(BF)
    stat_ref[0:1] = state[0:1] * RATE + jnp.log2(state[1:2])
    stat_ref[1:2] = jnp.sum(flip(x_ref[3]).astype(F32) * combined, axis=0, keepdims=True)
    middle = slice(LOW, LOW + MID)
    near = (state[0:1, middle], state[1:2, middle], acc[:, middle])
    near = merge(*near, *forward_of(x_ref[0, middle], vt_ref[:, middle], x_ref[2, middle]))
    inner = slice(LOW + 64, LOW + 192)
    peak, total, summed = forward_of(x_ref[0, inner], flip(x_ref[1, inner]), x_ref[2, inner])
    near = merge(*near, widen(peak, NEG), widen(total, 0.0), widen(summed, 0.0))
    mid_stat_ref[0:1], mid_stat_ref[1:2], mid_acc_ref[...] = near


def widen(part, filler):
    return pltpu.roll(jnp.concatenate([part, jnp.full_like(part, filler)], axis=1), 64, 1)


def narrow(whole):
    return pltpu.roll(whole, MID - 64, 1)[:, :128]


def forward_of(keys, values_flipped, queries):
    scores = nt(keys, queries)
    peak = jnp.max(scores, axis=0, keepdims=True)
    weights = jnp.exp2((scores - peak) * RATE)
    return (
        peak,
        jnp.sum(weights, axis=0, keepdims=True),
        nn(values_flipped, weights.astype(BF)),
    )


def backward_of(keys, values, queries, grads, log_total, dot):
    probs = jnp.exp2(nt(keys, queries) * RATE - log_total)
    score_grad = (probs * (nt(values, grads) - dot)).astype(BF)
    return (
        nn(flip(keys), score_grad),
        nn(score_grad, queries),
        nn(probs.astype(BF), grads),
    )


def join(whole, part):
    return jnp.concatenate([whole[:64], whole[64:192] + part, whole[192:]], axis=0)


def forward_kernel(mid_ref, stat_ref, acc_ref, two_ref, three_ref, out_stat_ref, out_acc_ref):
    keys = jnp.concatenate([two_ref[0], three_ref[0]], axis=0)
    values = jnp.concatenate([two_ref[1], three_ref[1]], axis=0)
    peak, total, summed = forward_of(keys, flip(values), mid_ref[2, 64:192])
    out_stat_ref[0:1], out_stat_ref[1:2], out_acc_ref[...] = merge(
        stat_ref[0:1], stat_ref[1:2], acc_ref[...],
        widen(peak, NEG), widen(total, 0.0), widen(summed, 0.0),
    )


def far_kernel(mid_ref, stat_ref, acc_ref, one_ref, two_ref, three_ref,
               out_stat_ref, comb_ref, query_ref, send_one_ref, send_two_ref, send_three_ref):
    keys3 = jnp.concatenate([one_ref[0, 64:192], two_ref[0], three_ref[0]], axis=0)
    values3 = jnp.concatenate([one_ref[1, 64:192], two_ref[1], three_ref[1]], axis=0)
    grads2 = mid_ref[3]
    queries3, grads3 = mid_ref[2, 64:192], mid_ref[3, 64:192]
    state = (stat_ref[0:1], stat_ref[1:2], acc_ref[...])
    flipped = flip(one_ref[1])
    state = merge(*state, *forward_of(one_ref[0], flipped, mid_ref[2]))
    peak, total, summed = forward_of(one_ref[0, 64:192], flip(one_ref[1, 64:192]), queries3)
    peak, total, acc = merge(*state, widen(peak, NEG), widen(total, 0.0), widen(summed, 0.0))
    combined = acc / total
    log_total = peak * RATE + jnp.log2(total)
    dot = jnp.sum(flip(grads2).astype(F32) * combined, axis=0, keepdims=True)
    out_stat_ref[0:1] = log_total
    out_stat_ref[1:2] = dot
    comb_ref[...] = combined.astype(BF)
    dq2, dk2, dv2 = backward_of(one_ref[0], one_ref[1], mid_ref[2], grads2, log_total, dot)
    dq3, dk3, dv3 = backward_of(keys3, values3, queries3, grads3, narrow(log_total), narrow(dot))
    query_ref[...] = dq2 + widen(dq3, 0.0)
    for index, (near, far, scale) in enumerate(((dk2, dk3, SCALE), (dv2, dv3, 1.0))):
        send_one_ref[index] = (join(near, far[:128]) * scale).astype(BF)
        send_two_ref[index] = (far[128:256] * scale).astype(BF)
        send_three_ref[index] = (far[256:] * scale).astype(BF)


def back_kernel(x_ref, stat_ref, comb_ref, mid_stat_ref, mid_comb_ref, mid_query_ref,
                out_ref, mid_grad_ref, kt, stat, dq, dk, dv):
    offset = head_offset()
    kt[...] = flip(x_ref[0])
    stat[...] = stat_ref[...]
    stat[:, LOW : LOW + MID] = mid_stat_ref[...]
    dq[...] = jnp.zeros_like(dq)
    dk[...] = jnp.zeros_like(dk)
    dv[...] = jnp.zeros_like(dv)

    def body(step, carry):
        start, first = segment_start(step)
        keys, values = x_ref[0, pl.ds(start, SEG)], x_ref[1, pl.ds(start, SEG)]
        queries, grads = x_ref[2, pl.ds(first, 256)], x_ref[3, pl.ds(first, 256)]
        cut = pl.ds(first, 256)
        probs = jnp.exp2(nt(keys, queries) * RATE - stat[0:1, cut])
        score_grad = (probs * (nt(values, grads) - stat[1:2, cut])).astype(BF)
        dq[:, cut] += nn(kt[:, pl.ds(start, SEG)], score_grad)
        dk[pl.ds(start, SEG)] += nn(score_grad, queries)
        dv[pl.ds(start, SEG)] += nn(probs.astype(BF), grads)
        return carry

    lax.fori_loop(0, 6, body, 0, unroll=6)
    for first, last in ((LOW, LOW + MID), (LOW + 64, LOW + 192)):
        cut = slice(first, last)
        log_total, dot = stat[0:1, LOW : LOW + MID], stat[1:2, LOW : LOW + MID]
        if last - first < MID:
            log_total, dot = narrow(log_total), narrow(dot)
        part, key_part, value_part = backward_of(
            x_ref[0, cut], x_ref[1, cut], x_ref[2, cut], x_ref[3, cut], log_total, dot
        )
        dq[:, LOW : LOW + MID] += part if last - first == MID else widen(part, 0.0)
        dk[cut] += key_part
        dv[cut] += value_part
    mid_grad_ref[0] = dk[LOW : LOW + MID] * SCALE
    mid_grad_ref[1] = dv[LOW : LOW + MID]
    dq[:, LOW : LOW + MID] += mid_query_ref[...]
    query = (dq[...] * SCALE).astype(BF)
    comb = jnp.concatenate(
        [comb_ref[:, :LOW], mid_comb_ref[...], comb_ref[:, LOW + MID :]], axis=1
    )
    both = jnp.concatenate([comb, query], axis=0)
    for half in range(2):
        plain = nt(unordering(offset, half, 0, SEG), both[:, half * SEG : half * SEG + SEG]).astype(BF)
        put_half(out_ref, half, 0, plain[:, :HEAD_DIM])
        put_half(out_ref, half, 1, plain[:, HEAD_DIM:])
        outer = slice(0, LOW) if half == 0 else slice(LOW + MID, TOKENS)
        pair = jnp.concatenate([dk[outer] * SCALE, dv[outer]], axis=1).astype(BF)
        plain = nn(unordering(offset, half, 0 if half == 0 else 128, LOW), pair).astype(BF)
        put_half(out_ref, half, 2, plain[:, :HEAD_DIM])
        put_half(out_ref, half, 3, plain[:, HEAD_DIM:])


def finish_kernel(in_ref, mid_grad_ref, one_ref, two_ref, three_ref, out_ref):
    offset = head_offset()
    grads = []
    for index in range(2):
        near = mid_grad_ref[index] + one_ref[index].astype(F32)
        far = two_ref[index].astype(F32) + three_ref[index].astype(F32)
        grads.append(join(near, far).astype(BF))
    pair = jnp.concatenate(grads, axis=1)
    for half in range(2):
        cut = slice(half * 128, half * 128 + 128)
        plain = nn(unordering(offset, half, LOW if half == 0 else 0, 128), pair[cut]).astype(BF)
        for index in range(2):
            part = plain[:, index * HEAD_DIM : (index + 1) * HEAD_DIM]
            put_half(out_ref, half, index, half_of(in_ref, half, index) + part)


def shape(dims, kind):
    return jax.ShapeDtypeStruct(dims, kind)


PARAMS = pltpu.CompilerParams(vmem_limit_bytes=32 * 1024 * 1024)


def whole(array):
    return pl.BlockSpec(array.shape, lambda: (0,) * len(array.shape))


def call(kernel, outs, args, scratch=(), flops=0):
    return pl.pallas_call(
        kernel,
        out_shape=outs,
        scratch_shapes=list(scratch),
        compiler_params=PARAMS,
        cost_estimate=pl.CostEstimate(flops=flops, bytes_accessed=2 << 20, transcendentals=0),
    )(*args)


def pack(arrays):
    return pl.pallas_call(
        pack_kernel,
        in_specs=[pl.BlockSpec(memory_space=pl.ANY)] * 4,
        out_shape=shape((PLANE, 4, ROWS, HEAD_DIM), BF),
        scratch_shapes=[
            pltpu.VMEM((4, ROWS, PLANE * HEAD_DIM), BF),
            pltpu.SemaphoreType.DMA((4,)),
        ],
        compiler_params=PARAMS,
    )(*[pltpu.with_memory_space_constraint(array, pltpu.HBM) for array in arrays])


def unpack(packed):
    return pl.pallas_call(
        unpack_kernel,
        out_specs=[pl.BlockSpec(memory_space=pl.ANY)] * 4,
        out_shape=[shape((ROWS, PLANE * HEAD_DIM), BF)] * 4,
        scratch_shapes=[
            pltpu.VMEM((4, ROWS, PLANE * HEAD_DIM), BF),
            pltpu.SemaphoreType.DMA((4,)),
        ],
        compiler_params=PARAMS,
    )(packed)


def plane_exchange(packed):
    return lax.all_to_all(packed, ("x", "y_lo", "y_hi", "core"), split_axis=0, concat_axis=0, tiled=True)


def z_exchange(block, apart):
    count = lax.axis_size("zed")
    return lax.ppermute(block, "zed", [(at, at ^ apart) for at in range(count)])


def per_device(query_rows, key_rows, value_rows, grad_rows):
    got = plane_exchange(pack([key_rows, value_rows, query_rows, grad_rows]))
    half_block = pl.BlockSpec((PLANE, 2, ROWS, HEAD_DIM), lambda i: (0, 0, 0, 0))
    near = pl.pallas_call(
        select_kernel,
        grid=(1,),
        in_specs=[half_block],
        out_specs=pl.BlockSpec((2, MID, HEAD_DIM), lambda i: (0, 0, 0)),
        out_shape=shape((2, MID, HEAD_DIM), BF),
        compiler_params=PARAMS,
    )(got)
    inner = near[:, 64:192]
    one = z_exchange(near, 1)
    two = z_exchange(inner, 2)
    three = z_exchange(inner, 3)
    ordered, mid, vt, state, acc = call(
        first_kernel,
        [
            shape((4, TOKENS, HEAD_DIM), BF),
            shape((4, MID, HEAD_DIM), BF),
            shape((HEAD_DIM, TOKENS), BF),
            shape((2, TOKENS), F32),
            shape((HEAD_DIM, TOKENS), F32),
        ],
        [got],
        flops=2 * 4 * SEG * SEG * HEAD_DIM,
    )
    stat, comb, mid_stat, mid_acc = call(
        second_kernel,
        [
            shape((2, TOKENS), F32),
            shape((HEAD_DIM, TOKENS), BF),
            shape((2, MID), F32),
            shape((HEAD_DIM, MID), F32),
        ],
        [ordered, vt, state, acc],
        [pltpu.VMEM((2, TOKENS), F32), pltpu.VMEM((HEAD_DIM, TOKENS), F32)],
        flops=4 * SEG * SEG * HEAD_DIM,
    )
    mid_stat, mid_acc = call(
        forward_kernel,
        [shape((2, MID), F32), shape((HEAD_DIM, MID), F32)],
        [mid, mid_stat, mid_acc, two, three],
        flops=8 * 4 * SEG * SEG * HEAD_DIM,
    )
    mid_out_stat, mid_comb, mid_query, send_one, send_two, send_three = call(
        far_kernel,
        [
            shape((2, MID), F32),
            shape((HEAD_DIM, MID), BF),
            shape((HEAD_DIM, MID), F32),
            shape((2, MID, HEAD_DIM), BF),
            shape((2, 128, HEAD_DIM), BF),
            shape((2, 128, HEAD_DIM), BF),
        ],
        [mid, mid_stat, mid_acc, one, two, three],
        flops=2 * 4 * SEG * SEG * HEAD_DIM,
    )
    back_one = z_exchange(send_one, 1)
    back_two = z_exchange(send_two, 2)
    back_three = z_exchange(send_three, 3)
    packed, mid_grad = call(
        back_kernel,
        [shape((PLANE, 4, ROWS, HEAD_DIM), BF), shape((2, MID, HEAD_DIM), F32)],
        [ordered, stat, comb, mid_out_stat, mid_comb, mid_query],
        [
            pltpu.VMEM((HEAD_DIM, TOKENS), BF),
            pltpu.VMEM((2, TOKENS), F32),
            pltpu.VMEM((HEAD_DIM, TOKENS), F32),
            pltpu.VMEM((TOKENS, HEAD_DIM), F32),
            pltpu.VMEM((TOKENS, HEAD_DIM), F32),
        ],
        flops=3 * 10 * SEG * SEG * HEAD_DIM,
    )
    upper_half = pl.BlockSpec((PLANE, 2, ROWS, HEAD_DIM), lambda i: (0, 1, 0, 0))
    mid_block = pl.BlockSpec((2, MID, HEAD_DIM), lambda i: (0, 0, 0))
    inner_block = pl.BlockSpec((2, 128, HEAD_DIM), lambda i: (0, 0, 0))
    packed = pl.pallas_call(
        finish_kernel,
        grid=(1,),
        in_specs=[upper_half, mid_block, mid_block, inner_block, inner_block],
        out_specs=upper_half,
        out_shape=shape((PLANE, 4, ROWS, HEAD_DIM), BF),
        input_output_aliases={0: 0},
        compiler_params=PARAMS,
    )(packed, mid_grad, back_one, back_two, back_three)
    return tuple(unpack(plane_exchange(packed)))


def solution(mesh):
    axes = ("zed", "y_lo", "core", "y_hi", "x")
    planes = Mesh(mesh.devices.reshape(-1, 2, 2, 2, 4), axes)
    spec = P(axes, None)
    return jax.shard_map(
        per_device, mesh=planes, in_specs=(spec,) * 4, out_specs=(spec,) * 4, check_vma=False
    )
```

```python
import functools

import jax
import jax.numpy as jnp
from jax import lax
from jax.experimental import pallas as pl
from jax.experimental.pallas import tpu as pltpu
from jax.sharding import Mesh, PartitionSpec as P

HEAD_DIM = 128
PLANE = 32
ROWS = 32
TOKENS = PLANE * ROWS
SEG = 512
MID = 256
LOW = 384
SCALE = HEAD_DIM**-0.5
RATE = SCALE * 1.4426950408889634
NEG = -1e30
BF = jnp.bfloat16
F32 = jnp.float32

ORDER = [
    y_lo * 16 + core * 8 + y_hi * 4 + x
    for x in range(4)
    for y_lo in range(2)
    for y_hi in range(2)
    for core in range(2)
]
PLACE = [ORDER.index(device) for device in range(PLANE)]


def nn(a, b):
    return jnp.dot(a, b, preferred_element_type=F32)


def nt(a, b):
    return lax.dot_general(a, b, (((1,), (1,)), ((), ())), preferred_element_type=F32)


def flip(a):
    return jnp.swapaxes(a, 0, 1)


def token_of(spot, offset, half):
    if half == 0:
        far = [2 * spot, 4 * (spot - 256), 8 * (spot - 384), 8 * (spot - 448)]
        tests = [spot < 256, spot < 384, spot < 448]
    else:
        far = [2 * (spot - 256), 4 * (spot - 128), 8 * (spot - 64), 8 * spot]
        tests = [spot >= 256, spot >= 128, spot >= 64]
    return jnp.where(
        tests[0],
        far[0] + ((offset + 1) & 1),
        jnp.where(
            tests[1],
            far[1] + ((offset + 2) & 3),
            jnp.where(tests[2], far[2] + ((offset + 4) & 7), far[3] + offset),
        ),
    )


def ordering(offset, half, first, count):
    spot = lax.broadcasted_iota(jnp.int32, (count, 1), 0) + first
    token = lax.broadcasted_iota(jnp.int32, (count, SEG), 1)
    return jnp.where(token_of(spot, offset, half) == token, 1.0, 0.0).astype(BF)


def unordering(offset, half, first, count):
    spot = lax.broadcasted_iota(jnp.int32, (1, count), 1) + first
    token = lax.broadcasted_iota(jnp.int32, (SEG, count), 0)
    return jnp.where(token_of(spot, offset, half) == token, 1.0, 0.0).astype(BF)


def head_offset():
    return lax.axis_index("y_hi") * 4 + lax.axis_index("x")


def half_of(ref, half, index):
    return jnp.concatenate([ref[PLACE[block], index] for block in range(half * 16, half * 16 + 16)], axis=0)


def put_half(ref, half, index, value):
    for block in range(16):
        ref[PLACE[half * 16 + block], index] = value[block * ROWS : block * ROWS + ROWS]


def pack_kernel(key_ref, value_ref, query_ref, grad_ref, out_ref, held, arrived):
    copies = [
        pltpu.make_async_copy(source, held.at[index], arrived.at[index])
        for index, source in enumerate((key_ref, value_ref, query_ref, grad_ref))
    ]
    for copy in copies:
        copy.start()
    for index, copy in enumerate(copies):
        copy.wait()
        for head in range(PLANE):
            out_ref[PLACE[head], index] = held[index, :, head * HEAD_DIM : (head + 1) * HEAD_DIM]


def unpack_kernel(in_ref, att_ref, query_ref, key_ref, value_ref, held, sent):
    copies = []
    for index, target in enumerate((att_ref, query_ref, key_ref, value_ref)):
        for head in range(PLANE):
            held[index, :, head * HEAD_DIM : (head + 1) * HEAD_DIM] = in_ref[PLACE[head], index]
        copies.append(pltpu.make_async_copy(held.at[index], target, sent.at[index]))
        copies[-1].start()
    for copy in copies:
        copy.wait()


def select_kernel(got_ref, out_ref):
    offset = head_offset()
    for half in range(2):
        pair = jnp.concatenate([half_of(got_ref, half, 0), half_of(got_ref, half, 1)], axis=1)
        picked = nn(ordering(offset, half, LOW if half == 0 else 0, 128), pair).astype(BF)
        out_ref[0, half * 128 : half * 128 + 128] = picked[:, :HEAD_DIM]
        out_ref[1, half * 128 : half * 128 + 128] = picked[:, HEAD_DIM:]


def segment_start(step):
    segment = step // 2
    start = jnp.where(segment == 2, 256, segment * SEG)
    return pl.multiple_of(start, 256), pl.multiple_of(start + (step % 2) * 256, 256)


def merge(peak, total, acc, peak_new, total_new, acc_new):
    best = jnp.maximum(peak, peak_new)
    left = jnp.exp2((peak - best) * RATE)
    right = jnp.exp2((peak_new - best) * RATE)
    return best, left * total + right * total_new, left * acc + right * acc_new


def first_kernel(got_ref, x_ref, mid_ref, vt_ref, state_ref, acc_ref):
    offset = head_offset()
    for half in range(2):
        four = jnp.concatenate([half_of(got_ref, half, index) for index in range(4)], axis=1)
        ordered = nn(ordering(offset, half, 0, SEG), four).astype(BF)
        for index in range(4):
            x_ref[index, half * SEG : half * SEG + SEG] = ordered[
                :, index * HEAD_DIM : (index + 1) * HEAD_DIM
            ]
        vt_ref[:, half * SEG : half * SEG + SEG] = flip(ordered[:, HEAD_DIM : 2 * HEAD_DIM])
    for index in range(4):
        mid_ref[index] = x_ref[index, LOW : LOW + MID]

    def body(step, carry):
        start, first = segment_start(step)
        scores = nt(x_ref[0, pl.ds(start, SEG)], x_ref[2, pl.ds(first, 256)])
        peak = jnp.max(scores, axis=0, keepdims=True)
        weights = jnp.exp2((scores - peak) * RATE)
        cut = pl.ds(first, 256)
        state_ref[0:1, cut] = peak
        state_ref[1:2, cut] = jnp.sum(weights, axis=0, keepdims=True)
        acc_ref[:, cut] = nn(vt_ref[:, pl.ds(start, SEG)], weights.astype(BF))
        return carry

    lax.fori_loop(0, 4, body, 0, unroll=4)


def second_kernel(x_ref, vt_ref, state_in, acc_in, stat_ref, comb_ref, mid_stat_ref, mid_acc_ref, state, acc):
    state[...] = state_in[...]
    acc[...] = acc_in[...]

    def body(step, carry):
        start, first = segment_start(step)
        scores = nt(x_ref[0, pl.ds(start, SEG)], x_ref[2, pl.ds(first, 256)])
        top = jnp.max(scores, axis=0, keepdims=True)
        weights = jnp.exp2((scores - top) * RATE)
        cut = pl.ds(first, 256)
        state[0:1, cut], state[1:2, cut], acc[:, cut] = merge(
            state[0:1, cut],
            state[1:2, cut],
            acc[:, cut],
            top,
            jnp.sum(weights, axis=0, keepdims=True),
            nn(vt_ref[:, pl.ds(start, SEG)], weights.astype(BF)),
        )
        return carry

    lax.fori_loop(4, 6, body, 0, unroll=2)
    combined = acc[...] / state[1:2]
    comb_ref[...] = combined.astype(BF)
    stat_ref[0:1] = state[0:1] * RATE + jnp.log2(state[1:2])
    stat_ref[1:2] = jnp.sum(flip(x_ref[3]).astype(F32) * combined, axis=0, keepdims=True)
    middle = slice(LOW, LOW + MID)
    near = (state[0:1, middle], state[1:2, middle], acc[:, middle])
    near = merge(*near, *forward_of(x_ref[0, middle], vt_ref[:, middle], x_ref[2, middle]))
    inner = slice(LOW + 64, LOW + 192)
    peak, total, summed = forward_of(x_ref[0, inner], flip(x_ref[1, inner]), x_ref[2, inner])
    near = merge(*near, widen(peak, NEG), widen(total, 0.0), widen(summed, 0.0))
    mid_stat_ref[0:1], mid_stat_ref[1:2], mid_acc_ref[...] = near


def widen(part, filler):
    return pltpu.roll(jnp.concatenate([part, jnp.full_like(part, filler)], axis=1), 64, 1)


def narrow(whole):
    return pltpu.roll(whole, MID - 64, 1)[:, :128]


def forward_of(keys, values_flipped, queries):
    scores = nt(keys, queries)
    peak = jnp.max(scores, axis=0, keepdims=True)
    weights = jnp.exp2((scores - peak) * RATE)
    return (
        peak,
        jnp.sum(weights, axis=0, keepdims=True),
        nn(values_flipped, weights.astype(BF)),
    )


def backward_of(keys, values, queries, grads, log_total, dot):
    probs = jnp.exp2(nt(keys, queries) * RATE - log_total)
    score_grad = (probs * (nt(values, grads) - dot)).astype(BF)
    return (
        nn(flip(keys), score_grad),
        nn(score_grad, queries),
        nn(probs.astype(BF), grads),
    )


def join(whole, part):
    return jnp.concatenate([whole[:64], whole[64:192] + part, whole[192:]], axis=0)


def forward_kernel(mid_ref, stat_ref, acc_ref, one_ref, out_stat_ref, out_acc_ref):
    state = (stat_ref[0:1], stat_ref[1:2], acc_ref[...])
    state = merge(*state, *forward_of(one_ref[0], flip(one_ref[1]), mid_ref[2]))
    peak, total, summed = forward_of(one_ref[0, 64:192], flip(one_ref[1, 64:192]), mid_ref[2, 64:192])
    out_stat_ref[0:1], out_stat_ref[1:2], out_acc_ref[...] = merge(
        *state, widen(peak, NEG), widen(total, 0.0), widen(summed, 0.0)
    )


def far_kernel(mid_ref, stat_ref, acc_ref, one_ref, two_ref, three_ref,
               out_stat_ref, comb_ref, query_ref, send_one_ref, send_two_ref, send_three_ref):
    keys3 = jnp.concatenate([one_ref[0, 64:192], two_ref[0], three_ref[0]], axis=0)
    values3 = jnp.concatenate([one_ref[1, 64:192], two_ref[1], three_ref[1]], axis=0)
    grads2 = mid_ref[3]
    queries3, grads3 = mid_ref[2, 64:192], mid_ref[3, 64:192]
    state = (stat_ref[0:1], stat_ref[1:2], acc_ref[...])
    peak, total, summed = forward_of(keys3[128:], flip(values3[128:]), queries3)
    peak, total, acc = merge(*state, widen(peak, NEG), widen(total, 0.0), widen(summed, 0.0))
    combined = acc / total
    log_total = peak * RATE + jnp.log2(total)
    dot = jnp.sum(flip(grads2).astype(F32) * combined, axis=0, keepdims=True)
    out_stat_ref[0:1] = log_total
    out_stat_ref[1:2] = dot
    comb_ref[...] = combined.astype(BF)
    dq2, dk2, dv2 = backward_of(one_ref[0], one_ref[1], mid_ref[2], grads2, log_total, dot)
    dq3, dk3, dv3 = backward_of(keys3, values3, queries3, grads3, narrow(log_total), narrow(dot))
    query_ref[...] = dq2 + widen(dq3, 0.0)
    for index, (near, far, scale) in enumerate(((dk2, dk3, SCALE), (dv2, dv3, 1.0))):
        send_one_ref[index] = (join(near, far[:128]) * scale).astype(BF)
        send_two_ref[index] = (far[128:256] * scale).astype(BF)
        send_three_ref[index] = (far[256:] * scale).astype(BF)


def back_kernel(x_ref, stat_ref, comb_ref, mid_stat_ref, mid_comb_ref, mid_query_ref,
                out_ref, mid_grad_ref, kt, stat, dq, dk, dv):
    offset = head_offset()
    kt[...] = flip(x_ref[0])
    stat[...] = stat_ref[...]
    stat[:, LOW : LOW + MID] = mid_stat_ref[...]
    dq[...] = jnp.zeros_like(dq)
    dk[...] = jnp.zeros_like(dk)
    dv[...] = jnp.zeros_like(dv)

    def body(step, carry):
        start, first = segment_start(step)
        keys, values = x_ref[0, pl.ds(start, SEG)], x_ref[1, pl.ds(start, SEG)]
        queries, grads = x_ref[2, pl.ds(first, 256)], x_ref[3, pl.ds(first, 256)]
        cut = pl.ds(first, 256)
        probs = jnp.exp2(nt(keys, queries) * RATE - stat[0:1, cut])
        score_grad = (probs * (nt(values, grads) - stat[1:2, cut])).astype(BF)
        dq[:, cut] += nn(kt[:, pl.ds(start, SEG)], score_grad)
        dk[pl.ds(start, SEG)] += nn(score_grad, queries)
        dv[pl.ds(start, SEG)] += nn(probs.astype(BF), grads)
        return carry

    lax.fori_loop(0, 6, body, 0, unroll=6)
    for first, last in ((LOW, LOW + MID), (LOW + 64, LOW + 192)):
        cut = slice(first, last)
        log_total, dot = stat[0:1, LOW : LOW + MID], stat[1:2, LOW : LOW + MID]
        if last - first < MID:
            log_total, dot = narrow(log_total), narrow(dot)
        part, key_part, value_part = backward_of(
            x_ref[0, cut], x_ref[1, cut], x_ref[2, cut], x_ref[3, cut], log_total, dot
        )
        dq[:, LOW : LOW + MID] += part if last - first == MID else widen(part, 0.0)
        dk[cut] += key_part
        dv[cut] += value_part
    mid_grad_ref[0] = dk[LOW : LOW + MID] * SCALE
    mid_grad_ref[1] = dv[LOW : LOW + MID]
    dq[:, LOW : LOW + MID] += mid_query_ref[...]
    query = (dq[...] * SCALE).astype(BF)
    comb = jnp.concatenate(
        [comb_ref[:, :LOW], mid_comb_ref[...], comb_ref[:, LOW + MID :]], axis=1
    )
    both = jnp.concatenate([comb, query], axis=0)
    for half in range(2):
        plain = nt(unordering(offset, half, 0, SEG), both[:, half * SEG : half * SEG + SEG]).astype(BF)
        put_half(out_ref, half, 0, plain[:, :HEAD_DIM])
        put_half(out_ref, half, 1, plain[:, HEAD_DIM:])
        outer = slice(0, LOW) if half == 0 else slice(LOW + MID, TOKENS)
        pair = jnp.concatenate([dk[outer] * SCALE, dv[outer]], axis=1).astype(BF)
        plain = nn(unordering(offset, half, 0 if half == 0 else 128, LOW), pair).astype(BF)
        put_half(out_ref, half, 2, plain[:, :HEAD_DIM])
        put_half(out_ref, half, 3, plain[:, HEAD_DIM:])


def finish_kernel(in_ref, mid_grad_ref, one_ref, two_ref, three_ref, out_ref):
    offset = head_offset()
    grads = []
    for index in range(2):
        near = mid_grad_ref[index] + one_ref[index].astype(F32)
        far = two_ref[index].astype(F32) + three_ref[index].astype(F32)
        grads.append(join(near, far).astype(BF))
    pair = jnp.concatenate(grads, axis=1)
    for half in range(2):
        cut = slice(half * 128, half * 128 + 128)
        plain = nn(unordering(offset, half, LOW if half == 0 else 0, 128), pair[cut]).astype(BF)
        for index in range(2):
            part = plain[:, index * HEAD_DIM : (index + 1) * HEAD_DIM]
            put_half(out_ref, half, index, half_of(in_ref, half, index) + part)


def shape(dims, kind):
    return jax.ShapeDtypeStruct(dims, kind)


PARAMS = pltpu.CompilerParams(vmem_limit_bytes=32 * 1024 * 1024)


def whole(array):
    return pl.BlockSpec(array.shape, lambda: (0,) * len(array.shape))


def call(kernel, outs, args, scratch=(), flops=0):
    return pl.pallas_call(
        kernel,
        out_shape=outs,
        scratch_shapes=list(scratch),
        compiler_params=PARAMS,
        cost_estimate=pl.CostEstimate(flops=flops, bytes_accessed=2 << 20, transcendentals=0),
    )(*args)


def pack(arrays):
    return pl.pallas_call(
        pack_kernel,
        in_specs=[pl.BlockSpec(memory_space=pl.ANY)] * 4,
        out_shape=shape((PLANE, 4, ROWS, HEAD_DIM), BF),
        scratch_shapes=[
            pltpu.VMEM((4, ROWS, PLANE * HEAD_DIM), BF),
            pltpu.SemaphoreType.DMA((4,)),
        ],
        compiler_params=PARAMS,
    )(*[pltpu.with_memory_space_constraint(array, pltpu.HBM) for array in arrays])


def unpack(packed):
    return pl.pallas_call(
        unpack_kernel,
        out_specs=[pl.BlockSpec(memory_space=pl.ANY)] * 4,
        out_shape=[shape((ROWS, PLANE * HEAD_DIM), BF)] * 4,
        scratch_shapes=[
            pltpu.VMEM((4, ROWS, PLANE * HEAD_DIM), BF),
            pltpu.SemaphoreType.DMA((4,)),
        ],
        compiler_params=PARAMS,
    )(packed)


def plane_exchange(packed):
    return lax.all_to_all(packed, ("x", "y_lo", "y_hi", "core"), split_axis=0, concat_axis=0, tiled=True)


def z_exchange(block, apart):
    count = lax.axis_size("zed")
    return lax.ppermute(block, "zed", [(at, at ^ apart) for at in range(count)])


def per_device(query_rows, key_rows, value_rows, grad_rows):
    got = plane_exchange(pack([key_rows, value_rows, query_rows, grad_rows]))
    half_block = pl.BlockSpec((PLANE, 2, ROWS, HEAD_DIM), lambda i: (0, 0, 0, 0))
    near = pl.pallas_call(
        select_kernel,
        grid=(1,),
        in_specs=[half_block],
        out_specs=pl.BlockSpec((2, MID, HEAD_DIM), lambda i: (0, 0, 0)),
        out_shape=shape((2, MID, HEAD_DIM), BF),
        compiler_params=PARAMS,
    )(got)
    inner = near[:, 64:192]
    one = z_exchange(near, 1)
    two = z_exchange(inner, 2)
    three = z_exchange(inner, 3)
    ordered, mid, vt, state, acc = call(
        first_kernel,
        [
            shape((4, TOKENS, HEAD_DIM), BF),
            shape((4, MID, HEAD_DIM), BF),
            shape((HEAD_DIM, TOKENS), BF),
            shape((2, TOKENS), F32),
            shape((HEAD_DIM, TOKENS), F32),
        ],
        [got],
        flops=2 * 4 * SEG * SEG * HEAD_DIM,
    )
    stat, comb, mid_stat, mid_acc = call(
        second_kernel,
        [
            shape((2, TOKENS), F32),
            shape((HEAD_DIM, TOKENS), BF),
            shape((2, MID), F32),
            shape((HEAD_DIM, MID), F32),
        ],
        [ordered, vt, state, acc],
        [pltpu.VMEM((2, TOKENS), F32), pltpu.VMEM((HEAD_DIM, TOKENS), F32)],
        flops=4 * SEG * SEG * HEAD_DIM,
    )
    mid_stat, mid_acc = call(
        forward_kernel,
        [shape((2, MID), F32), shape((HEAD_DIM, MID), F32)],
        [mid, mid_stat, mid_acc, one],
        flops=8 * 4 * SEG * SEG * HEAD_DIM,
    )
    mid_out_stat, mid_comb, mid_query, send_one, send_two, send_three = call(
        far_kernel,
        [
            shape((2, MID), F32),
            shape((HEAD_DIM, MID), BF),
            shape((HEAD_DIM, MID), F32),
            shape((2, MID, HEAD_DIM), BF),
            shape((2, 128, HEAD_DIM), BF),
            shape((2, 128, HEAD_DIM), BF),
        ],
        [mid, mid_stat, mid_acc, one, two, three],
        flops=2 * 4 * SEG * SEG * HEAD_DIM,
    )
    back_one = z_exchange(send_one, 1)
    back_two = z_exchange(send_two, 2)
    back_three = z_exchange(send_three, 3)
    packed, mid_grad = call(
        back_kernel,
        [shape((PLANE, 4, ROWS, HEAD_DIM), BF), shape((2, MID, HEAD_DIM), F32)],
        [ordered, stat, comb, mid_out_stat, mid_comb, mid_query],
        [
            pltpu.VMEM((HEAD_DIM, TOKENS), BF),
            pltpu.VMEM((2, TOKENS), F32),
            pltpu.VMEM((HEAD_DIM, TOKENS), F32),
            pltpu.VMEM((TOKENS, HEAD_DIM), F32),
            pltpu.VMEM((TOKENS, HEAD_DIM), F32),
        ],
        flops=3 * 10 * SEG * SEG * HEAD_DIM,
    )
    upper_half = pl.BlockSpec((PLANE, 2, ROWS, HEAD_DIM), lambda i: (0, 1, 0, 0))
    mid_block = pl.BlockSpec((2, MID, HEAD_DIM), lambda i: (0, 0, 0))
    inner_block = pl.BlockSpec((2, 128, HEAD_DIM), lambda i: (0, 0, 0))
    packed = pl.pallas_call(
        finish_kernel,
        grid=(1,),
        in_specs=[upper_half, mid_block, mid_block, inner_block, inner_block],
        out_specs=upper_half,
        out_shape=shape((PLANE, 4, ROWS, HEAD_DIM), BF),
        input_output_aliases={0: 0},
        compiler_params=PARAMS,
    )(packed, mid_grad, back_one, back_two, back_three)
    return tuple(unpack(plane_exchange(packed)))


def solution(mesh):
    axes = ("zed", "y_lo", "core", "y_hi", "x")
    planes = Mesh(mesh.devices.reshape(-1, 2, 2, 2, 4), axes)
    spec = P(axes, None)
    return jax.shard_map(
        per_device, mesh=planes, in_specs=(spec,) * 4, out_specs=(spec,) * 4, check_vma=False
    )
```

```python
import functools

import jax
import jax.numpy as jnp
from jax import lax
from jax.experimental import pallas as pl
from jax.experimental.pallas import tpu as pltpu
from jax.sharding import Mesh, PartitionSpec as P

HEAD_DIM = 128
PLANE = 32
ROWS = 32
TOKENS = PLANE * ROWS
SEG = 512
MID = 256
LOW = 384
SCALE = HEAD_DIM**-0.5
RATE = SCALE * 1.4426950408889634
NEG = -1e30
BF = jnp.bfloat16
F32 = jnp.float32

ORDER = [
    y_lo * 16 + core * 8 + y_hi * 4 + x
    for x in range(4)
    for y_lo in range(2)
    for y_hi in range(2)
    for core in range(2)
]
PLACE = [ORDER.index(device) for device in range(PLANE)]


def nn(a, b):
    return jnp.dot(a, b, preferred_element_type=F32)


def nt(a, b):
    return lax.dot_general(a, b, (((1,), (1,)), ((), ())), preferred_element_type=F32)


def flip(a):
    return jnp.swapaxes(a, 0, 1)


def token_of(spot, offset, half):
    if half == 0:
        far = [2 * spot, 4 * (spot - 256), 8 * (spot - 384), 8 * (spot - 448)]
        tests = [spot < 256, spot < 384, spot < 448]
    else:
        far = [2 * (spot - 256), 4 * (spot - 128), 8 * (spot - 64), 8 * spot]
        tests = [spot >= 256, spot >= 128, spot >= 64]
    return jnp.where(
        tests[0],
        far[0] + ((offset + 1) & 1),
        jnp.where(
            tests[1],
            far[1] + ((offset + 2) & 3),
            jnp.where(tests[2], far[2] + ((offset + 4) & 7), far[3] + offset),
        ),
    )


def ordering(offset, half, first, count):
    spot = lax.broadcasted_iota(jnp.int32, (count, 1), 0) + first
    token = lax.broadcasted_iota(jnp.int32, (count, SEG), 1)
    return jnp.where(token_of(spot, offset, half) == token, 1.0, 0.0).astype(BF)


def unordering(offset, half, first, count):
    spot = lax.broadcasted_iota(jnp.int32, (1, count), 1) + first
    token = lax.broadcasted_iota(jnp.int32, (SEG, count), 0)
    return jnp.where(token_of(spot, offset, half) == token, 1.0, 0.0).astype(BF)


def head_offset():
    return lax.axis_index("y_hi") * 4 + lax.axis_index("x")


def half_of(ref, half, index):
    return jnp.concatenate([ref[PLACE[block], index] for block in range(half * 16, half * 16 + 16)], axis=0)


def put_half(ref, half, index, value):
    for block in range(16):
        ref[PLACE[half * 16 + block], index] = value[block * ROWS : block * ROWS + ROWS]


def pack_kernel(key_ref, value_ref, query_ref, grad_ref, out_ref, held, arrived):
    copies = [
        pltpu.make_async_copy(source, held.at[index], arrived.at[index])
        for index, source in enumerate((key_ref, value_ref, query_ref, grad_ref))
    ]
    for copy in copies:
        copy.start()
    for index, copy in enumerate(copies):
        copy.wait()
        for head in range(PLANE):
            out_ref[PLACE[head], index] = held[index, :, head * HEAD_DIM : (head + 1) * HEAD_DIM]


def unpack_kernel(in_ref, att_ref, query_ref, key_ref, value_ref, held, sent):
    copies = []
    for index, target in enumerate((att_ref, query_ref, key_ref, value_ref)):
        for head in range(PLANE):
            held[index, :, head * HEAD_DIM : (head + 1) * HEAD_DIM] = in_ref[PLACE[head], index]
        copies.append(pltpu.make_async_copy(held.at[index], target, sent.at[index]))
        copies[-1].start()
    for copy in copies:
        copy.wait()


def select_kernel(got_ref, out_ref):
    offset = head_offset()
    for half in range(2):
        pair = jnp.concatenate([half_of(got_ref, half, 0), half_of(got_ref, half, 1)], axis=1)
        picked = nn(ordering(offset, half, LOW if half == 0 else 0, 128), pair).astype(BF)
        out_ref[0, half * 128 : half * 128 + 128] = picked[:, :HEAD_DIM]
        out_ref[1, half * 128 : half * 128 + 128] = picked[:, HEAD_DIM:]


def segment_start(step):
    segment = step // 2
    start = jnp.where(segment == 2, 256, segment * SEG)
    return pl.multiple_of(start, 256), pl.multiple_of(start + (step % 2) * 256, 256)


def merge(peak, total, acc, peak_new, total_new, acc_new):
    best = jnp.maximum(peak, peak_new)
    left = jnp.exp2((peak - best) * RATE)
    right = jnp.exp2((peak_new - best) * RATE)
    return best, left * total + right * total_new, left * acc + right * acc_new


def first_kernel(got_ref, x_ref, mid_ref, vt_ref, state_ref, acc_ref):
    offset = head_offset()
    for half in range(2):
        four = jnp.concatenate([half_of(got_ref, half, index) for index in range(4)], axis=1)
        ordered = nn(ordering(offset, half, 0, SEG), four).astype(BF)
        for index in range(4):
            x_ref[index, half * SEG : half * SEG + SEG] = ordered[
                :, index * HEAD_DIM : (index + 1) * HEAD_DIM
            ]
        vt_ref[:, half * SEG : half * SEG + SEG] = flip(ordered[:, HEAD_DIM : 2 * HEAD_DIM])
    for index in range(4):
        mid_ref[index] = x_ref[index, LOW : LOW + MID]

    def body(step, carry):
        start, first = segment_start(step)
        scores = nt(x_ref[0, pl.ds(start, SEG)], x_ref[2, pl.ds(first, 256)])
        peak = jnp.max(scores, axis=0, keepdims=True)
        weights = jnp.exp2((scores - peak) * RATE)
        cut = pl.ds(first, 256)
        state_ref[0:1, cut] = peak
        state_ref[1:2, cut] = jnp.sum(weights, axis=0, keepdims=True)
        acc_ref[:, cut] = nn(vt_ref[:, pl.ds(start, SEG)], weights.astype(BF))
        return carry

    lax.fori_loop(0, 4, body, 0, unroll=4)


def second_kernel(x_ref, vt_ref, state_in, acc_in, stat_ref, comb_ref, mid_stat_ref, mid_acc_ref, flipped_ref, state, acc):
    state[...] = state_in[...]
    acc[...] = acc_in[...]

    def body(step, carry):
        start, first = segment_start(step)
        scores = nt(x_ref[0, pl.ds(start, SEG)], x_ref[2, pl.ds(first, 256)])
        top = jnp.max(scores, axis=0, keepdims=True)
        weights = jnp.exp2((scores - top) * RATE)
        cut = pl.ds(first, 256)
        state[0:1, cut], state[1:2, cut], acc[:, cut] = merge(
            state[0:1, cut],
            state[1:2, cut],
            acc[:, cut],
            top,
            jnp.sum(weights, axis=0, keepdims=True),
            nn(vt_ref[:, pl.ds(start, SEG)], weights.astype(BF)),
        )
        return carry

    lax.fori_loop(4, 6, body, 0, unroll=2)
    combined = acc[...] / state[1:2]
    comb_ref[...] = combined.astype(BF)
    stat_ref[0:1] = state[0:1] * RATE + jnp.log2(state[1:2])
    flipped = flip(x_ref[3])
    flipped_ref[...] = flipped[:, LOW : LOW + MID]
    stat_ref[1:2] = jnp.sum(flipped.astype(F32) * combined, axis=0, keepdims=True)
    middle = slice(LOW, LOW + MID)
    near = (state[0:1, middle], state[1:2, middle], acc[:, middle])
    near = merge(*near, *forward_of(x_ref[0, middle], vt_ref[:, middle], x_ref[2, middle]))
    inner = slice(LOW + 64, LOW + 192)
    peak, total, summed = forward_of(x_ref[0, inner], flip(x_ref[1, inner]), x_ref[2, inner])
    near = merge(*near, widen(peak, NEG), widen(total, 0.0), widen(summed, 0.0))
    mid_stat_ref[0:1], mid_stat_ref[1:2], mid_acc_ref[...] = near


def widen(part, filler):
    return pltpu.roll(jnp.concatenate([part, jnp.full_like(part, filler)], axis=1), 64, 1)


def narrow(whole):
    return pltpu.roll(whole, MID - 64, 1)[:, :128]


def forward_of(keys, values_flipped, queries):
    scores = nt(keys, queries)
    peak = jnp.max(scores, axis=0, keepdims=True)
    weights = jnp.exp2((scores - peak) * RATE)
    return (
        peak,
        jnp.sum(weights, axis=0, keepdims=True),
        nn(values_flipped, weights.astype(BF)),
    )


def backward_of(keys, values, queries, grads, log_total, dot):
    probs = jnp.exp2(nt(keys, queries) * RATE - log_total)
    score_grad = (probs * (nt(values, grads) - dot)).astype(BF)
    return (
        nn(flip(keys), score_grad),
        nn(score_grad, queries),
        nn(probs.astype(BF), grads),
    )


def join(whole, part):
    return jnp.concatenate([whole[:64], whole[64:192] + part, whole[192:]], axis=0)


def forward_kernel(mid_ref, flipped_ref, stat_ref, acc_ref, one_ref, out_stat_ref, out_acc_ref):
    state = (stat_ref[0:1], stat_ref[1:2], acc_ref[...])
    state = merge(*state, *forward_of(one_ref[0], flip(one_ref[1]), mid_ref[2]))
    peak, total, summed = forward_of(one_ref[0, 64:192], flip(one_ref[1, 64:192]), mid_ref[2, 64:192])
    peak, total, acc = merge(*state, widen(peak, NEG), widen(total, 0.0), widen(summed, 0.0))
    out_stat_ref[0:1], out_stat_ref[1:2], out_acc_ref[...] = peak, total, acc
    out_stat_ref[2:3] = jnp.sum(flipped_ref[...].astype(F32) * acc, axis=0, keepdims=True)


def far_kernel(mid_ref, stat_ref, acc_ref, one_ref, two_ref, three_ref,
               out_stat_ref, comb_ref, slope_ref, far_slope_ref, send_one_ref, send_two_ref, send_three_ref):
    inner = slice(64, 192)
    keys, values, queries, grads = one_ref[0], one_ref[1], mid_ref[2], mid_ref[3]
    keys3 = jnp.concatenate([keys[inner], two_ref[0], three_ref[0]], axis=0)
    values3 = jnp.concatenate([values[inner], two_ref[1], three_ref[1]], axis=0)
    scores3, grads3 = nt(keys3, queries[inner]), nt(values3, grads[inner])
    scores2, grads2 = nt(keys, queries), nt(values, grads)
    new = scores3[128:]
    peak3 = jnp.max(new, axis=0, keepdims=True)
    weights3 = jnp.exp2((new - peak3) * RATE)
    total3 = jnp.sum(weights3, axis=0, keepdims=True)
    dot3 = jnp.sum(weights3 * grads3[128:], axis=0, keepdims=True)
    summed3 = nn(flip(values3[128:]), weights3.astype(BF))
    peak3 = widen(peak3, NEG)
    best = jnp.maximum(stat_ref[0:1], peak3)
    left = jnp.exp2((stat_ref[0:1] - best) * RATE)
    right = jnp.exp2((peak3 - best) * RATE)
    total = left * stat_ref[1:2] + right * widen(total3, 0.0)
    dot = (left * stat_ref[2:3] + right * widen(dot3, 0.0)) / total
    log_total = best * RATE + jnp.log2(total)
    out_stat_ref[0:1] = log_total
    out_stat_ref[1:2] = dot
    probs3 = jnp.exp2(scores3 * RATE - narrow(log_total))
    slopes3 = (probs3 * (grads3 - narrow(dot))).astype(BF)
    probs2 = jnp.exp2(scores2 * RATE - log_total)
    slopes2 = (probs2 * (grads2 - dot)).astype(BF)
    dk3, dv3 = nn(slopes3, queries[inner]), nn(probs3.astype(BF), grads[inner])
    dk2, dv2 = nn(slopes2, queries), nn(probs2.astype(BF), grads)
    for index, (near, far, scale) in enumerate(((dk2, dk3, SCALE), (dv2, dv3, 1.0))):
        send_one_ref[index] = (join(near, far[:128]) * scale).astype(BF)
        send_two_ref[index] = (far[128:256] * scale).astype(BF)
        send_three_ref[index] = (far[256:] * scale).astype(BF)
    slope_ref[...] = slopes2
    far_slope_ref[...] = slopes3
    comb_ref[...] = ((left * acc_ref[...] + right * widen(summed3, 0.0)) / total).astype(BF)


def back_kernel(x_ref, stat_ref, comb_ref, mid_stat_ref, mid_comb_ref, one_ref, two_ref, three_ref, slope_ref, far_slope_ref,
                out_ref, mid_grad_ref, place_ref, kt, stat, dq, dk, dv):
    offset = head_offset()
    kt[...] = flip(x_ref[0])
    stat[...] = stat_ref[...]
    stat[:, LOW : LOW + MID] = mid_stat_ref[...]
    dq[...] = jnp.zeros_like(dq)
    dk[...] = jnp.zeros_like(dk)
    dv[...] = jnp.zeros_like(dv)

    def body(step, carry):
        start, first = segment_start(step)
        keys, values = x_ref[0, pl.ds(start, SEG)], x_ref[1, pl.ds(start, SEG)]
        queries, grads = x_ref[2, pl.ds(first, 256)], x_ref[3, pl.ds(first, 256)]
        cut = pl.ds(first, 256)
        probs = jnp.exp2(nt(keys, queries) * RATE - stat[0:1, cut])
        score_grad = (probs * (nt(values, grads) - stat[1:2, cut])).astype(BF)
        dq[:, cut] += nn(kt[:, pl.ds(start, SEG)], score_grad)
        dk[pl.ds(start, SEG)] += nn(score_grad, queries)
        dv[pl.ds(start, SEG)] += nn(probs.astype(BF), grads)
        return carry

    lax.fori_loop(0, 6, body, 0, unroll=6)
    for first, last in ((LOW, LOW + MID), (LOW + 64, LOW + 192)):
        cut = slice(first, last)
        log_total, dot = stat[0:1, LOW : LOW + MID], stat[1:2, LOW : LOW + MID]
        if last - first < MID:
            log_total, dot = narrow(log_total), narrow(dot)
        part, key_part, value_part = backward_of(
            x_ref[0, cut], x_ref[1, cut], x_ref[2, cut], x_ref[3, cut], log_total, dot
        )
        dq[:, LOW : LOW + MID] += part if last - first == MID else widen(part, 0.0)
        dk[cut] += key_part
        dv[cut] += value_part
    mid_grad_ref[0] = dk[LOW : LOW + MID] * SCALE
    mid_grad_ref[1] = dv[LOW : LOW + MID]
    keys3 = jnp.concatenate([one_ref[0, 64:192], two_ref[0], three_ref[0]], axis=0)
    dq[:, LOW : LOW + MID] += nn(flip(one_ref[0]), slope_ref[...]) + widen(
        nn(flip(keys3), far_slope_ref[...]), 0.0
    )
    place_ref[0] = unordering(offset, 0, LOW, 128)
    place_ref[1] = unordering(offset, 1, 0, 128)
    query = (dq[...] * SCALE).astype(BF)
    comb = jnp.concatenate(
        [comb_ref[:, :LOW], mid_comb_ref[...], comb_ref[:, LOW + MID :]], axis=1
    )
    both = jnp.concatenate([comb, query], axis=0)
    for half in range(2):
        plain = nt(unordering(offset, half, 0, SEG), both[:, half * SEG : half * SEG + SEG]).astype(BF)
        put_half(out_ref, half, 0, plain[:, :HEAD_DIM])
        put_half(out_ref, half, 1, plain[:, HEAD_DIM:])
        outer = slice(0, LOW) if half == 0 else slice(LOW + MID, TOKENS)
        pair = jnp.concatenate([dk[outer] * SCALE, dv[outer]], axis=1).astype(BF)
        plain = nn(unordering(offset, half, 0 if half == 0 else 128, LOW), pair).astype(BF)
        put_half(out_ref, half, 2, plain[:, :HEAD_DIM])
        put_half(out_ref, half, 3, plain[:, HEAD_DIM:])


def finish_kernel(in_ref, mid_grad_ref, place_ref, one_ref, two_ref, three_ref, out_ref):
    grads = []
    for index in range(2):
        near = mid_grad_ref[index] + one_ref[index].astype(F32)
        far = two_ref[index].astype(F32) + three_ref[index].astype(F32)
        grads.append(join(near, far).astype(BF))
    pair = jnp.concatenate(grads, axis=1)
    for half in range(2):
        cut = slice(half * 128, half * 128 + 128)
        plain = nn(place_ref[half], pair[cut]).astype(BF)
        for index in range(2):
            part = plain[:, index * HEAD_DIM : (index + 1) * HEAD_DIM]
            put_half(out_ref, half, index, half_of(in_ref, half, index) + part)


def shape(dims, kind):
    return jax.ShapeDtypeStruct(dims, kind)


PARAMS = pltpu.CompilerParams(vmem_limit_bytes=32 * 1024 * 1024)


def whole(array):
    return pl.BlockSpec(array.shape, lambda: (0,) * len(array.shape))


def call(kernel, outs, args, scratch=(), flops=0):
    return pl.pallas_call(
        kernel,
        out_shape=outs,
        scratch_shapes=list(scratch),
        compiler_params=PARAMS,
        cost_estimate=pl.CostEstimate(flops=flops, bytes_accessed=2 << 20, transcendentals=0),
    )(*args)


def pack(arrays):
    return pl.pallas_call(
        pack_kernel,
        in_specs=[pl.BlockSpec(memory_space=pl.ANY)] * 4,
        out_shape=shape((PLANE, 4, ROWS, HEAD_DIM), BF),
        scratch_shapes=[
            pltpu.VMEM((4, ROWS, PLANE * HEAD_DIM), BF),
            pltpu.SemaphoreType.DMA((4,)),
        ],
        compiler_params=PARAMS,
    )(*[pltpu.with_memory_space_constraint(array, pltpu.HBM) for array in arrays])


def unpack(packed):
    return pl.pallas_call(
        unpack_kernel,
        out_specs=[pl.BlockSpec(memory_space=pl.ANY)] * 4,
        out_shape=[shape((ROWS, PLANE * HEAD_DIM), BF)] * 4,
        scratch_shapes=[
            pltpu.VMEM((4, ROWS, PLANE * HEAD_DIM), BF),
            pltpu.SemaphoreType.DMA((4,)),
        ],
        compiler_params=PARAMS,
    )(packed)


def plane_exchange(packed):
    return lax.all_to_all(packed, ("x", "y_lo", "y_hi", "core"), split_axis=0, concat_axis=0, tiled=True)


def z_exchange(block, apart):
    count = lax.axis_size("zed")
    return lax.ppermute(block, "zed", [(at, at ^ apart) for at in range(count)])


def per_device(query_rows, key_rows, value_rows, grad_rows):
    got = plane_exchange(pack([key_rows, value_rows, query_rows, grad_rows]))
    half_block = pl.BlockSpec((PLANE, 2, ROWS, HEAD_DIM), lambda i: (0, 0, 0, 0))
    near = pl.pallas_call(
        select_kernel,
        grid=(1,),
        in_specs=[half_block],
        out_specs=pl.BlockSpec((2, MID, HEAD_DIM), lambda i: (0, 0, 0)),
        out_shape=shape((2, MID, HEAD_DIM), BF),
        compiler_params=PARAMS,
    )(got)
    inner = near[:, 64:192]
    one = z_exchange(near, 1)
    two = z_exchange(inner, 2)
    three = z_exchange(inner, 3)
    ordered, mid, vt, state, acc = call(
        first_kernel,
        [
            shape((4, TOKENS, HEAD_DIM), BF),
            shape((4, MID, HEAD_DIM), BF),
            shape((HEAD_DIM, TOKENS), BF),
            shape((2, TOKENS), F32),
            shape((HEAD_DIM, TOKENS), F32),
        ],
        [got],
        flops=2 * 4 * SEG * SEG * HEAD_DIM,
    )
    stat, comb, mid_stat, mid_acc, flipped = call(
        second_kernel,
        [
            shape((2, TOKENS), F32),
            shape((HEAD_DIM, TOKENS), BF),
            shape((2, MID), F32),
            shape((HEAD_DIM, MID), F32),
            shape((HEAD_DIM, MID), BF),
        ],
        [ordered, vt, state, acc],
        [pltpu.VMEM((2, TOKENS), F32), pltpu.VMEM((HEAD_DIM, TOKENS), F32)],
        flops=4 * SEG * SEG * HEAD_DIM,
    )
    mid_stat, mid_acc = call(
        forward_kernel,
        [shape((3, MID), F32), shape((HEAD_DIM, MID), F32)],
        [mid, flipped, mid_stat, mid_acc, one],
        flops=8 * 4 * SEG * SEG * HEAD_DIM,
    )
    mid_out_stat, mid_comb, slope, far_slope, send_one, send_two, send_three = call(
        far_kernel,
        [
            shape((2, MID), F32),
            shape((HEAD_DIM, MID), BF),
            shape((MID, MID), BF),
            shape((384, 128), BF),
            shape((2, MID, HEAD_DIM), BF),
            shape((2, 128, HEAD_DIM), BF),
            shape((2, 128, HEAD_DIM), BF),
        ],
        [mid, mid_stat, mid_acc, one, two, three],
        flops=2 * 4 * SEG * SEG * HEAD_DIM,
    )
    back_one = z_exchange(send_one, 1)
    back_two = z_exchange(send_two, 2)
    back_three = z_exchange(send_three, 3)
    packed, mid_grad, place = call(
        back_kernel,
        [
            shape((PLANE, 4, ROWS, HEAD_DIM), BF),
            shape((2, MID, HEAD_DIM), F32),
            shape((2, SEG, 128), BF),
        ],
        [ordered, stat, comb, mid_out_stat, mid_comb, one, two, three, slope, far_slope],
        [
            pltpu.VMEM((HEAD_DIM, TOKENS), BF),
            pltpu.VMEM((2, TOKENS), F32),
            pltpu.VMEM((HEAD_DIM, TOKENS), F32),
            pltpu.VMEM((TOKENS, HEAD_DIM), F32),
            pltpu.VMEM((TOKENS, HEAD_DIM), F32),
        ],
        flops=3 * 10 * SEG * SEG * HEAD_DIM,
    )
    upper_half = pl.BlockSpec((PLANE, 2, ROWS, HEAD_DIM), lambda i: (0, 1, 0, 0))
    mid_block = pl.BlockSpec((2, MID, HEAD_DIM), lambda i: (0, 0, 0))
    place_block = pl.BlockSpec((2, SEG, 128), lambda i: (0, 0, 0))
    inner_block = pl.BlockSpec((2, 128, HEAD_DIM), lambda i: (0, 0, 0))
    packed = pl.pallas_call(
        finish_kernel,
        grid=(1,),
        in_specs=[upper_half, mid_block, place_block, mid_block, inner_block, inner_block],
        out_specs=upper_half,
        out_shape=shape((PLANE, 4, ROWS, HEAD_DIM), BF),
        input_output_aliases={0: 0},
        compiler_params=PARAMS,
    )(packed, mid_grad, place, back_one, back_two, back_three)
    return tuple(unpack(plane_exchange(packed)))


def solution(mesh):
    axes = ("zed", "y_lo", "core", "y_hi", "x")
    planes = Mesh(mesh.devices.reshape(-1, 2, 2, 2, 4), axes)
    spec = P(axes, None)
    return jax.shard_map(
        per_device, mesh=planes, in_specs=(spec,) * 4, out_specs=(spec,) * 4, check_vma=False
    )
```

```python
import functools

import jax
import jax.numpy as jnp
from jax import lax
from jax.experimental import pallas as pl
from jax.experimental.pallas import tpu as pltpu
from jax.sharding import Mesh, PartitionSpec as P

HEAD_DIM = 128
PLANE = 32
ROWS = 32
TOKENS = PLANE * ROWS
SEG = 512
MID = 256
LOW = 384
SCALE = HEAD_DIM**-0.5
RATE = SCALE * 1.4426950408889634
NEG = -1e30
BF = jnp.bfloat16
F32 = jnp.float32

ORDER = [
    y_lo * 16 + core * 8 + y_hi * 4 + x
    for x in range(4)
    for y_lo in range(2)
    for y_hi in range(2)
    for core in range(2)
]
PLACE = [ORDER.index(device) for device in range(PLANE)]


def nn(a, b):
    return jnp.dot(a, b, preferred_element_type=F32)


def nt(a, b):
    return lax.dot_general(a, b, (((1,), (1,)), ((), ())), preferred_element_type=F32)


def flip(a):
    return jnp.swapaxes(a, 0, 1)


def token_of(spot, offset, half):
    if half == 0:
        far = [2 * spot, 4 * (spot - 256), 8 * (spot - 384), 8 * (spot - 448)]
        tests = [spot < 256, spot < 384, spot < 448]
    else:
        far = [2 * (spot - 256), 4 * (spot - 128), 8 * (spot - 64), 8 * spot]
        tests = [spot >= 256, spot >= 128, spot >= 64]
    return jnp.where(
        tests[0],
        far[0] + ((offset + 1) & 1),
        jnp.where(
            tests[1],
            far[1] + ((offset + 2) & 3),
            jnp.where(tests[2], far[2] + ((offset + 4) & 7), far[3] + offset),
        ),
    )


def ordering(offset, half, first, count):
    spot = lax.broadcasted_iota(jnp.int32, (count, 1), 0) + first
    token = lax.broadcasted_iota(jnp.int32, (count, SEG), 1)
    return jnp.where(token_of(spot, offset, half) == token, 1.0, 0.0).astype(BF)


def unordering(offset, half, first, count):
    spot = lax.broadcasted_iota(jnp.int32, (1, count), 1) + first
    token = lax.broadcasted_iota(jnp.int32, (SEG, count), 0)
    return jnp.where(token_of(spot, offset, half) == token, 1.0, 0.0).astype(BF)


def head_offset():
    return lax.axis_index("y_hi") * 4 + lax.axis_index("x")


def half_of(ref, half, index):
    return jnp.concatenate([ref[PLACE[block], index] for block in range(half * 16, half * 16 + 16)], axis=0)


def put_half(ref, half, index, value):
    for block in range(16):
        ref[PLACE[half * 16 + block], index] = value[block * ROWS : block * ROWS + ROWS]


def pack_kernel(key_ref, value_ref, query_ref, grad_ref, out_ref, held, arrived):
    copies = [
        pltpu.make_async_copy(source, held.at[index], arrived.at[index])
        for index, source in enumerate((key_ref, value_ref, query_ref, grad_ref))
    ]
    for copy in copies:
        copy.start()
    for index, copy in enumerate(copies):
        copy.wait()
        for head in range(PLANE):
            out_ref[PLACE[head], index] = held[index, :, head * HEAD_DIM : (head + 1) * HEAD_DIM]


def unpack_kernel(in_ref, att_ref, query_ref, key_ref, value_ref, held, sent):
    copies = []
    for index, target in enumerate((att_ref, query_ref, key_ref, value_ref)):
        for head in range(PLANE):
            held[index, :, head * HEAD_DIM : (head + 1) * HEAD_DIM] = in_ref[PLACE[head], index]
        copies.append(pltpu.make_async_copy(held.at[index], target, sent.at[index]))
        copies[-1].start()
    for copy in copies:
        copy.wait()


def select_kernel(got_ref, out_ref):
    offset = head_offset()
    for half in range(2):
        pair = jnp.concatenate([half_of(got_ref, half, 0), half_of(got_ref, half, 1)], axis=1)
        picked = nn(ordering(offset, half, LOW if half == 0 else 0, 128), pair).astype(BF)
        out_ref[0, half * 128 : half * 128 + 128] = picked[:, :HEAD_DIM]
        out_ref[1, half * 128 : half * 128 + 128] = picked[:, HEAD_DIM:]


def segment_start(step):
    segment = step // 2
    start = jnp.where(segment == 2, 256, segment * SEG)
    return pl.multiple_of(start, 256), pl.multiple_of(start + (step % 2) * 256, 256)


def merge(peak, total, acc, peak_new, total_new, acc_new):
    best = jnp.maximum(peak, peak_new)
    left = jnp.exp2((peak - best) * RATE)
    right = jnp.exp2((peak_new - best) * RATE)
    return best, left * total + right * total_new, left * acc + right * acc_new


def first_kernel(got_ref, x_ref, mid_ref, vt_ref, state_ref, acc_ref):
    offset = head_offset()
    for half in range(2):
        four = jnp.concatenate([half_of(got_ref, half, index) for index in range(4)], axis=1)
        ordered = nn(ordering(offset, half, 0, SEG), four).astype(BF)
        for index in range(4):
            x_ref[index, half * SEG : half * SEG + SEG] = ordered[
                :, index * HEAD_DIM : (index + 1) * HEAD_DIM
            ]
        vt_ref[:, half * SEG : half * SEG + SEG] = flip(ordered[:, HEAD_DIM : 2 * HEAD_DIM])
    for index in range(4):
        mid_ref[index] = x_ref[index, LOW : LOW + MID]

    def body(step, carry):
        start, first = segment_start(step)
        scores = nt(x_ref[0, pl.ds(start, SEG)], x_ref[2, pl.ds(first, 256)])
        peak = jnp.max(scores, axis=0, keepdims=True)
        weights = jnp.exp2((scores - peak) * RATE)
        cut = pl.ds(first, 256)
        state_ref[0:1, cut] = peak
        state_ref[1:2, cut] = jnp.sum(weights, axis=0, keepdims=True)
        acc_ref[:, cut] = nn(vt_ref[:, pl.ds(start, SEG)], weights.astype(BF))
        return carry

    lax.fori_loop(0, 4, body, 0, unroll=4)


def second_kernel(x_ref, vt_ref, state_in, acc_in, stat_ref, comb_ref, mid_stat_ref, mid_acc_ref, flipped_ref, state, acc):
    state[...] = state_in[...]
    acc[...] = acc_in[...]

    def body(step, carry):
        start, first = segment_start(step)
        scores = nt(x_ref[0, pl.ds(start, SEG)], x_ref[2, pl.ds(first, 256)])
        top = jnp.max(scores, axis=0, keepdims=True)
        weights = jnp.exp2((scores - top) * RATE)
        cut = pl.ds(first, 256)
        state[0:1, cut], state[1:2, cut], acc[:, cut] = merge(
            state[0:1, cut],
            state[1:2, cut],
            acc[:, cut],
            top,
            jnp.sum(weights, axis=0, keepdims=True),
            nn(vt_ref[:, pl.ds(start, SEG)], weights.astype(BF)),
        )
        return carry

    lax.fori_loop(4, 6, body, 0, unroll=2)
    combined = acc[...] / state[1:2]
    comb_ref[...] = combined.astype(BF)
    stat_ref[0:1] = state[0:1] * RATE + jnp.log2(state[1:2])
    flipped = flip(x_ref[3])
    flipped_ref[...] = flipped[:, LOW : LOW + MID]
    stat_ref[1:2] = jnp.sum(flipped.astype(F32) * combined, axis=0, keepdims=True)
    middle = slice(LOW, LOW + MID)
    near = (state[0:1, middle], state[1:2, middle], acc[:, middle])
    near = merge(*near, *forward_of(x_ref[0, middle], vt_ref[:, middle], x_ref[2, middle]))
    inner = slice(LOW + 64, LOW + 192)
    peak, total, summed = forward_of(x_ref[0, inner], flip(x_ref[1, inner]), x_ref[2, inner])
    near = merge(*near, widen(peak, NEG), widen(total, 0.0), widen(summed, 0.0))
    mid_stat_ref[0:1], mid_stat_ref[1:2], mid_acc_ref[...] = near


def widen(part, filler):
    return pltpu.roll(jnp.concatenate([part, jnp.full_like(part, filler)], axis=1), 64, 1)


def narrow(whole):
    return pltpu.roll(whole, MID - 64, 1)[:, :128]


def forward_of(keys, values_flipped, queries):
    scores = nt(keys, queries)
    peak = jnp.max(scores, axis=0, keepdims=True)
    weights = jnp.exp2((scores - peak) * RATE)
    return (
        peak,
        jnp.sum(weights, axis=0, keepdims=True),
        nn(values_flipped, weights.astype(BF)),
    )


def backward_of(keys, values, queries, grads, log_total, dot):
    probs = jnp.exp2(nt(keys, queries) * RATE - log_total)
    score_grad = (probs * (nt(values, grads) - dot)).astype(BF)
    return (
        nn(flip(keys), score_grad),
        nn(score_grad, queries),
        nn(probs.astype(BF), grads),
    )


def join(whole, part):
    return jnp.concatenate([whole[:64], whole[64:192] + part, whole[192:]], axis=0)


def forward_kernel(mid_ref, flipped_ref, stat_ref, acc_ref, one_ref, out_stat_ref, out_acc_ref):
    state = (stat_ref[0:1], stat_ref[1:2], acc_ref[...])
    state = merge(*state, *forward_of(one_ref[0], flip(one_ref[1]), mid_ref[2]))
    peak, total, summed = forward_of(one_ref[0, 64:192], flip(one_ref[1, 64:192]), mid_ref[2, 64:192])
    peak, total, acc = merge(*state, widen(peak, NEG), widen(total, 0.0), widen(summed, 0.0))
    out_stat_ref[0:1], out_stat_ref[1:2], out_acc_ref[...] = peak, total, acc
    out_stat_ref[2:3] = jnp.sum(flipped_ref[...].astype(F32) * acc, axis=0, keepdims=True)


def far_kernel(mid_ref, stat_ref, acc_ref, one_ref, three_ref, two_ref,
               out_stat_ref, comb_ref, slope_ref, far_slope_ref, send_one_ref, send_two_ref, send_three_ref):
    inner = slice(64, 192)
    keys, values, queries, grads = one_ref[0], one_ref[1], mid_ref[2], mid_ref[3]
    keys3 = jnp.concatenate([keys[inner], two_ref[0], three_ref[0]], axis=0)
    values3 = jnp.concatenate([values[inner], two_ref[1], three_ref[1]], axis=0)
    scores3, grads3 = nt(keys3, queries[inner]), nt(values3, grads[inner])
    scores2, grads2 = nt(keys, queries), nt(values, grads)
    new = scores3[128:]
    peak3 = jnp.max(new, axis=0, keepdims=True)
    weights3 = jnp.exp2((new - peak3) * RATE)
    total3 = jnp.sum(weights3, axis=0, keepdims=True)
    dot3 = jnp.sum(weights3 * grads3[128:], axis=0, keepdims=True)
    summed3 = nn(flip(values3[128:]), weights3.astype(BF))
    peak3 = widen(peak3, NEG)
    best = jnp.maximum(stat_ref[0:1], peak3)
    left = jnp.exp2((stat_ref[0:1] - best) * RATE)
    right = jnp.exp2((peak3 - best) * RATE)
    total = left * stat_ref[1:2] + right * widen(total3, 0.0)
    dot = (left * stat_ref[2:3] + right * widen(dot3, 0.0)) / total
    log_total = best * RATE + jnp.log2(total)
    out_stat_ref[0:1] = log_total
    out_stat_ref[1:2] = dot
    probs3 = jnp.exp2(scores3 * RATE - narrow(log_total))
    slopes3 = (probs3 * (grads3 - narrow(dot))).astype(BF)
    probs2 = jnp.exp2(scores2 * RATE - log_total)
    slopes2 = (probs2 * (grads2 - dot)).astype(BF)
    dk3, dv3 = nn(slopes3, queries[inner]), nn(probs3.astype(BF), grads[inner])
    dk2, dv2 = nn(slopes2, queries), nn(probs2.astype(BF), grads)
    for index, (near, far, scale) in enumerate(((dk2, dk3, SCALE), (dv2, dv3, 1.0))):
        send_one_ref[index] = (join(near, far[:128]) * scale).astype(BF)
        send_two_ref[index] = (far[128:256] * scale).astype(BF)
        send_three_ref[index] = (far[256:] * scale).astype(BF)
    slope_ref[...] = slopes2
    far_slope_ref[...] = slopes3
    comb_ref[...] = ((left * acc_ref[...] + right * widen(summed3, 0.0)) / total).astype(BF)


def back_kernel(x_ref, stat_ref, comb_ref, mid_stat_ref, mid_comb_ref, one_ref, three_ref, two_ref, slope_ref, far_slope_ref,
                out_ref, mid_grad_ref, place_ref, kt, stat, dq, dk, dv):
    offset = head_offset()
    kt[...] = flip(x_ref[0])
    stat[...] = stat_ref[...]
    stat[:, LOW : LOW + MID] = mid_stat_ref[...]
    dq[...] = jnp.zeros_like(dq)
    dk[...] = jnp.zeros_like(dk)
    dv[...] = jnp.zeros_like(dv)

    def body(step, carry):
        start, first = segment_start(step)
        keys, values = x_ref[0, pl.ds(start, SEG)], x_ref[1, pl.ds(start, SEG)]
        queries, grads = x_ref[2, pl.ds(first, 256)], x_ref[3, pl.ds(first, 256)]
        cut = pl.ds(first, 256)
        probs = jnp.exp2(nt(keys, queries) * RATE - stat[0:1, cut])
        score_grad = (probs * (nt(values, grads) - stat[1:2, cut])).astype(BF)
        dq[:, cut] += nn(kt[:, pl.ds(start, SEG)], score_grad)
        dk[pl.ds(start, SEG)] += nn(score_grad, queries)
        dv[pl.ds(start, SEG)] += nn(probs.astype(BF), grads)
        return carry

    lax.fori_loop(0, 6, body, 0, unroll=6)
    for first, last in ((LOW, LOW + MID), (LOW + 64, LOW + 192)):
        cut = slice(first, last)
        log_total, dot = stat[0:1, LOW : LOW + MID], stat[1:2, LOW : LOW + MID]
        if last - first < MID:
            log_total, dot = narrow(log_total), narrow(dot)
        part, key_part, value_part = backward_of(
            x_ref[0, cut], x_ref[1, cut], x_ref[2, cut], x_ref[3, cut], log_total, dot
        )
        dq[:, LOW : LOW + MID] += part if last - first == MID else widen(part, 0.0)
        dk[cut] += key_part
        dv[cut] += value_part
    mid_grad_ref[0] = dk[LOW : LOW + MID] * SCALE
    mid_grad_ref[1] = dv[LOW : LOW + MID]
    keys3 = jnp.concatenate([one_ref[0, 64:192], two_ref[0], three_ref[0]], axis=0)
    dq[:, LOW : LOW + MID] += nn(flip(one_ref[0]), slope_ref[...]) + widen(
        nn(flip(keys3), far_slope_ref[...]), 0.0
    )
    place_ref[0] = unordering(offset, 0, LOW, 128)
    place_ref[1] = unordering(offset, 1, 0, 128)
    query = (dq[...] * SCALE).astype(BF)
    comb = jnp.concatenate(
        [comb_ref[:, :LOW], mid_comb_ref[...], comb_ref[:, LOW + MID :]], axis=1
    )
    both = jnp.concatenate([comb, query], axis=0)
    for half in range(2):
        plain = nt(unordering(offset, half, 0, SEG), both[:, half * SEG : half * SEG + SEG]).astype(BF)
        put_half(out_ref, half, 0, plain[:, :HEAD_DIM])
        put_half(out_ref, half, 1, plain[:, HEAD_DIM:])
        outer = slice(0, LOW) if half == 0 else slice(LOW + MID, TOKENS)
        pair = jnp.concatenate([dk[outer] * SCALE, dv[outer]], axis=1).astype(BF)
        plain = nn(unordering(offset, half, 0 if half == 0 else 128, LOW), pair).astype(BF)
        put_half(out_ref, half, 2, plain[:, :HEAD_DIM])
        put_half(out_ref, half, 3, plain[:, HEAD_DIM:])


def finish_kernel(in_ref, mid_grad_ref, place_ref, one_ref, two_ref, three_ref, out_ref):
    grads = []
    for index in range(2):
        near = mid_grad_ref[index] + one_ref[index].astype(F32)
        far = two_ref[index].astype(F32) + three_ref[index].astype(F32)
        grads.append(join(near, far).astype(BF))
    pair = jnp.concatenate(grads, axis=1)
    out_ref[:, 0:2] = in_ref[:, 0:2]
    for half in range(2):
        cut = slice(half * 128, half * 128 + 128)
        plain = nn(place_ref[half], pair[cut]).astype(BF)
        for index in range(2):
            part = plain[:, index * HEAD_DIM : (index + 1) * HEAD_DIM]
            put_half(out_ref, half, index + 2, half_of(in_ref, half, index + 2) + part)


def shape(dims, kind):
    return jax.ShapeDtypeStruct(dims, kind)


PARAMS = pltpu.CompilerParams(vmem_limit_bytes=32 * 1024 * 1024)


def whole(array):
    return pl.BlockSpec(array.shape, lambda: (0,) * len(array.shape))


def call(kernel, outs, args, scratch=(), flops=0):
    return pl.pallas_call(
        kernel,
        out_shape=outs,
        scratch_shapes=list(scratch),
        compiler_params=PARAMS,
        cost_estimate=pl.CostEstimate(flops=flops, bytes_accessed=2 << 20, transcendentals=0),
    )(*args)


def pack(arrays):
    return pl.pallas_call(
        pack_kernel,
        in_specs=[pl.BlockSpec(memory_space=pl.ANY)] * 4,
        out_shape=shape((PLANE, 4, ROWS, HEAD_DIM), BF),
        scratch_shapes=[
            pltpu.VMEM((4, ROWS, PLANE * HEAD_DIM), BF),
            pltpu.SemaphoreType.DMA((4,)),
        ],
        compiler_params=PARAMS,
    )(*[pltpu.with_memory_space_constraint(array, pltpu.HBM) for array in arrays])


def unpack(packed):
    return pl.pallas_call(
        unpack_kernel,
        out_specs=[pl.BlockSpec(memory_space=pl.ANY)] * 4,
        out_shape=[shape((ROWS, PLANE * HEAD_DIM), BF)] * 4,
        scratch_shapes=[
            pltpu.VMEM((4, ROWS, PLANE * HEAD_DIM), BF),
            pltpu.SemaphoreType.DMA((4,)),
        ],
        compiler_params=PARAMS,
    )(packed)


def plane_exchange(packed):
    return lax.all_to_all(packed, ("x", "y_lo", "y_hi", "core"), split_axis=0, concat_axis=0, tiled=True)


def z_exchange(block, apart):
    count = lax.axis_size("zed")
    return lax.ppermute(block, "zed", [(at, at ^ apart) for at in range(count)])


def per_device(query_rows, key_rows, value_rows, grad_rows):
    got = plane_exchange(pack([key_rows, value_rows, query_rows, grad_rows]))
    near = call(select_kernel, shape((2, MID, HEAD_DIM), BF), [got])
    inner = near[:, 64:192]
    one = z_exchange(near, 1)
    three = z_exchange(inner, 3)
    two = z_exchange(inner, 2)
    ordered, mid, vt, state, acc = call(
        first_kernel,
        [
            shape((4, TOKENS, HEAD_DIM), BF),
            shape((4, MID, HEAD_DIM), BF),
            shape((HEAD_DIM, TOKENS), BF),
            shape((2, TOKENS), F32),
            shape((HEAD_DIM, TOKENS), F32),
        ],
        [got],
        flops=2 * 4 * SEG * SEG * HEAD_DIM,
    )
    stat, comb, mid_stat, mid_acc, flipped = call(
        second_kernel,
        [
            shape((2, TOKENS), F32),
            shape((HEAD_DIM, TOKENS), BF),
            shape((2, MID), F32),
            shape((HEAD_DIM, MID), F32),
            shape((HEAD_DIM, MID), BF),
        ],
        [ordered, vt, state, acc],
        [pltpu.VMEM((2, TOKENS), F32), pltpu.VMEM((HEAD_DIM, TOKENS), F32)],
        flops=4 * SEG * SEG * HEAD_DIM,
    )
    mid_stat, mid_acc = call(
        forward_kernel,
        [shape((3, MID), F32), shape((HEAD_DIM, MID), F32)],
        [mid, flipped, mid_stat, mid_acc, one],
        flops=8 * 4 * SEG * SEG * HEAD_DIM,
    )
    mid_out_stat, mid_comb, slope, far_slope, send_one, send_two, send_three = call(
        far_kernel,
        [
            shape((2, MID), F32),
            shape((HEAD_DIM, MID), BF),
            shape((MID, MID), BF),
            shape((384, 128), BF),
            shape((2, MID, HEAD_DIM), BF),
            shape((2, 128, HEAD_DIM), BF),
            shape((2, 128, HEAD_DIM), BF),
        ],
        [mid, mid_stat, mid_acc, one, three, two],
        flops=2 * 4 * SEG * SEG * HEAD_DIM,
    )
    back_one = z_exchange(send_one, 1)
    back_two = z_exchange(send_two, 2)
    back_three = z_exchange(send_three, 3)
    packed, mid_grad, place = call(
        back_kernel,
        [
            shape((PLANE, 4, ROWS, HEAD_DIM), BF),
            shape((2, MID, HEAD_DIM), F32),
            shape((2, SEG, 128), BF),
        ],
        [ordered, stat, comb, mid_out_stat, mid_comb, one, three, two, slope, far_slope],
        [
            pltpu.VMEM((HEAD_DIM, TOKENS), BF),
            pltpu.VMEM((2, TOKENS), F32),
            pltpu.VMEM((HEAD_DIM, TOKENS), F32),
            pltpu.VMEM((TOKENS, HEAD_DIM), F32),
            pltpu.VMEM((TOKENS, HEAD_DIM), F32),
        ],
        flops=3 * 10 * SEG * SEG * HEAD_DIM,
    )
    packed = call(
        finish_kernel,
        shape((PLANE, 4, ROWS, HEAD_DIM), BF),
        [packed, mid_grad, place, back_one, back_two, back_three],
    )
    return tuple(unpack(plane_exchange(packed)))


def solution(mesh):
    axes = ("zed", "y_lo", "core", "y_hi", "x")
    planes = Mesh(mesh.devices.reshape(-1, 2, 2, 2, 4), axes)
    spec = P(axes, None)
    return jax.shard_map(
        per_device, mesh=planes, in_specs=(spec,) * 4, out_specs=(spec,) * 4, check_vma=False
    )
```

```python
import functools

import jax
import jax.numpy as jnp
from jax import lax
from jax.experimental import pallas as pl
from jax.experimental.pallas import tpu as pltpu
from jax.sharding import Mesh, PartitionSpec as P

HEAD_DIM = 128
PLANE = 32
ROWS = 32
TOKENS = PLANE * ROWS
SEG = 512
MID = 256
LOW = 384
SCALE = HEAD_DIM**-0.5
RATE = SCALE * 1.4426950408889634
NEG = -1e30
BF = jnp.bfloat16
F32 = jnp.float32

ORDER = [
    y_lo * 16 + core * 8 + y_hi * 4 + x
    for x in range(4)
    for y_lo in range(2)
    for y_hi in range(2)
    for core in range(2)
]
PLACE = [ORDER.index(device) for device in range(PLANE)]


def nn(a, b):
    return jnp.dot(a, b, preferred_element_type=F32)


def nt(a, b):
    return lax.dot_general(a, b, (((1,), (1,)), ((), ())), preferred_element_type=F32)


def flip(a):
    return jnp.swapaxes(a, 0, 1)


def token_of(spot, offset, half):
    if half == 0:
        far = [2 * spot, 4 * (spot - 256), 8 * (spot - 384), 8 * (spot - 448)]
        tests = [spot < 256, spot < 384, spot < 448]
    else:
        far = [2 * (spot - 256), 4 * (spot - 128), 8 * (spot - 64), 8 * spot]
        tests = [spot >= 256, spot >= 128, spot >= 64]
    return jnp.where(
        tests[0],
        far[0] + ((offset + 1) & 1),
        jnp.where(
            tests[1],
            far[1] + ((offset + 2) & 3),
            jnp.where(tests[2], far[2] + ((offset + 4) & 7), far[3] + offset),
        ),
    )


def ordering(offset, half, first, count):
    spot = lax.broadcasted_iota(jnp.int32, (count, 1), 0) + first
    token = lax.broadcasted_iota(jnp.int32, (count, SEG), 1)
    return jnp.where(token_of(spot, offset, half) == token, 1.0, 0.0).astype(BF)


def unordering(offset, half, first, count):
    spot = lax.broadcasted_iota(jnp.int32, (1, count), 1) + first
    token = lax.broadcasted_iota(jnp.int32, (SEG, count), 0)
    return jnp.where(token_of(spot, offset, half) == token, 1.0, 0.0).astype(BF)


def head_offset():
    return lax.axis_index("y_hi") * 4 + lax.axis_index("x")


def half_of(ref, half, index):
    return jnp.concatenate([ref[PLACE[block], index] for block in range(half * 16, half * 16 + 16)], axis=0)


def put_half(ref, half, index, value):
    for block in range(16):
        ref[PLACE[half * 16 + block], index] = value[block * ROWS : block * ROWS + ROWS]


def pack_kernel(key_ref, value_ref, query_ref, grad_ref, out_ref, held, arrived):
    copies = [
        pltpu.make_async_copy(source, held.at[index], arrived.at[index])
        for index, source in enumerate((key_ref, value_ref, query_ref, grad_ref))
    ]
    for copy in copies:
        copy.start()
    for index, copy in enumerate(copies):
        copy.wait()
        for head in range(PLANE):
            out_ref[PLACE[head], index] = held[index, :, head * HEAD_DIM : (head + 1) * HEAD_DIM]


def unpack_kernel(in_ref, att_ref, query_ref, key_ref, value_ref, held, sent):
    copies = []
    for index, target in enumerate((att_ref, query_ref, key_ref, value_ref)):
        for head in range(PLANE):
            held[index, :, head * HEAD_DIM : (head + 1) * HEAD_DIM] = in_ref[PLACE[head], index]
        copies.append(pltpu.make_async_copy(held.at[index], target, sent.at[index]))
        copies[-1].start()
    for copy in copies:
        copy.wait()


def select_kernel(got_ref, out_ref):
    offset = head_offset()
    for half in range(2):
        pair = jnp.concatenate([half_of(got_ref, half, 0), half_of(got_ref, half, 1)], axis=1)
        picked = nn(ordering(offset, half, LOW if half == 0 else 0, 128), pair).astype(BF)
        out_ref[0, half * 128 : half * 128 + 128] = picked[:, :HEAD_DIM]
        out_ref[1, half * 128 : half * 128 + 128] = picked[:, HEAD_DIM:]


def segment_start(step):
    segment = step // 2
    start = jnp.where(segment == 2, 256, segment * SEG)
    return pl.multiple_of(start, 256), pl.multiple_of(start + (step % 2) * 256, 256)


def merge(peak, total, acc, peak_new, total_new, acc_new):
    best = jnp.maximum(peak, peak_new)
    left = jnp.exp2((peak - best) * RATE)
    right = jnp.exp2((peak_new - best) * RATE)
    return best, left * total + right * total_new, left * acc + right * acc_new


def first_kernel(got_ref, x_ref, mid_ref, vt_ref, state_ref, acc_ref):
    offset = head_offset()
    for half in range(2):
        four = jnp.concatenate([half_of(got_ref, half, index) for index in range(4)], axis=1)
        ordered = nn(ordering(offset, half, 0, SEG), four).astype(BF)
        for index in range(4):
            x_ref[index, half * SEG : half * SEG + SEG] = ordered[
                :, index * HEAD_DIM : (index + 1) * HEAD_DIM
            ]
        vt_ref[:, half * SEG : half * SEG + SEG] = flip(ordered[:, HEAD_DIM : 2 * HEAD_DIM])
    for index in range(4):
        mid_ref[index] = x_ref[index, LOW : LOW + MID]

    def body(step, carry):
        start, first = segment_start(step)
        scores = nt(x_ref[0, pl.ds(start, SEG)], x_ref[2, pl.ds(first, 256)])
        peak = jnp.max(scores, axis=0, keepdims=True)
        weights = jnp.exp2((scores - peak) * RATE)
        cut = pl.ds(first, 256)
        state_ref[0:1, cut] = peak
        state_ref[1:2, cut] = jnp.sum(weights, axis=0, keepdims=True)
        acc_ref[:, cut] = nn(vt_ref[:, pl.ds(start, SEG)], weights.astype(BF))
        return carry

    lax.fori_loop(0, 4, body, 0, unroll=4)


def second_kernel(x_ref, vt_ref, state_in, acc_in, stat_ref, comb_ref, mid_stat_ref, mid_acc_ref, flipped_ref, state, acc):
    state[...] = state_in[...]
    acc[...] = acc_in[...]

    def body(step, carry):
        start, first = segment_start(step)
        scores = nt(x_ref[0, pl.ds(start, SEG)], x_ref[2, pl.ds(first, 256)])
        top = jnp.max(scores, axis=0, keepdims=True)
        weights = jnp.exp2((scores - top) * RATE)
        cut = pl.ds(first, 256)
        state[0:1, cut], state[1:2, cut], acc[:, cut] = merge(
            state[0:1, cut],
            state[1:2, cut],
            acc[:, cut],
            top,
            jnp.sum(weights, axis=0, keepdims=True),
            nn(vt_ref[:, pl.ds(start, SEG)], weights.astype(BF)),
        )
        return carry

    lax.fori_loop(4, 6, body, 0, unroll=2)
    combined = acc[...] / state[1:2]
    comb_ref[...] = combined.astype(BF)
    stat_ref[0:1] = state[0:1] * RATE + jnp.log2(state[1:2])
    flipped = flip(x_ref[3])
    flipped_ref[...] = flipped[:, LOW : LOW + MID]
    stat_ref[1:2] = jnp.sum(flipped.astype(F32) * combined, axis=0, keepdims=True)
    middle = slice(LOW, LOW + MID)
    near = (state[0:1, middle], state[1:2, middle], acc[:, middle])
    near = merge(*near, *forward_of(x_ref[0, middle], vt_ref[:, middle], x_ref[2, middle]))
    inner = slice(LOW + 64, LOW + 192)
    peak, total, summed = forward_of(x_ref[0, inner], flip(x_ref[1, inner]), x_ref[2, inner])
    near = merge(*near, widen(peak, NEG), widen(total, 0.0), widen(summed, 0.0))
    mid_stat_ref[0:1], mid_stat_ref[1:2], mid_acc_ref[...] = near


def widen(part, filler):
    return pltpu.roll(jnp.concatenate([part, jnp.full_like(part, filler)], axis=1), 64, 1)


def narrow(whole):
    return pltpu.roll(whole, MID - 64, 1)[:, :128]


def forward_of(keys, values_flipped, queries):
    scores = nt(keys, queries)
    peak = jnp.max(scores, axis=0, keepdims=True)
    weights = jnp.exp2((scores - peak) * RATE)
    return (
        peak,
        jnp.sum(weights, axis=0, keepdims=True),
        nn(values_flipped, weights.astype(BF)),
    )


def backward_of(keys, values, queries, grads, log_total, dot):
    probs = jnp.exp2(nt(keys, queries) * RATE - log_total)
    score_grad = (probs * (nt(values, grads) - dot)).astype(BF)
    return (
        nn(flip(keys), score_grad),
        nn(score_grad, queries),
        nn(probs.astype(BF), grads),
    )


def join(whole, part):
    return jnp.concatenate([whole[:64], whole[64:192] + part, whole[192:]], axis=0)


def forward_kernel(mid_ref, flipped_ref, stat_ref, acc_ref, one_ref, out_stat_ref, out_acc_ref):
    state = (stat_ref[0:1], stat_ref[1:2], acc_ref[...])
    state = merge(*state, *forward_of(one_ref[0], flip(one_ref[1]), mid_ref[2]))
    peak, total, summed = forward_of(one_ref[0, 64:192], flip(one_ref[1, 64:192]), mid_ref[2, 64:192])
    peak, total, acc = merge(*state, widen(peak, NEG), widen(total, 0.0), widen(summed, 0.0))
    out_stat_ref[0:1], out_stat_ref[1:2], out_acc_ref[...] = peak, total, acc
    out_stat_ref[2:3] = jnp.sum(flipped_ref[...].astype(F32) * acc, axis=0, keepdims=True)


def far_kernel(mid_ref, stat_ref, one_ref, three_ref, two_ref,
               out_stat_ref, weight_ref, slope_ref, far_slope_ref, send_one_ref, send_two_ref, send_three_ref):
    inner = slice(64, 192)
    keys, values, queries, grads = one_ref[0], one_ref[1], mid_ref[2], mid_ref[3]
    keys3 = jnp.concatenate([keys[inner], two_ref[0], three_ref[0]], axis=0)
    values3 = jnp.concatenate([values[inner], two_ref[1], three_ref[1]], axis=0)
    scores3, grads3 = nt(keys3, queries[inner]), nt(values3, grads[inner])
    scores2, grads2 = nt(keys, queries), nt(values, grads)
    new = scores3[128:]
    peak3 = jnp.max(new, axis=0, keepdims=True)
    weights3 = jnp.exp2((new - peak3) * RATE)
    total3 = jnp.sum(weights3, axis=0, keepdims=True)
    dot3 = jnp.sum(weights3 * grads3[128:], axis=0, keepdims=True)
    weight_ref[...] = weights3.astype(BF)
    peak3 = widen(peak3, NEG)
    best = jnp.maximum(stat_ref[0:1], peak3)
    left = jnp.exp2((stat_ref[0:1] - best) * RATE)
    right = jnp.exp2((peak3 - best) * RATE)
    total = left * stat_ref[1:2] + right * widen(total3, 0.0)
    dot = (left * stat_ref[2:3] + right * widen(dot3, 0.0)) / total
    log_total = best * RATE + jnp.log2(total)
    out_stat_ref[0:1] = log_total
    out_stat_ref[1:2] = dot
    out_stat_ref[2:3] = left / total
    out_stat_ref[3:4] = right / total
    probs3 = jnp.exp2(scores3 * RATE - narrow(log_total))
    slopes3 = (probs3 * (grads3 - narrow(dot))).astype(BF)
    probs2 = jnp.exp2(scores2 * RATE - log_total)
    slopes2 = (probs2 * (grads2 - dot)).astype(BF)
    dk3, dv3 = nn(slopes3, queries[inner]), nn(probs3.astype(BF), grads[inner])
    dk2, dv2 = nn(slopes2, queries), nn(probs2.astype(BF), grads)
    for index, (near, far, scale) in enumerate(((dk2, dk3, SCALE), (dv2, dv3, 1.0))):
        send_one_ref[index] = (join(near, far[:128]) * scale).astype(BF)
        send_two_ref[index] = (far[128:256] * scale).astype(BF)
        send_three_ref[index] = (far[256:] * scale).astype(BF)
    slope_ref[...] = slopes2
    far_slope_ref[...] = slopes3


def back_kernel(x_ref, stat_ref, comb_ref, mid_stat_ref, mid_acc_ref, weight_ref, one_ref, three_ref, two_ref, slope_ref, far_slope_ref,
                out_ref, mid_grad_ref, place_ref, kt, stat, dq, dk, dv):
    offset = head_offset()
    kt[...] = flip(x_ref[0])
    stat[...] = stat_ref[...]
    stat[:, LOW : LOW + MID] = mid_stat_ref[0:2]
    dq[...] = jnp.zeros_like(dq)
    dk[...] = jnp.zeros_like(dk)
    dv[...] = jnp.zeros_like(dv)

    def body(step, carry):
        start, first = segment_start(step)
        keys, values = x_ref[0, pl.ds(start, SEG)], x_ref[1, pl.ds(start, SEG)]
        queries, grads = x_ref[2, pl.ds(first, 256)], x_ref[3, pl.ds(first, 256)]
        cut = pl.ds(first, 256)
        probs = jnp.exp2(nt(keys, queries) * RATE - stat[0:1, cut])
        score_grad = (probs * (nt(values, grads) - stat[1:2, cut])).astype(BF)
        dq[:, cut] += nn(kt[:, pl.ds(start, SEG)], score_grad)
        dk[pl.ds(start, SEG)] += nn(score_grad, queries)
        dv[pl.ds(start, SEG)] += nn(probs.astype(BF), grads)
        return carry

    lax.fori_loop(0, 6, body, 0, unroll=6)
    for first, last in ((LOW, LOW + MID), (LOW + 64, LOW + 192)):
        cut = slice(first, last)
        log_total, dot = stat[0:1, LOW : LOW + MID], stat[1:2, LOW : LOW + MID]
        if last - first < MID:
            log_total, dot = narrow(log_total), narrow(dot)
        part, key_part, value_part = backward_of(
            x_ref[0, cut], x_ref[1, cut], x_ref[2, cut], x_ref[3, cut], log_total, dot
        )
        dq[:, LOW : LOW + MID] += part if last - first == MID else widen(part, 0.0)
        dk[cut] += key_part
        dv[cut] += value_part
    mid_grad_ref[0] = dk[LOW : LOW + MID] * SCALE
    mid_grad_ref[1] = dv[LOW : LOW + MID]
    keys3 = jnp.concatenate([one_ref[0, 64:192], two_ref[0], three_ref[0]], axis=0)
    distant = jnp.concatenate([two_ref[1], three_ref[1]], axis=0)
    mid_comb = mid_stat_ref[2:3] * mid_acc_ref[...] + mid_stat_ref[3:4] * widen(
        nn(flip(distant), weight_ref[...]), 0.0
    )
    dq[:, LOW : LOW + MID] += nn(flip(one_ref[0]), slope_ref[...]) + widen(
        nn(flip(keys3), far_slope_ref[...]), 0.0
    )
    place_ref[0] = unordering(offset, 0, LOW, 128)
    place_ref[1] = unordering(offset, 1, 0, 128)
    query = (dq[...] * SCALE).astype(BF)
    comb = jnp.concatenate(
        [comb_ref[:, :LOW], mid_comb.astype(BF), comb_ref[:, LOW + MID :]], axis=1
    )
    both = jnp.concatenate([comb, query], axis=0)
    for half in range(2):
        plain = nt(unordering(offset, half, 0, SEG), both[:, half * SEG : half * SEG + SEG]).astype(BF)
        put_half(out_ref, half, 0, plain[:, :HEAD_DIM])
        put_half(out_ref, half, 1, plain[:, HEAD_DIM:])
        outer = slice(0, LOW) if half == 0 else slice(LOW + MID, TOKENS)
        pair = jnp.concatenate([dk[outer] * SCALE, dv[outer]], axis=1).astype(BF)
        plain = nn(unordering(offset, half, 0 if half == 0 else 128, LOW), pair).astype(BF)
        put_half(out_ref, half, 2, plain[:, :HEAD_DIM])
        put_half(out_ref, half, 3, plain[:, HEAD_DIM:])


def finish_kernel(in_ref, mid_grad_ref, place_ref, one_ref, two_ref, three_ref, out_ref):
    grads = []
    for index in range(2):
        near = mid_grad_ref[index] + one_ref[index].astype(F32)
        far = two_ref[index].astype(F32) + three_ref[index].astype(F32)
        grads.append(join(near, far).astype(BF))
    pair = jnp.concatenate(grads, axis=1)
    out_ref[:, 0:2] = in_ref[:, 0:2]
    for half in range(2):
        cut = slice(half * 128, half * 128 + 128)
        plain = nn(place_ref[half], pair[cut]).astype(BF)
        for index in range(2):
            part = plain[:, index * HEAD_DIM : (index + 1) * HEAD_DIM]
            put_half(out_ref, half, index + 2, half_of(in_ref, half, index + 2) + part)


def shape(dims, kind):
    return jax.ShapeDtypeStruct(dims, kind)


PARAMS = pltpu.CompilerParams(vmem_limit_bytes=32 * 1024 * 1024)


def whole(array):
    return pl.BlockSpec(array.shape, lambda: (0,) * len(array.shape))


def call(kernel, outs, args, scratch=(), flops=0):
    return pl.pallas_call(
        kernel,
        out_shape=outs,
        scratch_shapes=list(scratch),
        compiler_params=PARAMS,
        cost_estimate=pl.CostEstimate(flops=flops, bytes_accessed=2 << 20, transcendentals=0),
    )(*args)


def pack(arrays):
    return pl.pallas_call(
        pack_kernel,
        in_specs=[pl.BlockSpec(memory_space=pl.ANY)] * 4,
        out_shape=shape((PLANE, 4, ROWS, HEAD_DIM), BF),
        scratch_shapes=[
            pltpu.VMEM((4, ROWS, PLANE * HEAD_DIM), BF),
            pltpu.SemaphoreType.DMA((4,)),
        ],
        compiler_params=PARAMS,
    )(*[pltpu.with_memory_space_constraint(array, pltpu.HBM) for array in arrays])


def unpack(packed):
    return pl.pallas_call(
        unpack_kernel,
        out_specs=[pl.BlockSpec(memory_space=pl.ANY)] * 4,
        out_shape=[shape((ROWS, PLANE * HEAD_DIM), BF)] * 4,
        scratch_shapes=[
            pltpu.VMEM((4, ROWS, PLANE * HEAD_DIM), BF),
            pltpu.SemaphoreType.DMA((4,)),
        ],
        compiler_params=PARAMS,
    )(packed)


def plane_exchange(packed):
    return lax.all_to_all(packed, ("x", "y_lo", "y_hi", "core"), split_axis=0, concat_axis=0, tiled=True)


def z_exchange(block, apart):
    count = lax.axis_size("zed")
    return lax.ppermute(block, "zed", [(at, at ^ apart) for at in range(count)])


def per_device(query_rows, key_rows, value_rows, grad_rows):
    got = plane_exchange(pack([key_rows, value_rows, query_rows, grad_rows]))
    near = call(select_kernel, shape((2, MID, HEAD_DIM), BF), [got])
    inner = near[:, 64:192]
    one = z_exchange(near, 1)
    three = z_exchange(inner, 3)
    two = z_exchange(inner, 2)
    ordered, mid, vt, state, acc = call(
        first_kernel,
        [
            shape((4, TOKENS, HEAD_DIM), BF),
            shape((4, MID, HEAD_DIM), BF),
            shape((HEAD_DIM, TOKENS), BF),
            shape((2, TOKENS), F32),
            shape((HEAD_DIM, TOKENS), F32),
        ],
        [got],
        flops=2 * 4 * SEG * SEG * HEAD_DIM,
    )
    stat, comb, mid_stat, mid_acc, flipped = call(
        second_kernel,
        [
            shape((2, TOKENS), F32),
            shape((HEAD_DIM, TOKENS), BF),
            shape((2, MID), F32),
            shape((HEAD_DIM, MID), F32),
            shape((HEAD_DIM, MID), BF),
        ],
        [ordered, vt, state, acc],
        [pltpu.VMEM((2, TOKENS), F32), pltpu.VMEM((HEAD_DIM, TOKENS), F32)],
        flops=4 * SEG * SEG * HEAD_DIM,
    )
    mid_stat, mid_acc = call(
        forward_kernel,
        [shape((3, MID), F32), shape((HEAD_DIM, MID), F32)],
        [mid, flipped, mid_stat, mid_acc, one],
        flops=8 * 4 * SEG * SEG * HEAD_DIM,
    )
    mid_out_stat, weight, slope, far_slope, send_one, send_two, send_three = call(
        far_kernel,
        [
            shape((4, MID), F32),
            shape((MID, 128), BF),
            shape((MID, MID), BF),
            shape((384, 128), BF),
            shape((2, MID, HEAD_DIM), BF),
            shape((2, 128, HEAD_DIM), BF),
            shape((2, 128, HEAD_DIM), BF),
        ],
        [mid, mid_stat, one, three, two],
        flops=2 * 4 * SEG * SEG * HEAD_DIM,
    )
    back_one = z_exchange(send_one, 1)
    back_two = z_exchange(send_two, 2)
    back_three = z_exchange(send_three, 3)
    packed, mid_grad, place = call(
        back_kernel,
        [
            shape((PLANE, 4, ROWS, HEAD_DIM), BF),
            shape((2, MID, HEAD_DIM), F32),
            shape((2, SEG, 128), BF),
        ],
        [ordered, stat, comb, mid_out_stat, mid_acc, weight, one, three, two, slope, far_slope],
        [
            pltpu.VMEM((HEAD_DIM, TOKENS), BF),
            pltpu.VMEM((2, TOKENS), F32),
            pltpu.VMEM((HEAD_DIM, TOKENS), F32),
            pltpu.VMEM((TOKENS, HEAD_DIM), F32),
            pltpu.VMEM((TOKENS, HEAD_DIM), F32),
        ],
        flops=3 * 10 * SEG * SEG * HEAD_DIM,
    )
    packed = call(
        finish_kernel,
        shape((PLANE, 4, ROWS, HEAD_DIM), BF),
        [packed, mid_grad, place, back_one, back_two, back_three],
    )
    return tuple(unpack(plane_exchange(packed)))


def solution(mesh):
    axes = ("zed", "y_lo", "core", "y_hi", "x")
    planes = Mesh(mesh.devices.reshape(-1, 2, 2, 2, 4), axes)
    spec = P(axes, None)
    return jax.shard_map(
        per_device, mesh=planes, in_specs=(spec,) * 4, out_specs=(spec,) * 4, check_vma=False
    )
```

```python
import functools

import jax
import jax.numpy as jnp
from jax import lax
from jax.experimental import pallas as pl
from jax.experimental.pallas import tpu as pltpu
from jax.sharding import Mesh, PartitionSpec as P

HEAD_DIM = 128
PLANE = 32
ROWS = 32
TOKENS = PLANE * ROWS
SEG = 512
MID = 256
LOW = 384
SCALE = HEAD_DIM**-0.5
RATE = SCALE * 1.4426950408889634
NEG = -1e30
BF = jnp.bfloat16
F32 = jnp.float32

ORDER = [
    y_lo * 16 + core * 8 + y_hi * 4 + x
    for x in range(4)
    for y_lo in range(2)
    for y_hi in range(2)
    for core in range(2)
]
PLACE = [ORDER.index(device) for device in range(PLANE)]


def nn(a, b):
    return jnp.dot(a, b, preferred_element_type=F32)


def nt(a, b):
    return lax.dot_general(a, b, (((1,), (1,)), ((), ())), preferred_element_type=F32)


def flip(a):
    return jnp.swapaxes(a, 0, 1)


def token_of(spot, offset, half):
    if half == 0:
        far = [2 * spot, 4 * (spot - 256), 8 * (spot - 384), 8 * (spot - 448)]
        tests = [spot < 256, spot < 384, spot < 448]
    else:
        far = [2 * (spot - 256), 4 * (spot - 128), 8 * (spot - 64), 8 * spot]
        tests = [spot >= 256, spot >= 128, spot >= 64]
    return jnp.where(
        tests[0],
        far[0] + ((offset + 1) & 1),
        jnp.where(
            tests[1],
            far[1] + ((offset + 2) & 3),
            jnp.where(tests[2], far[2] + ((offset + 4) & 7), far[3] + offset),
        ),
    )


def ordering(offset, half, first, count):
    spot = lax.broadcasted_iota(jnp.int32, (count, 1), 0) + first
    token = lax.broadcasted_iota(jnp.int32, (count, SEG), 1)
    return jnp.where(token_of(spot, offset, half) == token, 1.0, 0.0).astype(BF)


def unordering(offset, half, first, count):
    spot = lax.broadcasted_iota(jnp.int32, (1, count), 1) + first
    token = lax.broadcasted_iota(jnp.int32, (SEG, count), 0)
    return jnp.where(token_of(spot, offset, half) == token, 1.0, 0.0).astype(BF)


def head_offset():
    return lax.axis_index("y_hi") * 4 + lax.axis_index("x")


def half_of(ref, half, index):
    return jnp.concatenate([ref[PLACE[block], index] for block in range(half * 16, half * 16 + 16)], axis=0)


def put_half(ref, half, index, value):
    for block in range(16):
        ref[PLACE[half * 16 + block], index] = value[block * ROWS : block * ROWS + ROWS]


def pack_kernel(key_ref, value_ref, query_ref, grad_ref, out_ref, held, arrived):
    copies = [
        pltpu.make_async_copy(source, held.at[index], arrived.at[index])
        for index, source in enumerate((key_ref, value_ref, query_ref, grad_ref))
    ]
    for copy in copies:
        copy.start()
    for index, copy in enumerate(copies):
        copy.wait()
        for head in range(PLANE):
            out_ref[PLACE[head], index] = held[index, :, head * HEAD_DIM : (head + 1) * HEAD_DIM]


def unpack_kernel(in_ref, att_ref, query_ref, key_ref, value_ref, held, sent):
    copies = []
    for index, target in enumerate((att_ref, query_ref, key_ref, value_ref)):
        for head in range(PLANE):
            held[index, :, head * HEAD_DIM : (head + 1) * HEAD_DIM] = in_ref[PLACE[head], index]
        copies.append(pltpu.make_async_copy(held.at[index], target, sent.at[index]))
        copies[-1].start()
    for copy in copies:
        copy.wait()


def select_kernel(got_ref, out_ref):
    offset = head_offset()
    for half in range(2):
        pair = jnp.concatenate([half_of(got_ref, half, 0), half_of(got_ref, half, 1)], axis=1)
        picked = nn(ordering(offset, half, LOW if half == 0 else 0, 128), pair).astype(BF)
        out_ref[0, half * 128 : half * 128 + 128] = picked[:, :HEAD_DIM]
        out_ref[1, half * 128 : half * 128 + 128] = picked[:, HEAD_DIM:]


def segment_start(step):
    segment = step // 2
    start = jnp.where(segment == 2, 256, segment * SEG)
    return pl.multiple_of(start, 256), pl.multiple_of(start + (step % 2) * 256, 256)


def merge(peak, total, acc, peak_new, total_new, acc_new):
    best = jnp.maximum(peak, peak_new)
    left = jnp.exp2((peak - best) * RATE)
    right = jnp.exp2((peak_new - best) * RATE)
    return best, left * total + right * total_new, left * acc + right * acc_new


def first_kernel(got_ref, x_ref, mid_ref, vt_ref, state_ref, acc_ref):
    offset = head_offset()
    for half in range(2):
        four = jnp.concatenate([half_of(got_ref, half, index) for index in range(4)], axis=1)
        ordered = nn(ordering(offset, half, 0, SEG), four).astype(BF)
        for index in range(4):
            x_ref[index, half * SEG : half * SEG + SEG] = ordered[
                :, index * HEAD_DIM : (index + 1) * HEAD_DIM
            ]
        vt_ref[:, half * SEG : half * SEG + SEG] = flip(ordered[:, HEAD_DIM : 2 * HEAD_DIM])
    for index in range(4):
        mid_ref[index] = x_ref[index, LOW : LOW + MID]

    def body(step, carry):
        start, first = segment_start(step)
        scores = nt(x_ref[0, pl.ds(start, SEG)], x_ref[2, pl.ds(first, 256)])
        peak = jnp.max(scores, axis=0, keepdims=True)
        weights = jnp.exp2((scores - peak) * RATE)
        cut = pl.ds(first, 256)
        state_ref[0:1, cut] = peak
        state_ref[1:2, cut] = jnp.sum(weights, axis=0, keepdims=True)
        acc_ref[:, cut] = nn(vt_ref[:, pl.ds(start, SEG)], weights.astype(BF))
        return carry

    lax.fori_loop(0, 4, body, 0, unroll=4)


def second_kernel(x_ref, vt_ref, state_in, acc_in, stat_ref, comb_ref, mid_stat_ref, mid_acc_ref, flipped_ref, state, acc):
    state[...] = state_in[...]
    acc[...] = acc_in[...]

    def body(step, carry):
        start, first = segment_start(step)
        scores = nt(x_ref[0, pl.ds(start, SEG)], x_ref[2, pl.ds(first, 256)])
        top = jnp.max(scores, axis=0, keepdims=True)
        weights = jnp.exp2((scores - top) * RATE)
        cut = pl.ds(first, 256)
        state[0:1, cut], state[1:2, cut], acc[:, cut] = merge(
            state[0:1, cut],
            state[1:2, cut],
            acc[:, cut],
            top,
            jnp.sum(weights, axis=0, keepdims=True),
            nn(vt_ref[:, pl.ds(start, SEG)], weights.astype(BF)),
        )
        return carry

    lax.fori_loop(4, 6, body, 0, unroll=2)
    combined = acc[...] / state[1:2]
    comb_ref[...] = combined.astype(BF)
    stat_ref[0:1] = state[0:1] * RATE + jnp.log2(state[1:2])
    flipped = flip(x_ref[3])
    flipped_ref[...] = flipped[:, LOW : LOW + MID]
    stat_ref[1:2] = jnp.sum(flipped.astype(F32) * combined, axis=0, keepdims=True)
    middle = slice(LOW, LOW + MID)
    near = (state[0:1, middle], state[1:2, middle], acc[:, middle])
    near = merge(*near, *forward_of(x_ref[0, middle], vt_ref[:, middle], x_ref[2, middle]))
    inner = slice(LOW + 64, LOW + 192)
    peak, total, summed = forward_of(x_ref[0, inner], flip(x_ref[1, inner]), x_ref[2, inner])
    near = merge(*near, widen(peak, NEG), widen(total, 0.0), widen(summed, 0.0))
    mid_stat_ref[0:1], mid_stat_ref[1:2], mid_acc_ref[...] = near


def widen(part, filler):
    return pltpu.roll(jnp.concatenate([part, jnp.full_like(part, filler)], axis=1), 64, 1)


def narrow(whole):
    return pltpu.roll(whole, MID - 64, 1)[:, :128]


def forward_of(keys, values_flipped, queries):
    scores = nt(keys, queries)
    peak = jnp.max(scores, axis=0, keepdims=True)
    weights = jnp.exp2((scores - peak) * RATE)
    return (
        peak,
        jnp.sum(weights, axis=0, keepdims=True),
        nn(values_flipped, weights.astype(BF)),
    )


def backward_of(keys, values, queries, grads, log_total, dot):
    probs = jnp.exp2(nt(keys, queries) * RATE - log_total)
    score_grad = (probs * (nt(values, grads) - dot)).astype(BF)
    return (
        nn(flip(keys), score_grad),
        nn(score_grad, queries),
        nn(probs.astype(BF), grads),
    )


def join(whole, part):
    return jnp.concatenate([whole[:64], whole[64:192] + part, whole[192:]], axis=0)


def forward_kernel(mid_ref, flipped_ref, stat_ref, acc_ref, one_ref, out_stat_ref, out_acc_ref, score_ref, product_ref):
    state = (stat_ref[0:1], stat_ref[1:2], acc_ref[...])
    state = merge(*state, *forward_of(one_ref[0], flip(one_ref[1]), mid_ref[2]))
    score_ref[...] = nt(one_ref[0], mid_ref[2])
    product_ref[...] = nt(one_ref[1], mid_ref[3])
    peak, total, summed = forward_of(one_ref[0, 64:192], flip(one_ref[1, 64:192]), mid_ref[2, 64:192])
    peak, total, acc = merge(*state, widen(peak, NEG), widen(total, 0.0), widen(summed, 0.0))
    out_stat_ref[0:1], out_stat_ref[1:2], out_acc_ref[...] = peak, total, acc
    out_stat_ref[2:3] = jnp.sum(flipped_ref[...].astype(F32) * acc, axis=0, keepdims=True)


def far_kernel(mid_ref, stat_ref, score_ref, product_ref, one_ref, three_ref, two_ref,
               out_stat_ref, weight_ref, slope_ref, far_slope_ref, send_one_ref, send_two_ref, send_three_ref):
    inner = slice(64, 192)
    keys, values, queries, grads = one_ref[0], one_ref[1], mid_ref[2], mid_ref[3]
    keys3 = jnp.concatenate([keys[inner], two_ref[0], three_ref[0]], axis=0)
    values3 = jnp.concatenate([values[inner], two_ref[1], three_ref[1]], axis=0)
    scores3, grads3 = nt(keys3, queries[inner]), nt(values3, grads[inner])
    scores2, grads2 = score_ref[...], product_ref[...]
    new = scores3[128:]
    peak3 = jnp.max(new, axis=0, keepdims=True)
    weights3 = jnp.exp2((new - peak3) * RATE)
    total3 = jnp.sum(weights3, axis=0, keepdims=True)
    dot3 = jnp.sum(weights3 * grads3[128:], axis=0, keepdims=True)
    weight_ref[...] = weights3.astype(BF)
    peak3 = widen(peak3, NEG)
    best = jnp.maximum(stat_ref[0:1], peak3)
    left = jnp.exp2((stat_ref[0:1] - best) * RATE)
    right = jnp.exp2((peak3 - best) * RATE)
    total = left * stat_ref[1:2] + right * widen(total3, 0.0)
    dot = (left * stat_ref[2:3] + right * widen(dot3, 0.0)) / total
    log_total = best * RATE + jnp.log2(total)
    out_stat_ref[0:1] = log_total
    out_stat_ref[1:2] = dot
    out_stat_ref[2:3] = left / total
    out_stat_ref[3:4] = right / total
    probs3 = jnp.exp2(scores3 * RATE - narrow(log_total))
    slopes3 = (probs3 * (grads3 - narrow(dot))).astype(BF)
    probs2 = jnp.exp2(scores2 * RATE - log_total)
    slopes2 = (probs2 * (grads2 - dot)).astype(BF)
    dk3, dv3 = nn(slopes3, queries[inner]), nn(probs3.astype(BF), grads[inner])
    dk2, dv2 = nn(slopes2, queries), nn(probs2.astype(BF), grads)
    for index, (near, far, scale) in enumerate(((dk2, dk3, SCALE), (dv2, dv3, 1.0))):
        send_one_ref[index] = (join(near, far[:128]) * scale).astype(BF)
        send_two_ref[index] = (far[128:256] * scale).astype(BF)
        send_three_ref[index] = (far[256:] * scale).astype(BF)
    slope_ref[...] = slopes2
    far_slope_ref[...] = slopes3


def back_kernel(x_ref, stat_ref, comb_ref, mid_stat_ref, mid_acc_ref, weight_ref, one_ref, three_ref, two_ref, slope_ref, far_slope_ref,
                out_ref, mid_grad_ref, place_ref, kt, stat, dq, dk, dv):
    offset = head_offset()
    kt[...] = flip(x_ref[0])
    stat[...] = stat_ref[...]
    stat[:, LOW : LOW + MID] = mid_stat_ref[0:2]
    dq[...] = jnp.zeros_like(dq)
    dk[...] = jnp.zeros_like(dk)
    dv[...] = jnp.zeros_like(dv)

    def body(step, carry):
        start, first = segment_start(step)
        keys, values = x_ref[0, pl.ds(start, SEG)], x_ref[1, pl.ds(start, SEG)]
        queries, grads = x_ref[2, pl.ds(first, 256)], x_ref[3, pl.ds(first, 256)]
        cut = pl.ds(first, 256)
        probs = jnp.exp2(nt(keys, queries) * RATE - stat[0:1, cut])
        score_grad = (probs * (nt(values, grads) - stat[1:2, cut])).astype(BF)
        dq[:, cut] += nn(kt[:, pl.ds(start, SEG)], score_grad)
        dk[pl.ds(start, SEG)] += nn(score_grad, queries)
        dv[pl.ds(start, SEG)] += nn(probs.astype(BF), grads)
        return carry

    lax.fori_loop(0, 6, body, 0, unroll=6)
    for first, last in ((LOW, LOW + MID), (LOW + 64, LOW + 192)):
        cut = slice(first, last)
        log_total, dot = stat[0:1, LOW : LOW + MID], stat[1:2, LOW : LOW + MID]
        if last - first < MID:
            log_total, dot = narrow(log_total), narrow(dot)
        part, key_part, value_part = backward_of(
            x_ref[0, cut], x_ref[1, cut], x_ref[2, cut], x_ref[3, cut], log_total, dot
        )
        dq[:, LOW : LOW + MID] += part if last - first == MID else widen(part, 0.0)
        dk[cut] += key_part
        dv[cut] += value_part
    mid_grad_ref[0] = dk[LOW : LOW + MID] * SCALE
    mid_grad_ref[1] = dv[LOW : LOW + MID]
    keys3 = jnp.concatenate([one_ref[0, 64:192], two_ref[0], three_ref[0]], axis=0)
    distant = jnp.concatenate([two_ref[1], three_ref[1]], axis=0)
    mid_comb = mid_stat_ref[2:3] * mid_acc_ref[...] + mid_stat_ref[3:4] * widen(
        nn(flip(distant), weight_ref[...]), 0.0
    )
    dq[:, LOW : LOW + MID] += nn(flip(one_ref[0]), slope_ref[...]) + widen(
        nn(flip(keys3), far_slope_ref[...]), 0.0
    )
    place_ref[0] = unordering(offset, 0, LOW, 128)
    place_ref[1] = unordering(offset, 1, 0, 128)
    query = (dq[...] * SCALE).astype(BF)
    comb = jnp.concatenate(
        [comb_ref[:, :LOW], mid_comb.astype(BF), comb_ref[:, LOW + MID :]], axis=1
    )
    both = jnp.concatenate([comb, query], axis=0)
    for half in range(2):
        plain = nt(unordering(offset, half, 0, SEG), both[:, half * SEG : half * SEG + SEG]).astype(BF)
        put_half(out_ref, half, 0, plain[:, :HEAD_DIM])
        put_half(out_ref, half, 1, plain[:, HEAD_DIM:])
        outer = slice(0, LOW) if half == 0 else slice(LOW + MID, TOKENS)
        pair = jnp.concatenate([dk[outer] * SCALE, dv[outer]], axis=1).astype(BF)
        plain = nn(unordering(offset, half, 0 if half == 0 else 128, LOW), pair).astype(BF)
        put_half(out_ref, half, 2, plain[:, :HEAD_DIM])
        put_half(out_ref, half, 3, plain[:, HEAD_DIM:])


def finish_kernel(in_ref, mid_grad_ref, place_ref, one_ref, two_ref, three_ref, out_ref):
    grads = []
    for index in range(2):
        near = mid_grad_ref[index] + one_ref[index].astype(F32)
        far = two_ref[index].astype(F32) + three_ref[index].astype(F32)
        grads.append(join(near, far).astype(BF))
    pair = jnp.concatenate(grads, axis=1)
    out_ref[:, 0:2] = in_ref[:, 0:2]
    for half in range(2):
        cut = slice(half * 128, half * 128 + 128)
        plain = nn(place_ref[half], pair[cut]).astype(BF)
        for index in range(2):
            part = plain[:, index * HEAD_DIM : (index + 1) * HEAD_DIM]
            put_half(out_ref, half, index + 2, half_of(in_ref, half, index + 2) + part)


def shape(dims, kind):
    return jax.ShapeDtypeStruct(dims, kind)


PARAMS = pltpu.CompilerParams(vmem_limit_bytes=32 * 1024 * 1024)


def whole(array):
    return pl.BlockSpec(array.shape, lambda: (0,) * len(array.shape))


def call(kernel, outs, args, scratch=(), flops=0):
    return pl.pallas_call(
        kernel,
        out_shape=outs,
        scratch_shapes=list(scratch),
        compiler_params=PARAMS,
        cost_estimate=pl.CostEstimate(flops=flops, bytes_accessed=2 << 20, transcendentals=0),
    )(*args)


def pack(arrays):
    return pl.pallas_call(
        pack_kernel,
        in_specs=[pl.BlockSpec(memory_space=pl.ANY)] * 4,
        out_shape=shape((PLANE, 4, ROWS, HEAD_DIM), BF),
        scratch_shapes=[
            pltpu.VMEM((4, ROWS, PLANE * HEAD_DIM), BF),
            pltpu.SemaphoreType.DMA((4,)),
        ],
        compiler_params=PARAMS,
    )(*[pltpu.with_memory_space_constraint(array, pltpu.HBM) for array in arrays])


def unpack(packed):
    return pl.pallas_call(
        unpack_kernel,
        out_specs=[pl.BlockSpec(memory_space=pl.ANY)] * 4,
        out_shape=[shape((ROWS, PLANE * HEAD_DIM), BF)] * 4,
        scratch_shapes=[
            pltpu.VMEM((4, ROWS, PLANE * HEAD_DIM), BF),
            pltpu.SemaphoreType.DMA((4,)),
        ],
        compiler_params=PARAMS,
    )(packed)


def plane_exchange(packed):
    return lax.all_to_all(packed, ("x", "y_lo", "y_hi", "core"), split_axis=0, concat_axis=0, tiled=True)


def z_exchange(block, apart):
    count = lax.axis_size("zed")
    return lax.ppermute(block, "zed", [(at, at ^ apart) for at in range(count)])


def per_device(query_rows, key_rows, value_rows, grad_rows):
    got = plane_exchange(pack([key_rows, value_rows, query_rows, grad_rows]))
    near = call(select_kernel, shape((2, MID, HEAD_DIM), BF), [got])
    inner = near[:, 64:192]
    one = z_exchange(near, 1)
    three = z_exchange(inner, 3)
    two = z_exchange(inner, 2)
    ordered, mid, vt, state, acc = call(
        first_kernel,
        [
            shape((4, TOKENS, HEAD_DIM), BF),
            shape((4, MID, HEAD_DIM), BF),
            shape((HEAD_DIM, TOKENS), BF),
            shape((2, TOKENS), F32),
            shape((HEAD_DIM, TOKENS), F32),
        ],
        [got],
        flops=2 * 4 * SEG * SEG * HEAD_DIM,
    )
    stat, comb, mid_stat, mid_acc, flipped = call(
        second_kernel,
        [
            shape((2, TOKENS), F32),
            shape((HEAD_DIM, TOKENS), BF),
            shape((2, MID), F32),
            shape((HEAD_DIM, MID), F32),
            shape((HEAD_DIM, MID), BF),
        ],
        [ordered, vt, state, acc],
        [pltpu.VMEM((2, TOKENS), F32), pltpu.VMEM((HEAD_DIM, TOKENS), F32)],
        flops=4 * SEG * SEG * HEAD_DIM,
    )
    mid_stat, mid_acc, score, product = call(
        forward_kernel,
        [
            shape((3, MID), F32),
            shape((HEAD_DIM, MID), F32),
            shape((MID, MID), F32),
            shape((MID, MID), F32),
        ],
        [mid, flipped, mid_stat, mid_acc, one],
        flops=8 * 4 * SEG * SEG * HEAD_DIM,
    )
    mid_out_stat, weight, slope, far_slope, send_one, send_two, send_three = call(
        far_kernel,
        [
            shape((4, MID), F32),
            shape((MID, 128), BF),
            shape((MID, MID), BF),
            shape((384, 128), BF),
            shape((2, MID, HEAD_DIM), BF),
            shape((2, 128, HEAD_DIM), BF),
            shape((2, 128, HEAD_DIM), BF),
        ],
        [mid, mid_stat, score, product, one, three, two],
        flops=2 * 4 * SEG * SEG * HEAD_DIM,
    )
    back_one = z_exchange(send_one, 1)
    back_two = z_exchange(send_two, 2)
    back_three = z_exchange(send_three, 3)
    packed, mid_grad, place = call(
        back_kernel,
        [
            shape((PLANE, 4, ROWS, HEAD_DIM), BF),
            shape((2, MID, HEAD_DIM), F32),
            shape((2, SEG, 128), BF),
        ],
        [ordered, stat, comb, mid_out_stat, mid_acc, weight, one, three, two, slope, far_slope],
        [
            pltpu.VMEM((HEAD_DIM, TOKENS), BF),
            pltpu.VMEM((2, TOKENS), F32),
            pltpu.VMEM((HEAD_DIM, TOKENS), F32),
            pltpu.VMEM((TOKENS, HEAD_DIM), F32),
            pltpu.VMEM((TOKENS, HEAD_DIM), F32),
        ],
        flops=3 * 10 * SEG * SEG * HEAD_DIM,
    )
    packed = call(
        finish_kernel,
        shape((PLANE, 4, ROWS, HEAD_DIM), BF),
        [packed, mid_grad, place, back_one, back_two, back_three],
    )
    return tuple(unpack(plane_exchange(packed)))


def solution(mesh):
    axes = ("zed", "y_lo", "core", "y_hi", "x")
    planes = Mesh(mesh.devices.reshape(-1, 2, 2, 2, 4), axes)
    spec = P(axes, None)
    return jax.shard_map(
        per_device, mesh=planes, in_specs=(spec,) * 4, out_specs=(spec,) * 4, check_vma=False
    )
```

```python
import functools

import jax
import jax.numpy as jnp
from jax import lax
from jax.experimental import pallas as pl
from jax.experimental.pallas import tpu as pltpu
from jax.sharding import Mesh, PartitionSpec as P

HEAD_DIM = 128
PLANE = 32
ROWS = 32
TOKENS = PLANE * ROWS
SEG = 512
MID = 256
LOW = 384
SCALE = HEAD_DIM**-0.5
RATE = SCALE * 1.4426950408889634
NEG = -1e30
BF = jnp.bfloat16
F32 = jnp.float32

ORDER = [
    y_lo * 16 + core * 8 + y_hi * 4 + x
    for x in range(4)
    for y_lo in range(2)
    for y_hi in range(2)
    for core in range(2)
]
PLACE = [ORDER.index(device) for device in range(PLANE)]


def nn(a, b):
    return jnp.dot(a, b, preferred_element_type=F32)


def nt(a, b):
    return lax.dot_general(a, b, (((1,), (1,)), ((), ())), preferred_element_type=F32)


def flip(a):
    return jnp.swapaxes(a, 0, 1)


def token_of(spot, offset, half):
    if half == 0:
        far = [2 * spot, 4 * (spot - 256), 8 * (spot - 384), 8 * (spot - 448)]
        tests = [spot < 256, spot < 384, spot < 448]
    else:
        far = [2 * (spot - 256), 4 * (spot - 128), 8 * (spot - 64), 8 * spot]
        tests = [spot >= 256, spot >= 128, spot >= 64]
    return jnp.where(
        tests[0],
        far[0] + ((offset + 1) & 1),
        jnp.where(
            tests[1],
            far[1] + ((offset + 2) & 3),
            jnp.where(tests[2], far[2] + ((offset + 4) & 7), far[3] + offset),
        ),
    )


def ordering(offset, half, first, count):
    spot = lax.broadcasted_iota(jnp.int32, (count, 1), 0) + first
    token = lax.broadcasted_iota(jnp.int32, (count, SEG), 1)
    return jnp.where(token_of(spot, offset, half) == token, 1.0, 0.0).astype(BF)


def unordering(offset, half, first, count):
    spot = lax.broadcasted_iota(jnp.int32, (1, count), 1) + first
    token = lax.broadcasted_iota(jnp.int32, (SEG, count), 0)
    return jnp.where(token_of(spot, offset, half) == token, 1.0, 0.0).astype(BF)


def head_offset():
    return lax.axis_index("y_hi") * 4 + lax.axis_index("x")


def half_of(ref, half, index):
    return jnp.concatenate([ref[PLACE[block], index] for block in range(half * 16, half * 16 + 16)], axis=0)


def put_half(ref, half, index, value):
    for block in range(16):
        ref[PLACE[half * 16 + block], index] = value[block * ROWS : block * ROWS + ROWS]


def pack_kernel(key_ref, value_ref, query_ref, grad_ref, out_ref, held, arrived):
    copies = [
        pltpu.make_async_copy(source, held.at[index], arrived.at[index])
        for index, source in enumerate((key_ref, value_ref, query_ref, grad_ref))
    ]
    for copy in copies:
        copy.start()
    for index, copy in enumerate(copies):
        copy.wait()
        for head in range(PLANE):
            out_ref[PLACE[head], index] = held[index, :, head * HEAD_DIM : (head + 1) * HEAD_DIM]


def unpack_kernel(in_ref, att_ref, query_ref, key_ref, value_ref, held, sent):
    copies = []
    for index, target in enumerate((att_ref, query_ref, key_ref, value_ref)):
        for head in range(PLANE):
            held[index, :, head * HEAD_DIM : (head + 1) * HEAD_DIM] = in_ref[PLACE[head], index]
        copies.append(pltpu.make_async_copy(held.at[index], target, sent.at[index]))
        copies[-1].start()
    for copy in copies:
        copy.wait()


def select_kernel(got_ref, out_ref):
    offset = head_offset()
    for half in range(2):
        pair = jnp.concatenate([half_of(got_ref, half, 0), half_of(got_ref, half, 1)], axis=1)
        picked = nn(ordering(offset, half, LOW if half == 0 else 0, 128), pair).astype(BF)
        out_ref[0, half * 128 : half * 128 + 128] = picked[:, :HEAD_DIM]
        out_ref[1, half * 128 : half * 128 + 128] = picked[:, HEAD_DIM:]


def segment_start(step):
    segment = step // 2
    start = jnp.where(segment == 2, 256, segment * SEG)
    return pl.multiple_of(start, 256), pl.multiple_of(start + (step % 2) * 256, 256)


def merge(peak, total, acc, peak_new, total_new, acc_new):
    best = jnp.maximum(peak, peak_new)
    left = jnp.exp2((peak - best) * RATE)
    right = jnp.exp2((peak_new - best) * RATE)
    return best, left * total + right * total_new, left * acc + right * acc_new


def first_kernel(got_ref, x_ref, mid_ref, vt_ref, state_ref, acc_ref):
    offset = head_offset()
    for half in range(2):
        four = jnp.concatenate([half_of(got_ref, half, index) for index in range(4)], axis=1)
        ordered = nn(ordering(offset, half, 0, SEG), four).astype(BF)
        for index in range(4):
            x_ref[index, half * SEG : half * SEG + SEG] = ordered[
                :, index * HEAD_DIM : (index + 1) * HEAD_DIM
            ]
        vt_ref[:, half * SEG : half * SEG + SEG] = flip(ordered[:, HEAD_DIM : 2 * HEAD_DIM])
    for index in range(4):
        mid_ref[index] = x_ref[index, LOW : LOW + MID]

    def body(step, carry):
        start, first = segment_start(step)
        scores = nt(x_ref[0, pl.ds(start, SEG)], x_ref[2, pl.ds(first, 256)])
        peak = jnp.max(scores, axis=0, keepdims=True)
        weights = jnp.exp2((scores - peak) * RATE)
        cut = pl.ds(first, 256)
        state_ref[0:1, cut] = peak
        state_ref[1:2, cut] = jnp.sum(weights, axis=0, keepdims=True)
        acc_ref[:, cut] = nn(vt_ref[:, pl.ds(start, SEG)], weights.astype(BF))
        return carry

    lax.fori_loop(0, 4, body, 0, unroll=4)


def second_kernel(x_ref, vt_ref, state_in, acc_in, stat_ref, comb_ref, mid_stat_ref, mid_acc_ref, flipped_ref, state, acc):
    state[...] = state_in[...]
    acc[...] = acc_in[...]

    def body(step, carry):
        start, first = segment_start(step)
        scores = nt(x_ref[0, pl.ds(start, SEG)], x_ref[2, pl.ds(first, 256)])
        top = jnp.max(scores, axis=0, keepdims=True)
        weights = jnp.exp2((scores - top) * RATE)
        cut = pl.ds(first, 256)
        state[0:1, cut], state[1:2, cut], acc[:, cut] = merge(
            state[0:1, cut],
            state[1:2, cut],
            acc[:, cut],
            top,
            jnp.sum(weights, axis=0, keepdims=True),
            nn(vt_ref[:, pl.ds(start, SEG)], weights.astype(BF)),
        )
        return carry

    lax.fori_loop(4, 6, body, 0, unroll=2)
    combined = acc[...] / state[1:2]
    comb_ref[...] = combined.astype(BF)
    stat_ref[0:1] = state[0:1] * RATE + jnp.log2(state[1:2])
    flipped = flip(x_ref[3])
    flipped_ref[...] = flipped[:, LOW : LOW + MID]
    stat_ref[1:2] = jnp.sum(flipped.astype(F32) * combined, axis=0, keepdims=True)
    middle = slice(LOW, LOW + MID)
    near = (state[0:1, middle], state[1:2, middle], acc[:, middle])
    near = merge(*near, *forward_of(x_ref[0, middle], vt_ref[:, middle], x_ref[2, middle]))
    inner = slice(LOW + 64, LOW + 192)
    peak, total, summed = forward_of(x_ref[0, inner], flip(x_ref[1, inner]), x_ref[2, inner])
    near = merge(*near, widen(peak, NEG), widen(total, 0.0), widen(summed, 0.0))
    mid_stat_ref[0:1], mid_stat_ref[1:2], mid_acc_ref[...] = near


def widen(part, filler):
    return pltpu.roll(jnp.concatenate([part, jnp.full_like(part, filler)], axis=1), 64, 1)


def narrow(whole):
    return pltpu.roll(whole, MID - 64, 1)[:, :128]


def forward_of(keys, values_flipped, queries):
    scores = nt(keys, queries)
    peak = jnp.max(scores, axis=0, keepdims=True)
    weights = jnp.exp2((scores - peak) * RATE)
    return (
        peak,
        jnp.sum(weights, axis=0, keepdims=True),
        nn(values_flipped, weights.astype(BF)),
    )


def backward_of(keys, values, queries, grads, log_total, dot):
    probs = jnp.exp2(nt(keys, queries) * RATE - log_total)
    score_grad = (probs * (nt(values, grads) - dot)).astype(BF)
    return (
        nn(flip(keys), score_grad),
        nn(score_grad, queries),
        nn(probs.astype(BF), grads),
    )


def join(whole, part):
    return jnp.concatenate([whole[:64], whole[64:192] + part, whole[192:]], axis=0)


def forward_kernel(mid_ref, flipped_ref, stat_ref, acc_ref, one_ref, out_stat_ref, out_acc_ref, score_ref, product_ref):
    state = (stat_ref[0:1], stat_ref[1:2], acc_ref[...])
    state = merge(*state, *forward_of(one_ref[0], flip(one_ref[1]), mid_ref[2]))
    score_ref[...] = nt(one_ref[0], mid_ref[2])
    product_ref[...] = nt(one_ref[1], mid_ref[3])
    peak, total, summed = forward_of(one_ref[0, 64:192], flip(one_ref[1, 64:192]), mid_ref[2, 64:192])
    peak, total, acc = merge(*state, widen(peak, NEG), widen(total, 0.0), widen(summed, 0.0))
    out_stat_ref[0:1], out_stat_ref[1:2], out_acc_ref[...] = peak, total, acc
    out_stat_ref[2:3] = jnp.sum(flipped_ref[...].astype(F32) * acc, axis=0, keepdims=True)


def far_kernel(mid_ref, stat_ref, score_ref, product_ref, one_ref, three_ref, two_ref,
               out_stat_ref, weight_ref, slope_ref, far_slope_ref, send_one_ref, send_two_ref, send_three_ref):
    inner = slice(64, 192)
    keys, values, queries, grads = one_ref[0], one_ref[1], mid_ref[2], mid_ref[3]
    keys3 = jnp.concatenate([two_ref[0], three_ref[0]], axis=0)
    values3 = jnp.concatenate([two_ref[1], three_ref[1]], axis=0)
    scores3, grads3 = nt(keys3, queries[inner]), nt(values3, grads[inner])
    scores2, grads2 = score_ref[...], product_ref[...]
    new = scores3
    peak3 = jnp.max(new, axis=0, keepdims=True)
    weights3 = jnp.exp2((new - peak3) * RATE)
    total3 = jnp.sum(weights3, axis=0, keepdims=True)
    dot3 = jnp.sum(weights3 * grads3, axis=0, keepdims=True)
    weight_ref[...] = weights3.astype(BF)
    peak3 = widen(peak3, NEG)
    best = jnp.maximum(stat_ref[0:1], peak3)
    left = jnp.exp2((stat_ref[0:1] - best) * RATE)
    right = jnp.exp2((peak3 - best) * RATE)
    total = left * stat_ref[1:2] + right * widen(total3, 0.0)
    dot = (left * stat_ref[2:3] + right * widen(dot3, 0.0)) / total
    log_total = best * RATE + jnp.log2(total)
    out_stat_ref[0:1] = log_total
    out_stat_ref[1:2] = dot
    out_stat_ref[2:3] = left / total
    out_stat_ref[3:4] = right / total
    probs3 = jnp.exp2(scores3 * RATE - narrow(log_total))
    slopes3 = (probs3 * (grads3 - narrow(dot))).astype(BF)
    probs2 = jnp.exp2(scores2 * RATE - log_total)
    row = lax.broadcasted_iota(jnp.int32, (MID, 1), 0)
    lane = lax.broadcasted_iota(jnp.int32, (1, MID), 1)
    both = jnp.where((row >= 64) & (row < 192), 1.0, 0.0) * jnp.where((lane >= 64) & (lane < 192), 1.0, 0.0)
    probs2 = probs2 * (1.0 + both)
    slopes2 = (probs2 * (grads2 - dot)).astype(BF)
    dk3, dv3 = nn(slopes3, queries[inner]), nn(probs3.astype(BF), grads[inner])
    dk2, dv2 = nn(slopes2, queries), nn(probs2.astype(BF), grads)
    for index, (near, far, scale) in enumerate(((dk2, dk3, SCALE), (dv2, dv3, 1.0))):
        send_one_ref[index] = (near * scale).astype(BF)
        send_two_ref[index] = (far[:128] * scale).astype(BF)
        send_three_ref[index] = (far[128:] * scale).astype(BF)
    slope_ref[...] = slopes2
    far_slope_ref[...] = slopes3


def back_kernel(x_ref, stat_ref, comb_ref, mid_stat_ref, mid_acc_ref, weight_ref, one_ref, three_ref, two_ref, slope_ref, far_slope_ref,
                out_ref, mid_grad_ref, place_ref, kt, stat, dq, dk, dv):
    offset = head_offset()
    kt[...] = flip(x_ref[0])
    stat[...] = stat_ref[...]
    stat[:, LOW : LOW + MID] = mid_stat_ref[0:2]
    dq[...] = jnp.zeros_like(dq)
    dk[...] = jnp.zeros_like(dk)
    dv[...] = jnp.zeros_like(dv)

    def body(step, carry):
        start, first = segment_start(step)
        keys, values = x_ref[0, pl.ds(start, SEG)], x_ref[1, pl.ds(start, SEG)]
        queries, grads = x_ref[2, pl.ds(first, 256)], x_ref[3, pl.ds(first, 256)]
        cut = pl.ds(first, 256)
        probs = jnp.exp2(nt(keys, queries) * RATE - stat[0:1, cut])
        score_grad = (probs * (nt(values, grads) - stat[1:2, cut])).astype(BF)
        dq[:, cut] += nn(kt[:, pl.ds(start, SEG)], score_grad)
        dk[pl.ds(start, SEG)] += nn(score_grad, queries)
        dv[pl.ds(start, SEG)] += nn(probs.astype(BF), grads)
        return carry

    lax.fori_loop(0, 6, body, 0, unroll=6)
    for first, last in ((LOW, LOW + MID), (LOW + 64, LOW + 192)):
        cut = slice(first, last)
        log_total, dot = stat[0:1, LOW : LOW + MID], stat[1:2, LOW : LOW + MID]
        if last - first < MID:
            log_total, dot = narrow(log_total), narrow(dot)
        part, key_part, value_part = backward_of(
            x_ref[0, cut], x_ref[1, cut], x_ref[2, cut], x_ref[3, cut], log_total, dot
        )
        dq[:, LOW : LOW + MID] += part if last - first == MID else widen(part, 0.0)
        dk[cut] += key_part
        dv[cut] += value_part
    mid_grad_ref[0] = dk[LOW : LOW + MID] * SCALE
    mid_grad_ref[1] = dv[LOW : LOW + MID]
    keys3 = jnp.concatenate([two_ref[0], three_ref[0]], axis=0)
    distant = jnp.concatenate([two_ref[1], three_ref[1]], axis=0)
    mid_comb = mid_stat_ref[2:3] * mid_acc_ref[...] + mid_stat_ref[3:4] * widen(
        nn(flip(distant), weight_ref[...]), 0.0
    )
    dq[:, LOW : LOW + MID] += nn(flip(one_ref[0]), slope_ref[...]) + widen(
        nn(flip(keys3), far_slope_ref[...]), 0.0
    )
    place_ref[0] = unordering(offset, 0, LOW, 128)
    place_ref[1] = unordering(offset, 1, 0, 128)
    query = (dq[...] * SCALE).astype(BF)
    comb = jnp.concatenate(
        [comb_ref[:, :LOW], mid_comb.astype(BF), comb_ref[:, LOW + MID :]], axis=1
    )
    both = jnp.concatenate([comb, query], axis=0)
    for half in range(2):
        plain = nt(unordering(offset, half, 0, SEG), both[:, half * SEG : half * SEG + SEG]).astype(BF)
        put_half(out_ref, half, 0, plain[:, :HEAD_DIM])
        put_half(out_ref, half, 1, plain[:, HEAD_DIM:])
        outer = slice(0, LOW) if half == 0 else slice(LOW + MID, TOKENS)
        pair = jnp.concatenate([dk[outer] * SCALE, dv[outer]], axis=1).astype(BF)
        plain = nn(unordering(offset, half, 0 if half == 0 else 128, LOW), pair).astype(BF)
        put_half(out_ref, half, 2, plain[:, :HEAD_DIM])
        put_half(out_ref, half, 3, plain[:, HEAD_DIM:])


def finish_kernel(in_ref, mid_grad_ref, place_ref, one_ref, two_ref, three_ref, out_ref):
    grads = []
    for index in range(2):
        near = mid_grad_ref[index] + one_ref[index].astype(F32)
        far = two_ref[index].astype(F32) + three_ref[index].astype(F32)
        grads.append(join(near, far).astype(BF))
    pair = jnp.concatenate(grads, axis=1)
    out_ref[:, 0:2] = in_ref[:, 0:2]
    for half in range(2):
        cut = slice(half * 128, half * 128 + 128)
        plain = nn(place_ref[half], pair[cut]).astype(BF)
        for index in range(2):
            part = plain[:, index * HEAD_DIM : (index + 1) * HEAD_DIM]
            put_half(out_ref, half, index + 2, half_of(in_ref, half, index + 2) + part)


def shape(dims, kind):
    return jax.ShapeDtypeStruct(dims, kind)


PARAMS = pltpu.CompilerParams(vmem_limit_bytes=32 * 1024 * 1024)


def whole(array):
    return pl.BlockSpec(array.shape, lambda: (0,) * len(array.shape))


def call(kernel, outs, args, scratch=(), flops=0):
    return pl.pallas_call(
        kernel,
        out_shape=outs,
        scratch_shapes=list(scratch),
        compiler_params=PARAMS,
        cost_estimate=pl.CostEstimate(flops=flops, bytes_accessed=2 << 20, transcendentals=0),
    )(*args)


def pack(arrays):
    return pl.pallas_call(
        pack_kernel,
        in_specs=[pl.BlockSpec(memory_space=pl.ANY)] * 4,
        out_shape=shape((PLANE, 4, ROWS, HEAD_DIM), BF),
        scratch_shapes=[
            pltpu.VMEM((4, ROWS, PLANE * HEAD_DIM), BF),
            pltpu.SemaphoreType.DMA((4,)),
        ],
        compiler_params=PARAMS,
    )(*[pltpu.with_memory_space_constraint(array, pltpu.HBM) for array in arrays])


def unpack(packed):
    return pl.pallas_call(
        unpack_kernel,
        out_specs=[pl.BlockSpec(memory_space=pl.ANY)] * 4,
        out_shape=[shape((ROWS, PLANE * HEAD_DIM), BF)] * 4,
        scratch_shapes=[
            pltpu.VMEM((4, ROWS, PLANE * HEAD_DIM), BF),
            pltpu.SemaphoreType.DMA((4,)),
        ],
        compiler_params=PARAMS,
    )(packed)


def plane_exchange(packed):
    return lax.all_to_all(packed, ("x", "y_lo", "y_hi", "core"), split_axis=0, concat_axis=0, tiled=True)


def z_exchange(block, apart):
    count = lax.axis_size("zed")
    return lax.ppermute(block, "zed", [(at, at ^ apart) for at in range(count)])


def per_device(query_rows, key_rows, value_rows, grad_rows):
    got = plane_exchange(pack([key_rows, value_rows, query_rows, grad_rows]))
    near = call(select_kernel, shape((2, MID, HEAD_DIM), BF), [got])
    inner = near[:, 64:192]
    one = z_exchange(near, 1)
    three = z_exchange(inner, 3)
    two = z_exchange(inner, 2)
    ordered, mid, vt, state, acc = call(
        first_kernel,
        [
            shape((4, TOKENS, HEAD_DIM), BF),
            shape((4, MID, HEAD_DIM), BF),
            shape((HEAD_DIM, TOKENS), BF),
            shape((2, TOKENS), F32),
            shape((HEAD_DIM, TOKENS), F32),
        ],
        [got],
        flops=2 * 4 * SEG * SEG * HEAD_DIM,
    )
    stat, comb, mid_stat, mid_acc, flipped = call(
        second_kernel,
        [
            shape((2, TOKENS), F32),
            shape((HEAD_DIM, TOKENS), BF),
            shape((2, MID), F32),
            shape((HEAD_DIM, MID), F32),
            shape((HEAD_DIM, MID), BF),
        ],
        [ordered, vt, state, acc],
        [pltpu.VMEM((2, TOKENS), F32), pltpu.VMEM((HEAD_DIM, TOKENS), F32)],
        flops=4 * SEG * SEG * HEAD_DIM,
    )
    mid_stat, mid_acc, score, product = call(
        forward_kernel,
        [
            shape((3, MID), F32),
            shape((HEAD_DIM, MID), F32),
            shape((MID, MID), F32),
            shape((MID, MID), F32),
        ],
        [mid, flipped, mid_stat, mid_acc, one],
        flops=8 * 4 * SEG * SEG * HEAD_DIM,
    )
    mid_out_stat, weight, slope, far_slope, send_one, send_two, send_three = call(
        far_kernel,
        [
            shape((4, MID), F32),
            shape((MID, 128), BF),
            shape((MID, MID), BF),
            shape((256, 128), BF),
            shape((2, MID, HEAD_DIM), BF),
            shape((2, 128, HEAD_DIM), BF),
            shape((2, 128, HEAD_DIM), BF),
        ],
        [mid, mid_stat, score, product, one, three, two],
        flops=2 * 4 * SEG * SEG * HEAD_DIM,
    )
    back_one = z_exchange(send_one, 1)
    back_two = z_exchange(send_two, 2)
    back_three = z_exchange(send_three, 3)
    packed, mid_grad, place = call(
        back_kernel,
        [
            shape((PLANE, 4, ROWS, HEAD_DIM), BF),
            shape((2, MID, HEAD_DIM), F32),
            shape((2, SEG, 128), BF),
        ],
        [ordered, stat, comb, mid_out_stat, mid_acc, weight, one, three, two, slope, far_slope],
        [
            pltpu.VMEM((HEAD_DIM, TOKENS), BF),
            pltpu.VMEM((2, TOKENS), F32),
            pltpu.VMEM((HEAD_DIM, TOKENS), F32),
            pltpu.VMEM((TOKENS, HEAD_DIM), F32),
            pltpu.VMEM((TOKENS, HEAD_DIM), F32),
        ],
        flops=3 * 10 * SEG * SEG * HEAD_DIM,
    )
    packed = call(
        finish_kernel,
        shape((PLANE, 4, ROWS, HEAD_DIM), BF),
        [packed, mid_grad, place, back_one, back_two, back_three],
    )
    return tuple(unpack(plane_exchange(packed)))


def solution(mesh):
    axes = ("zed", "y_lo", "core", "y_hi", "x")
    planes = Mesh(mesh.devices.reshape(-1, 2, 2, 2, 4), axes)
    spec = P(axes, None)
    return jax.shard_map(
        per_device, mesh=planes, in_specs=(spec,) * 4, out_specs=(spec,) * 4, check_vma=False
    )
```
